128 devices in a mesh: grp: 16 (over x_hi, z, core), sp: 8 (over y, x_lo).
Axes of the slice: x: 4 (x_hi: 2, x_lo: 2; x = x_hi * 2 + x_lo), y: 4, z: 4, core: 2. Of those that a mesh axis runs over, the one named last changes fastest.
Arguments:
- hidden_states: bfloat16 [16, 1024, 5120], P('grp', 'sp'), may hold values from -6 to 6
- modulation: float32 [16, 2, 5120], P('grp'), may hold values from -3 to 3
- query_weight: bfloat16 [5120, 5120], P('grp', 'sp'), may hold values from -0.125 to 0.125
- key_weight: bfloat16 [5120, 5120], P('grp', 'sp'), may hold values from -0.125 to 0.125
- value_weight: bfloat16 [5120, 5120], P('grp', 'sp'), may hold values from -0.125 to 0.125
- query_mask: int32 [1280, 5120], P('grp', 'sp'), may hold values from 0 to 5
- key_mask: int32 [1280, 5120], P('grp', 'sp'), may hold values from 0 to 5
- value_mask: int32 [1280, 5120], P('grp', 'sp'), may hold values from 0 to 5
- query_gain: float32 [5120], P('sp'), may hold values from 1 to 12, as said below
- key_gain: float32 [5120], P('sp'), may hold values from 1 to 12, as said below
Outputs:
- attended: bfloat16 [16, 1024, 5120], P('grp', 'sp')
- gram: float32 [8, 640, 5120], P('sp', 'grp')
The draws below stay inside these ranges and needn't reach their ends.
Inputs may be any that keep to these rules, and one draw needn't show every extreme that they name: `query_mask`: index of the kept pair of positions, in the order (0,1), (0,2), (0,3), (1,2), (1,3), (2,3). `key_mask`: index of the kept pair of positions, in the order (0,1), (0,2), (0,3), (1,2), (1,3), (2,3). `value_mask`: index of the kept pair of positions, in the order (0,1), (0,2), (0,3), (1,2), (1,3), (2,3). `query_gain`: positive gains. `key_gain`: positive gains.
All inputs are finite; a program needn't handle non-finite values.
Results may differ from the reference program's by a relative error of at most 0.017.
The reference program's roundings to bfloat16 on the way (of `normed`, `values` and `probabilities`) count: a program that leaves them out, or rounds other values in their place, can miss the bound.
Values may be sent and summed in bfloat16 or wider, within the bound.
No kernel may reach another device: no remote copies, remote signals or barrier semaphores. Data moves between devices by JAX's collectives and lax.ppermute only.
A program may use at most 128 MiB of HBM per device.

```python
import jax
import jax.numpy as jnp
from jax import lax

D = 5120
HEADS = 40
HEAD_DIM = 128
HEIGHT = 16
WIDTH = 16
SEQ = 1024
BATCH = 16
N_SP = 8


def gain_values(seed_key, lower_end, upper_end):
    log_values = jax.random.uniform(seed_key, (D,), jnp.float32, jnp.log(lower_end), jnp.log(upper_end))
    return jnp.exp(log_values)


def draw_query_gain(key, part):
    key = jax.random.fold_in(key, 7)
    return gain_values(key, 1.0, 4.0)


def draw_key_gain(key, part):
    key = jax.random.fold_in(key, 13)
    return gain_values(key, 1.0, 4.0)


def set_ends(values, own_key, smallest, high):
    extent = values.shape
    spot = [jax.random.randint(jax.random.fold_in(own_key, axis), (), 0, extent[axis]) for axis in range(len(extent))]
    values = values.at[tuple(spot)].set(smallest)
    longest = extent.index(max(extent))
    spot[longest] = (spot[longest] + 1) % extent[longest]
    return values.at[tuple(spot)].set(high)


def block_levels(key, dims, pieces, low, high):
    def one(position, blocks):
        draws = jax.random.uniform(jax.random.fold_in(jax.random.fold_in(key, 6), position), (blocks,), jnp.float32, low / len(pieces), high / len(pieces))
        return jnp.repeat(jnp.exp(draws), dims[position] // blocks).reshape((-1,) + (1,) * (len(dims) - position - 1))

    factor_of = one(*pieces[0])
    for cut in pieces[1:]:
        factor_of = factor_of * one(*cut)
    return factor_of


def scatter_about(own_key, shape, spread, limit, shards=(), held_as=jnp.bfloat16):
    result = jax.random.normal(own_key, shape, jnp.float32) * spread
    if len(shards) > 0:
        result = block_levels(own_key, shape, shards, -0.22, 0.18) * result
    return jnp.clip(result, min=-limit, max=limit).astype(held_as)


def setup_inputs(seed: int = 0) -> dict:
    key_of = jax.random.split(jax.random.key(seed), 11)
    hidden_states = scatter_about(key_of[0], (BATCH, SEQ, D), 1.0, 6.0, ((0, 16), (1, 8)))
    modulation = scatter_about(key_of[1], (BATCH, 2, D), 0.5, 3.0, ((0, 16),), jnp.float32)
    query_weight = scatter_about(key_of[2], (D, D), (D // 2) ** -0.5, 0.125, ((0, 16), (1, 8)))
    key_weight = scatter_about(key_of[3], (D, D), (D // 2) ** -0.5, 0.125, ((0, 16), (1, 8)))
    value_weight = scatter_about(key_of[4], (D, D), (D // 2) ** -0.5, 0.125, ((0, 16), (1, 8)))
    query_mask = set_ends(jax.random.randint(key_of[5], (D // 4, D), 0, 6), jax.random.fold_in(key_of[5], 1), 0, 5).astype(jnp.int32)
    key_mask = set_ends(jax.random.randint(key_of[6], (D // 4, D), 0, 6), jax.random.fold_in(key_of[6], 1), 0, 5).astype(jnp.int32)
    value_mask = set_ends(jax.random.randint(key_of[7], (D // 4, D), 0, 6), jax.random.fold_in(key_of[7], 1), 0, 5).astype(jnp.int32)
    query_gain = draw_query_gain(jax.random.fold_in(key_of[10], 71), 0)
    key_gain = draw_key_gain(jax.random.fold_in(key_of[10], 71), 0)
    return {"hidden_states": hidden_states, "modulation": modulation, "query_weight": query_weight, "key_weight": key_weight, "value_weight": value_weight, "query_mask": query_mask, "key_mask": key_mask, "value_mask": value_mask, "query_gain": query_gain, "key_gain": key_gain}


def pair_tables(pair_index):
    first_slot = jnp.where(pair_index < 3, 0, jnp.where(pair_index < 5, 1, 2))
    second_slot = jnp.where(pair_index == 0, 1, jnp.where((pair_index == 1) | (pair_index == 3), 2, 3))
    return (first_slot, second_slot)

def keep_pattern(pair_index):
    first_slot, second_slot = pair_tables(pair_index)
    slot_ids = jnp.arange(4, dtype=jnp.int32)[None, :, None]
    chosen = (first_slot[:, None, :] == slot_ids) | (second_slot[:, None, :] == slot_ids)
    return chosen.reshape(pair_index.shape[0] * 4, pair_index.shape[1])

def rope_tables(seq_len, head_dim):
    positions = jnp.arange(seq_len, dtype=jnp.int32)
    frame_pos = (positions // (HEIGHT * WIDTH)).astype(jnp.float32)
    row_pos = (positions // WIDTH % HEIGHT).astype(jnp.float32)
    col_pos = (positions % WIDTH).astype(jnp.float32)
    half_dim = head_dim // 2
    spatial = head_dim // 6
    temporal = half_dim - 2 * spatial
    pair_ids = jnp.arange(half_dim, dtype=jnp.int32)
    exponent = jnp.where(pair_ids < temporal, 2.0 * pair_ids / (2.0 * temporal), jnp.where(pair_ids < temporal + spatial, 2.0 * (pair_ids - temporal) / (2.0 * spatial), 2.0 * (pair_ids - temporal - spatial) / (2.0 * spatial))).astype(jnp.float32)
    frequency = jnp.power(jnp.float32(10000.0), -exponent)
    chosen_pos = jnp.where(pair_ids[None, :] < temporal, frame_pos[:, None], jnp.where(pair_ids[None, :] < temporal + spatial, row_pos[:, None], col_pos[:, None]))
    angles = jnp.repeat(chosen_pos * frequency[None, :], 2, axis=1)
    return (jnp.cos(angles), jnp.sin(angles))

def swap_matrix(head_dim):
    entries = jnp.arange(head_dim, dtype=jnp.int32)
    source = entries[:, None]
    target = entries[None, :]
    negative = (target % 2 == 0) & (source == target + 1)
    positive = (target % 2 == 1) & (source == target - 1)
    return jnp.where(negative, -1.0, jnp.where(positive, 1.0, 0.0)).astype(jnp.float32)

def rotate_pairs(tensor, cosine_table, sine_table):
    swapped = jnp.einsum('shd,de->she', tensor, swap_matrix(tensor.shape[-1]), precision=lax.Precision.HIGHEST)
    return tensor * cosine_table[:, None, :] + swapped * sine_table[:, None, :]

def layer_norm(states, shift_row, scale_row):
    values_f32 = states.astype(jnp.float32)
    average = lax.optimization_barrier(jnp.mean(values_f32, axis=-1, keepdims=True))
    centred = values_f32 - average
    variance = lax.optimization_barrier(jnp.mean(centred * centred, axis=-1, keepdims=True))
    return (centred * lax.rsqrt(variance + 1e-06) * (1.0 + scale_row) + shift_row).astype(jnp.bfloat16)

def attend(query_rot, key_rot, values_proj):
    seq_len, head_count, head_dim = query_rot.shape
    block_rows = min(512, seq_len)
    blocks = query_rot.reshape(seq_len // block_rows, block_rows, head_count, head_dim)
    keys_f32 = key_rot.astype(jnp.float32)
    values_f32 = values_proj.astype(jnp.float32)

    def one_block(query_block):
        scores = jnp.einsum('qhd,khd->hqk', query_block.astype(jnp.float32), keys_f32) * head_dim ** (-0.5)
        top_score = lax.optimization_barrier(jnp.max(scores, axis=-1, keepdims=True))
        expo_scores = jnp.exp(scores - top_score)
        probabilities = (expo_scores / lax.optimization_barrier(jnp.sum(expo_scores, axis=-1, keepdims=True))).astype(jnp.bfloat16)
        return jnp.einsum('hqk,khd->qhd', probabilities.astype(jnp.float32), values_f32).astype(jnp.bfloat16)
    outputs = lax.map(one_block, blocks)
    return outputs.reshape(seq_len, head_count * head_dim)

def reference(hidden_states, modulation, query_weight, key_weight, value_weight, query_mask, key_mask, value_mask, query_gain, key_gain):
    zero_bf = jnp.zeros((), jnp.bfloat16)
    masked_query = jnp.where(keep_pattern(query_mask), query_weight, zero_bf)
    masked_key = jnp.where(keep_pattern(key_mask), key_weight, zero_bf)
    masked_value = jnp.where(keep_pattern(value_mask), value_weight, zero_bf)
    cosine_table, sine_table = rope_tables(SEQ, HEAD_DIM)

    def one_sample(inputs):
        states, modulate = inputs
        normed = layer_norm(states, modulate[0], modulate[1])
        queries = jnp.dot(normed, masked_query, preferred_element_type=jnp.float32)
        keys_proj = jnp.dot(normed, masked_key, preferred_element_type=jnp.float32)
        values_proj = jnp.dot(normed, masked_value, preferred_element_type=jnp.float32).astype(jnp.bfloat16)
        query_sq = lax.optimization_barrier(jnp.sum(queries * queries, axis=1))
        key_sq = lax.optimization_barrier(jnp.sum(keys_proj * keys_proj, axis=1))
        queries = queries * lax.rsqrt(query_sq / D + 1e-06)[:, None] * query_gain
        keys_proj = keys_proj * lax.rsqrt(key_sq / D + 1e-06)[:, None] * key_gain
        query_rot = rotate_pairs(queries.reshape(SEQ, HEADS, HEAD_DIM), cosine_table, sine_table).astype(jnp.bfloat16)
        key_rot = rotate_pairs(keys_proj.reshape(SEQ, HEADS, HEAD_DIM), cosine_table, sine_table).astype(jnp.bfloat16)
        attended = attend(query_rot, key_rot, values_proj.reshape(SEQ, HEADS, HEAD_DIM))
        return (attended, normed)
    attended, normed_all = lax.map(one_sample, (hidden_states, modulation))
    flat = normed_all.reshape(BATCH * SEQ, D)
    gram = lax.dot_general(flat, flat, (((0,), (0,)), ((), ())), preferred_element_type=jnp.float32)
    gram = gram / (BATCH * SEQ)
    return (attended, gram.reshape(N_SP, D // N_SP, D))
```

```python
import functools

import jax
import jax.numpy as jnp
from jax import lax
from jax.experimental import pallas as pl
from jax.experimental.pallas import tpu as pltpu
from jax.sharding import Mesh
from jax.sharding import PartitionSpec as P

HEAD_DIM = 128
HEIGHT = 16
WIDTH = 16
XH, Z, C, Y, XL = 2, 4, 2, 4, 2
AXES = ("xh", "z", "c", "y", "xl")
TOK = 128
D = 5120
COLS = 640
ROWS = 320
HALF = D // 2
HEADS = 5
BF16, F32, I32 = jnp.bfloat16, jnp.float32, jnp.int32
MIB = 1 << 20


def linear(xh, z, c, y, xl):
    return (((xh * Z + z) * C + c) * Y + y) * XL + xl


def permute(x, move):
    pairs = []
    for xh in range(XH):
        for z in range(Z):
            for c in range(C):
                for y in range(Y):
                    for xl in range(XL):
                        pairs.append((linear(xh, z, c, y, xl), linear(*move(xh, z, c, y, xl))))
    return lax.ppermute(x, AXES, pairs)


def turn(c):
    return 1 if c == 0 else -1


def ring_y(x):
    return permute(x, lambda xh, z, c, y, xl: (xh, z, c, (y + turn(c)) % Y, xl))


def ring_z(x):
    return permute(x, lambda xh, z, c, y, xl: (xh, (z + turn(c)) % Z, c, y, xl))


def swap_xl(x):
    return permute(x, lambda xh, z, c, y, xl: (xh, z, c, y, 1 - xl))


def swap_xh(x):
    return permute(x, lambda xh, z, c, y, xl: (1 - xh, z, c, y, xl))


def swap_c(x):
    return permute(x, lambda xh, z, c, y, xl: (xh, z, 1 - c, y, xl))


def to_owner(x, s, dx):
    return permute(x, lambda xh, z, c, y, xl: (xh, z, c, (y - turn(c) * s) % Y, xl ^ dx))


def mask_kernel(wq, wk, wv, mq, mk, mv, out):
    group = lax.broadcasted_iota(I32, (ROWS, ROWS // 4), 0) // 4
    spread = (group == lax.broadcasted_iota(I32, (ROWS, ROWS // 4), 1)).astype(F32).astype(BF16)
    slot = lax.broadcasted_iota(I32, (ROWS, COLS), 0) % 4
    for i, (w, m) in enumerate(((wq, mq), (wk, mk), (wv, mv))):
        p = m[...]
        bits = jnp.where(p == 0, 3, jnp.where(p == 1, 5, jnp.where(p == 2, 9, jnp.where(p == 3, 6, jnp.where(p == 4, 10, 12)))))
        rows = jnp.dot(spread, bits.astype(F32).astype(BF16), preferred_element_type=F32).astype(I32)
        kept = (lax.shift_right_logical(rows, slot) & 1) == 1
        out[:, i * COLS : (i + 1) * COLS] = jnp.where(kept, w[...].astype(F32), 0.0).astype(BF16)


def masked_weights(wq, wk, wv, mq, mk, mv):
    return pl.pallas_call(
        mask_kernel,
        out_shape=jax.ShapeDtypeStruct((ROWS, 3 * COLS), BF16),
        compiler_params=pltpu.CompilerParams(vmem_limit_bytes=24 * MIB),
        cost_estimate=pl.CostEstimate(flops=10**8, bytes_accessed=3 * 10**6, transcendentals=0),
        name="masked_weights",
    )(wq, wk, wv, mq, mk, mv)


def norm_kernel(h, modulation, out):
    x = h[0].astype(F32)
    average = jnp.mean(x, axis=-1, keepdims=True)
    centred = x - average
    variance = jnp.mean(centred * centred, axis=-1, keepdims=True)
    scale = 1.0 + modulation[0, 1:2, :]
    out[...] = (centred * lax.rsqrt(variance + 1e-06) * scale + modulation[0, 0:1, :]).astype(BF16)


def layer_norm(h, modulation):
    rows = 32
    return pl.pallas_call(
        norm_kernel,
        out_shape=jax.ShapeDtypeStruct((TOK, D), BF16),
        grid=(TOK // rows,),
        in_specs=[pl.BlockSpec((1, rows, D), lambda i: (0, i, 0)), pl.BlockSpec((1, 2, D), lambda i: (0, 0, 0))],
        out_specs=pl.BlockSpec((rows, D), lambda i: (i, 0)),
        compiler_params=pltpu.CompilerParams(vmem_limit_bytes=24 * MIB),
        cost_estimate=pl.CostEstimate(flops=10**7, bytes_accessed=3 * 10**6, transcendentals=0),
        name="layer_norm",
    )(h, modulation)


def project_kernel(n_x, first, last, place, *refs):
    xs, refs = refs[:n_x], refs[n_x:]
    ws, refs = refs[:8], refs[8:]
    if not first:
        acc_in, refs = refs[0], refs[1:]
    if last:
        q_out, k_out, v_out, sq_out, x_v, w_v, sem_x, sem_w = refs
    else:
        acc_out, x_v, w_v, sem_x, sem_w = refs
    column = pl.multiple_of(place[0] * HALF, HALF)
    copies_w = []
    for j in range(8):
        row = pl.multiple_of(place[1 + j] * ROWS, ROWS)
        copies_w.append(pltpu.make_async_copy(ws[j], w_v.at[pl.ds(row, ROWS), :], sem_w.at[j]))
    copies_x = [
        pltpu.make_async_copy(xs[j].at[:, pl.ds(column, HALF)], x_v.at[j * TOK : (j + 1) * TOK, :], sem_x.at[j])
        for j in range(n_x)
    ]
    for copy in copies_w:
        copy.start()
    for copy in copies_x:
        copy.start()
    for copy in copies_w:
        copy.wait()
    for copy in copies_x:
        copy.wait()
    tile = 512

    @pl.loop(0, n_x * TOK // tile)
    def _(i):
        rows = pl.ds(pl.multiple_of(i * tile, tile), tile)
        x = x_v[rows, :]
        for part in range(3):
            cols = slice(part * COLS, (part + 1) * COLS)
            y = jnp.dot(x, w_v[:, cols], preferred_element_type=F32)
            if not first:
                y = y + acc_in[rows, cols]
            if not last:
                acc_out[rows, cols] = y
            elif part == 2:
                v_out[rows, :] = y.astype(BF16)
            else:
                (q_out if part == 0 else k_out)[rows, :] = y
                squares = y * y
                lanes = sum(squares[:, h * 128 : (h + 1) * 128] for h in range(HEADS))
                for b in range(tile // TOK):
                    line = jnp.sum(lanes[b * TOK : (b + 1) * TOK, :].T, axis=0, keepdims=True)
                    sq_out[place[9 + i * (tile // TOK) + b], part : part + 1, :] = line


def project(place, xs, ws, acc=None, last=False):
    n_x = len(xs)
    first = acc is None
    rows = n_x * TOK
    anywhere = pl.BlockSpec(memory_space=pl.ANY)
    vmem = pl.BlockSpec(memory_space=pltpu.VMEM)
    if last:
        out_shape = (
            jax.ShapeDtypeStruct((rows, COLS), F32),
            jax.ShapeDtypeStruct((rows, COLS), F32),
            jax.ShapeDtypeStruct((rows, COLS), BF16),
            jax.ShapeDtypeStruct((8, 8, TOK), F32),
        )
        out_specs = (vmem,) * 4
    else:
        out_shape = jax.ShapeDtypeStruct((rows, 3 * COLS), F32)
        out_specs = vmem
    return pl.pallas_call(
        functools.partial(project_kernel, n_x, first, last),
        out_shape=out_shape,
        in_specs=[pl.BlockSpec(memory_space=pltpu.SMEM)] + [anywhere] * (n_x + 8) + ([] if first else [vmem]),
        out_specs=out_specs,
        scratch_shapes=[
            pltpu.VMEM((rows, HALF), BF16),
            pltpu.VMEM((HALF, 3 * COLS), BF16),
            pltpu.SemaphoreType.DMA((n_x,)),
            pltpu.SemaphoreType.DMA((8,)),
        ],
        compiler_params=pltpu.CompilerParams(vmem_limit_bytes=48 * MIB),
        cost_estimate=pl.CostEstimate(
            flops=2 * rows * HALF * 3 * COLS, bytes_accessed=15 * 10**6, transcendentals=0
        ),
        name=f"project_{n_x}_{int(first)}_{int(last)}",
    )(place, *xs, *ws, *([] if first else [acc]))


def gram_kernel(tokens, place, *refs):
    xs, (out, x_v, own, o_v, sem_x, sem_o) = refs[:8], refs[8:]
    copies = [
        pltpu.make_async_copy(xs[j], x_v.at[j * TOK : (j + 1) * TOK, :], sem_x.at[j]) for j in range(8)
    ]
    for copy in copies:
        copy.start()
    for copy in copies:
        copy.wait()
    column = pl.multiple_of(place[0] * COLS, COLS)
    own[...] = x_v[:, pl.ds(column, COLS)].T

    @pl.loop(0, D // COLS)
    def _(i):
        cols = pl.ds(pl.multiple_of(i * COLS, COLS), COLS)
        slot = i % 2

        def send(j, at):
            to = pl.ds(pl.multiple_of(j * COLS, COLS), COLS)
            return pltpu.make_async_copy(o_v.at[at], out.at[:, to], sem_o.at[at])

        @pl.when(i >= 2)
        def _():
            send(i - 2, slot).wait()

        y = jnp.dot(own[...], x_v[:, cols], preferred_element_type=F32)
        o_v[slot] = (y * (1.0 / tokens)).astype(BF16)
        send(i, slot).start()

    for j in range(D // COLS - 2, D // COLS):
        to = slice(j * COLS, (j + 1) * COLS)
        pltpu.make_async_copy(o_v.at[j % 2], out.at[:, to], sem_o.at[j % 2]).wait()


def gram_rows(place, xs, tokens):
    anywhere = pl.BlockSpec(memory_space=pl.ANY)
    return pl.pallas_call(
        functools.partial(gram_kernel, tokens),
        out_shape=jax.ShapeDtypeStruct((COLS, D), BF16),
        in_specs=[pl.BlockSpec(memory_space=pltpu.SMEM)] + [anywhere] * 8,
        out_specs=anywhere,
        scratch_shapes=[
            pltpu.VMEM((8 * TOK, D), BF16),
            pltpu.VMEM((COLS, 8 * TOK), BF16),
            pltpu.VMEM((2, COLS, COLS), BF16),
            pltpu.SemaphoreType.DMA((8,)),
            pltpu.SemaphoreType.DMA((2,)),
        ],
        compiler_params=pltpu.CompilerParams(vmem_limit_bytes=40 * MIB),
        cost_estimate=pl.CostEstimate(flops=2 * COLS * 1024 * D, bytes_accessed=17 * 10**6, transcendentals=0),
        name="gram_rows",
    )(place, *xs)


def rope_tables(place):
    inside = jnp.arange(TOK, dtype=I32)[None, :]
    blocks = place[:, None]
    frame_pos = jnp.broadcast_to(blocks // 2, (8, TOK)).reshape(-1).astype(F32)
    row_pos = (blocks % 2 * 8 + inside // WIDTH).reshape(-1).astype(F32)
    col_pos = jnp.broadcast_to(inside % WIDTH, (8, TOK)).reshape(-1).astype(F32)
    half_dim = HEAD_DIM // 2
    spatial = HEAD_DIM // 6
    temporal = half_dim - 2 * spatial
    entry = jnp.arange(HEAD_DIM, dtype=I32)
    pair_ids = entry // 2
    exponent = jnp.where(
        pair_ids < temporal,
        2.0 * pair_ids / (2.0 * temporal),
        jnp.where(
            pair_ids < temporal + spatial,
            2.0 * (pair_ids - temporal) / (2.0 * spatial),
            2.0 * (pair_ids - temporal - spatial) / (2.0 * spatial),
        ),
    ).astype(F32)
    frequency = jnp.power(jnp.float32(10000.0), -exponent)
    chosen_pos = jnp.where(
        pair_ids[None, :] < temporal,
        frame_pos[:, None],
        jnp.where(pair_ids[None, :] < temporal + spatial, row_pos[:, None], col_pos[:, None]),
    )
    angles = chosen_pos * frequency[None, :]
    sine = jnp.sin(angles)
    even = (entry % 2 == 0)[None, :]
    return jnp.cos(angles), jnp.where(even, -sine, 0.0), jnp.where(even, 0.0, sine)


def attend_kernel(place, q_ref, k_ref, v_ref, *refs):
    squares, (gain_q, gain_k, cosine, sine_l, sine_r), outs = refs[:8], refs[8:13], refs[13:21]
    scale_v, k_v = refs[21:]

    @pl.when(pl.program_id(0) == 0)
    def _():
        total = squares[0][...]
        for other in squares[1:]:
            total = total + other[...]
        factor = lax.rsqrt(total / D + 1e-06)
        scale_v[2] = jnp.zeros((8 * TOK, TOK), F32)
        for b in range(8):
            scale_v[2, b * 8 : (b + 1) * 8, :] = factor[b]
        for b in range(8):
            source = place[b]
            for part in range(2):
                line = scale_v[2, pl.ds(source * 8 + part, 1), :]
                scale_v[part, b * TOK : (b + 1) * TOK, :] = jnp.broadcast_to(line, (TOK, TOK)).T

    def rotate(x, part, gain, rows):
        x = x * scale_v[part, rows, :] * gain
        left = pltpu.roll(x, HEAD_DIM - 1, 1)
        right = pltpu.roll(x, 1, 1)
        return (x * cosine[rows, :] + left * sine_l[rows, :] + right * sine_r[rows, :]).astype(BF16)

    every = slice(0, 8 * TOK)
    keys = rotate(k_ref[...], 1, gain_k[...], every)
    values = v_ref[...]
    factor = HEAD_DIM ** (-0.5) * 1.4426950408889634
    tile = 256
    for i in range(8 * TOK // tile):
        rows = slice(i * tile, (i + 1) * tile)
        q = rotate(q_ref[rows, :], 0, gain_q[...], rows)
        scores = lax.dot_general(q, keys, (((1,), (1,)), ((), ())), preferred_element_type=F32)
        top = jnp.max(scores, axis=-1, keepdims=True)
        weights = jnp.exp2((scores - top) * factor)
        total = jnp.sum(weights, axis=-1, keepdims=True)
        probabilities = (weights * (1.0 / total)).astype(BF16)
        out = jnp.dot(probabilities, values, preferred_element_type=F32).astype(BF16)
        for b in range(tile // TOK):
            outs[i * (tile // TOK) + b][...] = out[b * TOK : (b + 1) * TOK, :]


def attend(place, q, k, v, squares, gain_q, gain_k, tables):
    head = pl.BlockSpec((8 * TOK, HEAD_DIM), lambda h: (0, h))
    gain = pl.BlockSpec((1, HEAD_DIM), lambda h: (0, h))
    table = pl.BlockSpec((8 * TOK, HEAD_DIM), lambda h: (0, 0))
    square = pl.BlockSpec((8, 8, TOK), lambda h: (0, 0, 0))
    return pl.pallas_call(
        attend_kernel,
        out_shape=(jax.ShapeDtypeStruct((TOK, COLS), BF16),) * 8,
        grid=(HEADS,),
        in_specs=[pl.BlockSpec(memory_space=pltpu.SMEM), head, head, head]
        + [square] * 8
        + [gain, gain, table, table, table],
        out_specs=(pl.BlockSpec((TOK, HEAD_DIM), lambda h: (0, h)),) * 8,
        scratch_shapes=[pltpu.VMEM((3, 8 * TOK, TOK), F32), pltpu.VMEM((8 * TOK, HEAD_DIM), BF16)],
        compiler_params=pltpu.CompilerParams(vmem_limit_bytes=40 * MIB),
        cost_estimate=pl.CostEstimate(flops=4 * 1024 * 1024 * COLS, bytes_accessed=10**7, transcendentals=5 * 2**20),
        name="attend",
    )(place, q, k, v, *squares, gain_q[None], gain_k[None], *tables)


def gather_kernel(place, *refs):
    pieces, out, sem = refs[:8], refs[8], refs[9]
    copies = []
    for j in range(8):
        column = pl.multiple_of(place[j] * COLS, COLS)
        copies.append(pltpu.make_async_copy(pieces[j], out.at[0, :, pl.ds(column, COLS)], sem.at[j]))
    for copy in copies:
        copy.start()
    for copy in copies:
        copy.wait()


def gather_columns(place, pieces):
    anywhere = pl.BlockSpec(memory_space=pl.ANY)
    return pl.pallas_call(
        gather_kernel,
        out_shape=jax.ShapeDtypeStruct((1, TOK, D), BF16),
        in_specs=[pl.BlockSpec(memory_space=pltpu.SMEM)] + [anywhere] * 8,
        out_specs=anywhere,
        scratch_shapes=[pltpu.SemaphoreType.DMA((8,))],
        cost_estimate=pl.CostEstimate(flops=0, bytes_accessed=3 * 10**6, transcendentals=0),
        name="gather_columns",
    )(place, *pieces)


def per_device(h, modulation, wq, wk, wv, mq, mk, mv, gain_q, gain_k):
    xh, z, c, y, xl = (lax.axis_index(a).astype(I32) for a in AXES)
    way = 1 - 2 * c
    blocks = [(s, dx) for dx in range(2) for s in range(4)]
    canonical = jnp.stack([((y - way * s) % Y) * 2 + (xl ^ dx) for s, dx in blocks])
    sources = jnp.stack([((y + way * s) % Y) * 2 + (xl ^ dx) for s, dx in blocks])
    rows = [((z - way * s) % Z) * 2 + c for s in range(4)] + [((z + way * s) % Z) * 2 + 1 - c for s in range(4)]
    place_1 = jnp.concatenate([jnp.stack([xh] + rows), canonical])
    place_2 = jnp.concatenate([jnp.stack([1 - xh] + rows), canonical])
    me = (y * 2 + xl)[None]

    w0 = masked_weights(wq, wk, wv, mq, mk, mv)
    x0 = layer_norm(h, modulation)

    w1 = ring_z(w0)
    p0 = swap_xh(w0)
    x1 = ring_y(x0)
    b0 = swap_xl(x0)
    w2 = ring_z(w1)
    x2 = ring_y(x1)
    w3 = ring_z(w2)
    x3 = ring_y(x2)
    own = [w0, w1, w2, w3]
    own_half = own + [swap_c(w) for w in own]
    p1 = ring_z(p0)
    b1 = ring_y(b0)
    b3 = swap_xl(x3)
    p2 = ring_z(p1)
    b2 = ring_y(b1)
    p3 = ring_z(p2)
    other = [p0, p1, p2, p3]
    other_half = other + [swap_c(w) for w in other]
    xs_a = [x0, x1, x2, x3]
    xs_b = [b0, b1, b2, b3]
    tables = rope_tables(canonical)

    acc_a = project(place_1, xs_a, own_half)
    acc_b = project(place_1, xs_b, own_half)
    product = gram_rows(me, xs_a + xs_b, XH * Z * C * 8 * TOK)
    gram = lax.psum_scatter(product, ("xh", "z", "c"), scatter_dimension=0, tiled=True)
    acc = jnp.concatenate([acc_a, acc_b])
    q, k, v, squares = project(place_2, xs_a + xs_b, other_half, acc, True)
    all_squares = [squares] + [to_owner(squares, s, dx) for s, dx in blocks[1:]]
    outs = attend(canonical, q, k, v, all_squares, gain_q, gain_k, tables)
    pieces = [outs[0]] + [to_owner(o, s, dx) for o, (s, dx) in zip(outs[1:], blocks[1:])]
    return gather_columns(sources, pieces), gram.astype(F32)[None]


def solution(mesh):
    fine = Mesh(mesh.devices.reshape(XH, Z, C, Y, XL), AXES)
    grp, sp = ("xh", "z", "c"), ("y", "xl")
    return jax.shard_map(
        per_device,
        mesh=fine,
        in_specs=(
            P(grp, sp, None),
            P(grp, None, None),
            P(grp, sp),
            P(grp, sp),
            P(grp, sp),
            P(grp, sp),
            P(grp, sp),
            P(grp, sp),
            P(sp),
            P(sp),
        ),
        out_specs=(P(grp, sp, None), P(sp, grp, None)),
        check_vma=False,
    )
```

```python
import functools

import jax
import jax.numpy as jnp
from jax import lax
from jax.experimental import pallas as pl
from jax.experimental.pallas import tpu as pltpu
from jax.sharding import Mesh
from jax.sharding import PartitionSpec as P

HEAD_DIM = 128
HEIGHT = 16
WIDTH = 16
XH, Z, C, Y, XL = 2, 4, 2, 4, 2
AXES = ("xh", "z", "c", "y", "xl")
TOK = 128
D = 5120
COLS = 640
ROWS = 320
HALF = D // 2
HEADS = 5
BF16, F32, I32 = jnp.bfloat16, jnp.float32, jnp.int32
MIB = 1 << 20


def linear(xh, z, c, y, xl):
    return (((xh * Z + z) * C + c) * Y + y) * XL + xl


def permute(x, move):
    pairs = []
    for xh in range(XH):
        for z in range(Z):
            for c in range(C):
                for y in range(Y):
                    for xl in range(XL):
                        pairs.append((linear(xh, z, c, y, xl), linear(*move(xh, z, c, y, xl))))
    return lax.ppermute(x, AXES, pairs)


def turn(c):
    return 1 if c == 0 else -1


def ring_y(x):
    return permute(x, lambda xh, z, c, y, xl: (xh, z, c, (y + turn(c)) % Y, xl))


def ring_z(x):
    return permute(x, lambda xh, z, c, y, xl: (xh, (z + turn(c)) % Z, c, y, xl))


def swap_xl(x):
    return permute(x, lambda xh, z, c, y, xl: (xh, z, c, y, 1 - xl))


def swap_xh(x):
    return permute(x, lambda xh, z, c, y, xl: (1 - xh, z, c, y, xl))


def swap_c(x):
    return permute(x, lambda xh, z, c, y, xl: (xh, z, 1 - c, y, xl))


def to_owner(x, s, dx):
    return permute(x, lambda xh, z, c, y, xl: (xh, z, c, (y - turn(c) * s) % Y, xl ^ dx))


def stage(*arrays):
    return lax.optimization_barrier(arrays)


def mask_kernel(wq, wk, wv, mq, mk, mv, out):
    group = lax.broadcasted_iota(I32, (ROWS, ROWS // 4), 0) // 4
    spread = (group == lax.broadcasted_iota(I32, (ROWS, ROWS // 4), 1)).astype(F32).astype(BF16)
    slot = lax.broadcasted_iota(I32, (ROWS, COLS), 0) % 4
    for i, (w, m) in enumerate(((wq, mq), (wk, mk), (wv, mv))):
        p = m[...]
        bits = jnp.where(p == 0, 3, jnp.where(p == 1, 5, jnp.where(p == 2, 9, jnp.where(p == 3, 6, jnp.where(p == 4, 10, 12)))))
        rows = jnp.dot(spread, bits.astype(F32).astype(BF16), preferred_element_type=F32).astype(I32)
        kept = (lax.shift_right_logical(rows, slot) & 1) == 1
        out[:, i * COLS : (i + 1) * COLS] = jnp.where(kept, w[...].astype(F32), 0.0).astype(BF16)


def masked_weights(wq, wk, wv, mq, mk, mv):
    return pl.pallas_call(
        mask_kernel,
        out_shape=jax.ShapeDtypeStruct((ROWS, 3 * COLS), BF16),
        compiler_params=pltpu.CompilerParams(vmem_limit_bytes=24 * MIB),
        cost_estimate=pl.CostEstimate(flops=10**8, bytes_accessed=3 * 10**6, transcendentals=0),
        name="masked_weights",
    )(wq, wk, wv, mq, mk, mv)


def norm_kernel(h, modulation, out):
    x = h[0].astype(F32)
    average = jnp.mean(x, axis=-1, keepdims=True)
    centred = x - average
    variance = jnp.mean(centred * centred, axis=-1, keepdims=True)
    scale = 1.0 + modulation[0, 1:2, :]
    out[...] = (centred * lax.rsqrt(variance + 1e-06) * scale + modulation[0, 0:1, :]).astype(BF16)


def layer_norm(h, modulation):
    rows = 32
    return pl.pallas_call(
        norm_kernel,
        out_shape=jax.ShapeDtypeStruct((TOK, D), BF16),
        grid=(TOK // rows,),
        in_specs=[pl.BlockSpec((1, rows, D), lambda i: (0, i, 0)), pl.BlockSpec((1, 2, D), lambda i: (0, 0, 0))],
        out_specs=pl.BlockSpec((rows, D), lambda i: (i, 0)),
        compiler_params=pltpu.CompilerParams(vmem_limit_bytes=24 * MIB),
        cost_estimate=pl.CostEstimate(flops=10**7, bytes_accessed=3 * 10**6, transcendentals=0),
        name="layer_norm",
    )(h, modulation)


def project_kernel(n_x, first, last, place, *refs):
    xs, refs = refs[:n_x], refs[n_x:]
    ws, refs = refs[:8], refs[8:]
    if not first:
        accs, refs = refs[:2], refs[2:]
    if last:
        q_out, k_out, v_out, sq_out, x_v, w_v, sem_x, sem_w = refs[:8]
    else:
        acc_out, x_v, w_v, sem_x, sem_w = refs[:5]
    column = pl.multiple_of(place[0] * HALF, HALF)
    tile = 4 * TOK
    tiles = n_x // 4
    copies_x = [
        pltpu.make_async_copy(xs[j].at[:, pl.ds(column, HALF)], x_v.at[j * TOK : (j + 1) * TOK, :], sem_x.at[j])
        for j in range(n_x)
    ]
    copies_w, copies_a = [], []
    for part in range(3):
        cols = slice(part * COLS, (part + 1) * COLS)
        for j in range(8):
            row = pl.multiple_of(place[1 + j] * ROWS, ROWS)
            copies_w.append(
                pltpu.make_async_copy(ws[j].at[:, cols], w_v.at[pl.ds(row, ROWS), cols], sem_w.at[part * 8 + j])
            )
        if not first:
            a_v, sem_a = refs[8:]
            for i in range(2):
                copies_a.append(
                    pltpu.make_async_copy(accs[i].at[:, cols], a_v.at[i, :, cols], sem_a.at[part * 2 + i])
                )
    for copy in copies_w[:8] + copies_x + copies_a[:2]:
        copy.start()
    for part in (1, 2):
        for copy in copies_w[part * 8 : part * 8 + 8] + copies_a[part * 2 : part * 2 + 2]:
            copy.start()
    for part in range(3):
        cols = slice(part * COLS, (part + 1) * COLS)
        for copy in copies_w[part * 8 : part * 8 + 8]:
            copy.wait()
        for i in range(tiles):
            rows = slice(i * tile, (i + 1) * tile)
            if part == 0:
                for copy in copies_x[i * 4 : i * 4 + 4]:
                    copy.wait()
            y = jnp.dot(x_v[rows, :], w_v[:, cols], preferred_element_type=F32)
            if not first:
                copies_a[part * 2 + i].wait()
                y = y + a_v[i, :, cols]
            if not last:
                acc_out[rows, cols] = y
            elif part == 2:
                v_out[rows, :] = y.astype(BF16)
            else:
                (q_out if part == 0 else k_out)[rows, :] = y
                squares = y * y
                lanes = sum(squares[:, h * 128 : (h + 1) * 128] for h in range(HEADS))
                for b in range(4):
                    line = jnp.sum(lanes[b * TOK : (b + 1) * TOK, :].T, axis=0, keepdims=True)
                    sq_out[place[9 + i * 4 + b], part : part + 1, :] = line


def project(place, xs, ws, accs=(), last=False):
    n_x = len(xs)
    first = not accs
    rows = n_x * TOK
    anywhere = pl.BlockSpec(memory_space=pl.ANY)
    vmem = pl.BlockSpec(memory_space=pltpu.VMEM)
    scratch = [
        pltpu.VMEM((rows, HALF), BF16),
        pltpu.VMEM((HALF, 3 * COLS), BF16),
        pltpu.SemaphoreType.DMA((n_x,)),
        pltpu.SemaphoreType.DMA((24,)),
    ]
    if accs:
        scratch += [pltpu.VMEM((2, 4 * TOK, 3 * COLS), F32), pltpu.SemaphoreType.DMA((6,))]
    if last:
        out_shape = (
            jax.ShapeDtypeStruct((rows, COLS), F32),
            jax.ShapeDtypeStruct((rows, COLS), F32),
            jax.ShapeDtypeStruct((rows, COLS), BF16),
            jax.ShapeDtypeStruct((8, 8, TOK), F32),
        )
        out_specs = (vmem,) * 4
    else:
        out_shape = jax.ShapeDtypeStruct((rows, 3 * COLS), F32)
        out_specs = vmem
    return pl.pallas_call(
        functools.partial(project_kernel, n_x, first, last),
        out_shape=out_shape,
        in_specs=[pl.BlockSpec(memory_space=pltpu.SMEM)] + [anywhere] * (n_x + 8 + len(accs)),
        out_specs=out_specs,
        scratch_shapes=scratch,
        compiler_params=pltpu.CompilerParams(vmem_limit_bytes=44 * MIB),
        cost_estimate=pl.CostEstimate(
            flops=2 * rows * HALF * 3 * COLS, bytes_accessed=15 * 10**6, transcendentals=0
        ),
        name=f"project_{n_x}_{int(first)}_{int(last)}",
    )(place, *xs, *ws, *accs)


def gram_kernel(tokens, place, *refs):
    xs, (mine, theirs, x_v, own, o_v, sem_x, sem_o) = refs[:8], refs[8:]
    copies = [
        pltpu.make_async_copy(xs[j], x_v.at[j * TOK : (j + 1) * TOK, :], sem_x.at[j]) for j in range(8)
    ]
    for copy in copies:
        copy.start()
    line = lax.broadcasted_iota(I32, (COLS, COLS), 0)
    part = line // ROWS
    z = line // 80 % Z
    xh = line // 40 % XH
    core = jnp.where(part == 0, place[1], 1 - place[1])
    source = ((xh * Z + z) * C + core) * 40 + line % 40
    order = (source == lax.broadcasted_iota(I32, (COLS, COLS), 1)).astype(F32).astype(BF16)
    for copy in copies:
        copy.wait()
    column = pl.multiple_of(place[0] * COLS, COLS)
    own[...] = lax.dot_general(
        order, x_v[:, pl.ds(column, COLS)], (((1,), (1,)), ((), ())), preferred_element_type=F32
    ).astype(BF16)
    n = D // COLS
    sends = [None] * n
    for i in range(n):
        cols = slice(i * COLS, (i + 1) * COLS)
        if i >= 2:
            for copy in sends[i - 2]:
                copy.wait()
        y = jnp.dot(own[...], x_v[:, cols], preferred_element_type=F32)
        o_v[i % 2] = (y * (1.0 / tokens)).astype(BF16)
        sends[i] = [
            pltpu.make_async_copy(o_v.at[i % 2, j * ROWS : (j + 1) * ROWS, :], out.at[:, cols], sem_o.at[i % 2, j])
            for j, out in enumerate((mine, theirs))
        ]
        for copy in sends[i]:
            copy.start()
    for copy in sends[n - 2] + sends[n - 1]:
        copy.wait()


def gram_rows(place, xs, tokens):
    anywhere = pl.BlockSpec(memory_space=pl.ANY)
    return pl.pallas_call(
        functools.partial(gram_kernel, tokens),
        out_shape=(jax.ShapeDtypeStruct((ROWS, D), BF16),) * 2,
        in_specs=[pl.BlockSpec(memory_space=pltpu.SMEM)] + [anywhere] * 8,
        out_specs=(anywhere,) * 2,
        scratch_shapes=[
            pltpu.VMEM((8 * TOK, D), BF16),
            pltpu.VMEM((COLS, 8 * TOK), BF16),
            pltpu.VMEM((2, COLS, COLS), BF16),
            pltpu.SemaphoreType.DMA((8,)),
            pltpu.SemaphoreType.DMA((2, 2)),
        ],
        compiler_params=pltpu.CompilerParams(vmem_limit_bytes=40 * MIB),
        cost_estimate=pl.CostEstimate(flops=2 * COLS * 1024 * D, bytes_accessed=17 * 10**6, transcendentals=0),
        name="gram_rows",
    )(place, *xs)


def rope_tables(place):
    inside = jnp.arange(TOK, dtype=I32)[None, :]
    blocks = place[:, None]
    frame_pos = jnp.broadcast_to(blocks // 2, (8, TOK)).reshape(-1).astype(F32)
    row_pos = (blocks % 2 * 8 + inside // WIDTH).reshape(-1).astype(F32)
    col_pos = jnp.broadcast_to(inside % WIDTH, (8, TOK)).reshape(-1).astype(F32)
    half_dim = HEAD_DIM // 2
    spatial = HEAD_DIM // 6
    temporal = half_dim - 2 * spatial
    entry = jnp.arange(HEAD_DIM, dtype=I32)
    pair_ids = entry // 2
    exponent = jnp.where(
        pair_ids < temporal,
        2.0 * pair_ids / (2.0 * temporal),
        jnp.where(
            pair_ids < temporal + spatial,
            2.0 * (pair_ids - temporal) / (2.0 * spatial),
            2.0 * (pair_ids - temporal - spatial) / (2.0 * spatial),
        ),
    ).astype(F32)
    frequency = jnp.power(jnp.float32(10000.0), -exponent)
    chosen_pos = jnp.where(
        pair_ids[None, :] < temporal,
        frame_pos[:, None],
        jnp.where(pair_ids[None, :] < temporal + spatial, row_pos[:, None], col_pos[:, None]),
    )
    angles = chosen_pos * frequency[None, :]
    sine = jnp.sin(angles)
    even = (entry % 2 == 0)[None, :]
    return jnp.cos(angles), jnp.where(even, -sine, 0.0), jnp.where(even, 0.0, sine)


def attend_kernel(place, q_ref, k_ref, v_ref, *refs):
    squares, (gain_q, gain_k, cosine, sine_l, sine_r), outs = refs[:8], refs[8:13], refs[13:21]
    scale_v, k_v = refs[21:]

    @pl.when(pl.program_id(0) == 0)
    def _():
        total = squares[0][...]
        for other in squares[1:]:
            total = total + other[...]
        factor = lax.rsqrt(total / D + 1e-06)
        scale_v[2] = jnp.zeros((8 * TOK, TOK), F32)
        for b in range(8):
            scale_v[2, b * 8 : (b + 1) * 8, :] = factor[b]
        for b in range(8):
            source = place[b]
            for part in range(2):
                line = scale_v[2, pl.ds(source * 8 + part, 1), :]
                scale_v[part, b * TOK : (b + 1) * TOK, :] = jnp.broadcast_to(line, (TOK, TOK)).T

    def rotate(x, part, gain, rows):
        x = x * scale_v[part, rows, :] * gain
        left = pltpu.roll(x, HEAD_DIM - 1, 1)
        right = pltpu.roll(x, 1, 1)
        return (x * cosine[rows, :] + left * sine_l[rows, :] + right * sine_r[rows, :]).astype(BF16)

    every = slice(0, 8 * TOK)
    keys = rotate(k_ref[...], 1, gain_k[...], every)
    values = v_ref[...]
    factor = HEAD_DIM ** (-0.5) * 1.4426950408889634
    tile = 256
    for i in range(8 * TOK // tile):
        rows = slice(i * tile, (i + 1) * tile)
        q = rotate(q_ref[rows, :], 0, gain_q[...], rows)
        scores = lax.dot_general(q, keys, (((1,), (1,)), ((), ())), preferred_element_type=F32)
        top = jnp.max(scores, axis=-1, keepdims=True)
        weights = jnp.exp2((scores - top) * factor)
        total = jnp.sum(weights, axis=-1, keepdims=True)
        out = jnp.dot(weights.astype(BF16), values, preferred_element_type=F32)
        out = (out * (1.0 / total)).astype(BF16)
        for b in range(tile // TOK):
            outs[i * (tile // TOK) + b][...] = out[b * TOK : (b + 1) * TOK, :]


def attend(place, q, k, v, squares, gain_q, gain_k, tables):
    head = pl.BlockSpec((8 * TOK, HEAD_DIM), lambda h: (0, h))
    gain = pl.BlockSpec((1, HEAD_DIM), lambda h: (0, h))
    table = pl.BlockSpec((8 * TOK, HEAD_DIM), lambda h: (0, 0))
    square = pl.BlockSpec((8, 8, TOK), lambda h: (0, 0, 0))
    return pl.pallas_call(
        attend_kernel,
        out_shape=(jax.ShapeDtypeStruct((TOK, COLS), BF16),) * 8,
        grid=(HEADS,),
        in_specs=[pl.BlockSpec(memory_space=pltpu.SMEM), head, head, head]
        + [square] * 8
        + [gain, gain, table, table, table],
        out_specs=(pl.BlockSpec((TOK, HEAD_DIM), lambda h: (0, h)),) * 8,
        scratch_shapes=[pltpu.VMEM((3, 8 * TOK, TOK), F32), pltpu.VMEM((8 * TOK, HEAD_DIM), BF16)],
        compiler_params=pltpu.CompilerParams(vmem_limit_bytes=40 * MIB),
        cost_estimate=pl.CostEstimate(flops=4 * 1024 * 1024 * COLS, bytes_accessed=10**7, transcendentals=5 * 2**20),
        name="attend",
    )(place, q, k, v, *squares, gain_q[None], gain_k[None], *tables)


def gather_kernel(place, *refs):
    pieces, out = refs[:8], refs[8]
    for j in range(8):
        column = pl.multiple_of(place[j] * COLS, COLS)
        out[0, :, pl.ds(column, COLS)] = pieces[j][...]


def gather_columns(place, pieces):
    vmem = pl.BlockSpec(memory_space=pltpu.VMEM)
    return pl.pallas_call(
        gather_kernel,
        out_shape=jax.ShapeDtypeStruct((1, TOK, D), BF16),
        in_specs=[pl.BlockSpec(memory_space=pltpu.SMEM)] + [vmem] * 8,
        out_specs=vmem,
        compiler_params=pltpu.CompilerParams(vmem_limit_bytes=16 * MIB),
        cost_estimate=pl.CostEstimate(flops=0, bytes_accessed=3 * 10**6, transcendentals=0),
        name="gather_columns",
    )(place, *pieces)


def per_device(h, modulation, wq, wk, wv, mq, mk, mv, gain_q, gain_k):
    xh, z, c, y, xl = (lax.axis_index(a).astype(I32) for a in AXES)
    way = 1 - 2 * c
    blocks = [(s, dx) for dx in range(2) for s in range(4)]
    canonical = jnp.stack([((y - way * s) % Y) * 2 + (xl ^ dx) for s, dx in blocks])
    sources = jnp.stack([((y + way * s) % Y) * 2 + (xl ^ dx) for s, dx in blocks])
    rows = [((z - way * s) % Z) * 2 + c for s in range(4)] + [((z + way * s) % Z) * 2 + 1 - c for s in range(4)]
    place_1 = jnp.concatenate([jnp.stack([xh] + rows), canonical])
    place_2 = jnp.concatenate([jnp.stack([1 - xh] + rows), canonical])
    me = jnp.stack([y * 2 + xl, c])

    w0 = masked_weights(wq, wk, wv, mq, mk, mv)
    x0 = layer_norm(h, modulation)
    half = TOK // 2

    x1, w1, b0_lo, p0 = stage(ring_y(x0), ring_z(w0), swap_xl(x0[:half]), swap_xh(w0))
    x2, w2, b0_hi, e0, e1 = stage(ring_y(x1), ring_z(w1), swap_xl(x0[half:]), swap_c(w0), swap_c(w1))
    b0 = jnp.concatenate([b0_lo, b0_hi])
    x3, w3, b2_lo, e2, f0 = stage(ring_y(x2), ring_z(w2), swap_xl(x2[:half]), swap_c(w2), swap_c(p0))
    e3 = swap_c(w3)
    own_half = [w0, w1, w2, w3, e0, e1, e2, e3]
    xs_a = [x0, x1, x2, x3]
    acc_a = project(place_1, xs_a, own_half)
    tables = rope_tables(canonical)
    b1, p1, b2_hi, e3, acc_a, tables = stage(ring_y(b0), ring_z(p0), swap_xl(x2[half:]), e3, acc_a, tables)
    b2 = jnp.concatenate([b2_lo, b2_hi])
    b3, p2, f1 = stage(ring_y(b2), ring_z(p1), swap_c(p1))
    xs_b = [b0, b1, b2, b3]
    f2 = swap_c(p2)
    f2, *xs_b = stage(f2, *xs_b)
    mine, theirs = gram_rows(me, xs_a + xs_b, XH * Z * C * 8 * TOK)
    theirs, *xs_b = stage(theirs, *xs_b)
    pair = (mine.astype(F32) + swap_c(theirs).astype(F32)).astype(BF16)
    summed = lax.psum_scatter(pair, "z", scatter_dimension=0, tiled=True)
    acc_b = project(place_1, xs_b, own_half)
    p3, acc_b = stage(ring_z(p2), acc_b)
    f3 = swap_c(p3)
    other_half = [p0, p1, p2, p3, f0, f1, f2, f3]

    q, k, v, squares = project(place_2, xs_a + xs_b, other_half, [acc_a, acc_b], True)
    all_squares = [squares] + [to_owner(squares, s, dx) for s, dx in blocks[1:]]
    outs = attend(canonical, q, k, v, all_squares, gain_q, gain_k, tables)
    *outs, summed = stage(*outs, summed)
    summed = summed.reshape(XH, 40, D)
    kept = lax.dynamic_index_in_dim(summed, xh, 0, False)
    sent = lax.dynamic_index_in_dim(summed, 1 - xh, 0, False)
    gram = kept.astype(F32) + swap_xh(sent).astype(F32)
    pieces = [outs[0]] + [to_owner(o, s, dx) for o, (s, dx) in zip(outs[1:], blocks[1:])]
    return gather_columns(sources, pieces), gram[None]


def solution(mesh):
    fine = Mesh(mesh.devices.reshape(XH, Z, C, Y, XL), AXES)
    grp, sp = ("xh", "z", "c"), ("y", "xl")
    return jax.shard_map(
        per_device,
        mesh=fine,
        in_specs=(
            P(grp, sp, None),
            P(grp, None, None),
            P(grp, sp),
            P(grp, sp),
            P(grp, sp),
            P(grp, sp),
            P(grp, sp),
            P(grp, sp),
            P(sp),
            P(sp),
        ),
        out_specs=(P(grp, sp, None), P(sp, grp, None)),
        check_vma=False,
    )
```

```python
import functools

import jax
import jax.numpy as jnp
from jax import lax
from jax.experimental import pallas as pl
from jax.experimental.pallas import tpu as pltpu
from jax.sharding import Mesh
from jax.sharding import PartitionSpec as P

HEAD_DIM = 128
HEIGHT = 16
WIDTH = 16
XH, Z, C, Y, XL = 2, 4, 2, 4, 2
AXES = ("xh", "z", "c", "y", "xl")
TOK = 128
D = 5120
COLS = 640
ROWS = 320
HALF = D // 2
HEADS = 5
BF16, F32, I32 = jnp.bfloat16, jnp.float32, jnp.int32
MIB = 1 << 20


def linear(xh, z, c, y, xl):
    return (((xh * Z + z) * C + c) * Y + y) * XL + xl


def permute(x, move):
    pairs = []
    for xh in range(XH):
        for z in range(Z):
            for c in range(C):
                for y in range(Y):
                    for xl in range(XL):
                        pairs.append((linear(xh, z, c, y, xl), linear(*move(xh, z, c, y, xl))))
    return lax.ppermute(x, AXES, pairs)


def turn(c):
    return 1 if c == 0 else -1


def ring_y(x):
    return permute(x, lambda xh, z, c, y, xl: (xh, z, c, (y + turn(c)) % Y, xl))


def ring_z(x):
    return permute(x, lambda xh, z, c, y, xl: (xh, (z + turn(c)) % Z, c, y, xl))


def swap_xl(x):
    return permute(x, lambda xh, z, c, y, xl: (xh, z, c, y, 1 - xl))


def swap_xh(x):
    return permute(x, lambda xh, z, c, y, xl: (1 - xh, z, c, y, xl))


def swap_c(x):
    return permute(x, lambda xh, z, c, y, xl: (xh, z, 1 - c, y, xl))


def to_owner(x, s, dx):
    return permute(x, lambda xh, z, c, y, xl: (xh, z, c, (y - turn(c) * s) % Y, xl ^ dx))


def stage(*arrays):
    return lax.optimization_barrier(arrays)


def mask_kernel(wq, wk, wv, mq, mk, mv, out):
    group = lax.broadcasted_iota(I32, (ROWS, ROWS // 4), 0) // 4
    spread = (group == lax.broadcasted_iota(I32, (ROWS, ROWS // 4), 1)).astype(F32).astype(BF16)
    slot = lax.broadcasted_iota(I32, (ROWS, COLS), 0) % 4
    for i, (w, m) in enumerate(((wq, mq), (wk, mk), (wv, mv))):
        p = m[...]
        bits = jnp.where(p == 0, 3, jnp.where(p == 1, 5, jnp.where(p == 2, 9, jnp.where(p == 3, 6, jnp.where(p == 4, 10, 12)))))
        rows = jnp.dot(spread, bits.astype(F32).astype(BF16), preferred_element_type=F32).astype(I32)
        kept = (lax.shift_right_logical(rows, slot) & 1) == 1
        out[:, i * COLS : (i + 1) * COLS] = jnp.where(kept, w[...].astype(F32), 0.0).astype(BF16)


def masked_weights(wq, wk, wv, mq, mk, mv):
    return pl.pallas_call(
        mask_kernel,
        out_shape=jax.ShapeDtypeStruct((ROWS, 3 * COLS), BF16),
        compiler_params=pltpu.CompilerParams(vmem_limit_bytes=24 * MIB),
        cost_estimate=pl.CostEstimate(flops=10**8, bytes_accessed=3 * 10**6, transcendentals=0),
        name="masked_weights",
    )(wq, wk, wv, mq, mk, mv)


def norm_kernel(h, modulation, out):
    x = h[0].astype(F32)
    average = jnp.mean(x, axis=-1, keepdims=True)
    centred = x - average
    variance = jnp.mean(centred * centred, axis=-1, keepdims=True)
    scale = 1.0 + modulation[0, 1:2, :]
    out[...] = (centred * lax.rsqrt(variance + 1e-06) * scale + modulation[0, 0:1, :]).astype(BF16)


def layer_norm(h, modulation):
    rows = 32
    return pl.pallas_call(
        norm_kernel,
        out_shape=jax.ShapeDtypeStruct((TOK, D), BF16),
        grid=(TOK // rows,),
        in_specs=[pl.BlockSpec((1, rows, D), lambda i: (0, i, 0)), pl.BlockSpec((1, 2, D), lambda i: (0, 0, 0))],
        out_specs=pl.BlockSpec((rows, D), lambda i: (i, 0)),
        compiler_params=pltpu.CompilerParams(vmem_limit_bytes=24 * MIB),
        cost_estimate=pl.CostEstimate(flops=10**7, bytes_accessed=3 * 10**6, transcendentals=0),
        name="layer_norm",
    )(h, modulation)


def project_kernel(n_x, parts, added, last, place, *refs):
    tiles = n_x // 4
    tile = 4 * TOK
    width = sum(parts)
    begin = 3 * COLS - width if last and width == COLS else 0
    xs, refs = refs[:n_x], refs[n_x:]
    ws, refs = refs[:8], refs[8:]
    accs, refs = refs[: 2 * added], refs[2 * added :]
    n_out = len(parts) if last else 1
    outs, refs = refs[:n_out], refs[n_out:]
    if last and width > COLS:
        sq_out, refs = refs[0], refs[1:]
    x_v, w_v, y_v, sem_x, sem_w, sem_y, *refs = refs
    if added:
        a_v, sem_a = refs
    column = pl.multiple_of(place[0] * HALF, HALF)
    copies_x = [
        pltpu.make_async_copy(xs[j].at[:, pl.ds(column, HALF)], x_v.at[j * TOK : (j + 1) * TOK, :], sem_x.at[j])
        for j in range(n_x)
    ]
    edges = [sum(parts[:p]) for p in range(len(parts) + 1)]
    copies_w, copies_a = [], []
    for p in range(len(parts)):
        here = slice(edges[p], edges[p + 1])
        there = slice(begin + edges[p], begin + edges[p + 1])
        some = []
        for j in range(8):
            row = pl.multiple_of(place[1 + j] * ROWS, ROWS)
            some.append(pltpu.make_async_copy(ws[j].at[:, there], w_v.at[pl.ds(row, ROWS), here], sem_w.at[p * 8 + j]))
        copies_w.append(some)
        if added:
            copies_a.append(
                [
                    pltpu.make_async_copy(accs[i].at[:, there], a_v.at[i, :, here], sem_a.at[p * 2 + i])
                    for i in range(2)
                ]
            )
    for copy in copies_w[0] + copies_x + (copies_a[0] if added else []):
        copy.start()
    for p in range(1, len(parts)):
        for copy in copies_w[p] + (copies_a[p] if added else []):
            copy.start()
    sent = []
    for p in range(len(parts)):
        here = slice(edges[p], edges[p + 1])
        for copy in copies_w[p]:
            copy.wait()
        for i in range(tiles):
            rows = slice(i * tile, (i + 1) * tile)
            if p == 0:
                for copy in copies_x[i * 4 : i * 4 + 4]:
                    copy.wait()
            y = jnp.dot(x_v[rows, :], w_v[:, here], preferred_element_type=F32)
            if added:
                copies_a[p][i].wait()
                y = y + a_v[i, :, here]
            y_v[rows, here] = y.astype(y_v.dtype)
            out = outs[p].at[rows, :] if last else outs[0].at[rows, here]
            copy = pltpu.make_async_copy(y_v.at[rows, here], out, sem_y.at[p * tiles + i])
            copy.start()
            sent.append(copy)
            if last and width > COLS:
                squares = y * y
                lanes = sum(squares[:, h * 128 : (h + 1) * 128] for h in range(HEADS))
                for b in range(4):
                    line = jnp.sum(lanes[b * TOK : (b + 1) * TOK, :].T, axis=0, keepdims=True)
                    sq_out[place[9 + i * 4 + b], p : p + 1, :] = line
    for copy in sent:
        copy.wait()


def project(place, xs, ws, parts, accs=(), last=False):
    n_x = len(xs)
    rows = n_x * TOK
    width = sum(parts)
    hbm = pl.BlockSpec(memory_space=pltpu.HBM)
    kind = BF16 if last and width == COLS else F32
    scratch = [
        pltpu.VMEM((rows, HALF), BF16),
        pltpu.VMEM((HALF, width), BF16),
        pltpu.VMEM((rows, width), kind),
        pltpu.SemaphoreType.DMA((n_x,)),
        pltpu.SemaphoreType.DMA((8 * len(parts),)),
        pltpu.SemaphoreType.DMA((n_x // 4 * len(parts),)),
    ]
    if accs:
        scratch += [pltpu.VMEM((2, 4 * TOK, width), F32), pltpu.SemaphoreType.DMA((2 * len(parts),))]
    if last:
        out_shape = [jax.ShapeDtypeStruct((rows, part), kind) for part in parts]
        out_specs = [hbm] * len(parts)
        if width > COLS:
            out_shape.append(jax.ShapeDtypeStruct((8, 8, TOK), F32))
            out_specs.append(pl.BlockSpec(memory_space=pltpu.VMEM))
    else:
        out_shape = [jax.ShapeDtypeStruct((rows, width), F32)]
        out_specs = [hbm]
    return pl.pallas_call(
        functools.partial(project_kernel, n_x, parts, bool(accs), last),
        out_shape=out_shape,
        in_specs=[pl.BlockSpec(memory_space=pltpu.SMEM)] + [hbm] * (n_x + 8 + len(accs)),
        out_specs=out_specs,
        scratch_shapes=scratch,
        compiler_params=pltpu.CompilerParams(vmem_limit_bytes=48 * MIB),
        cost_estimate=pl.CostEstimate(
            flops=2 * rows * HALF * width, bytes_accessed=15 * 10**6, transcendentals=0
        ),
        name=f"project_{n_x}_{width}_{int(last)}",
    )(place, *xs, *ws, *accs)


def gram_kernel(tokens, place, *refs):
    xs, (mine, theirs, own_x, x_v, own, o_v, sem_own, sem_x, sem_o) = refs[:8], refs[8:]
    n = 4
    step = D // n
    column = pl.multiple_of(place[0] * COLS, COLS)
    first = [
        pltpu.make_async_copy(xs[j].at[:, pl.ds(column, COLS)], own_x.at[j * TOK : (j + 1) * TOK, :], sem_own.at[j])
        for j in range(8)
    ]
    rest = []
    for i in range(n):
        cols = slice(i * step, (i + 1) * step)
        rest.append(
            [
                pltpu.make_async_copy(xs[j].at[:, cols], x_v.at[j * TOK : (j + 1) * TOK, cols], sem_x.at[i, j])
                for j in range(8)
            ]
        )
    for some in [first] + rest:
        for copy in some:
            copy.start()
    line = lax.broadcasted_iota(I32, (COLS, COLS), 0)
    part = line // ROWS
    z = line // 80 % Z
    xh = line // 40 % XH
    core = jnp.where(part == 0, place[1], 1 - place[1])
    source = ((xh * Z + z) * C + core) * 40 + line % 40
    order = (source == lax.broadcasted_iota(I32, (COLS, COLS), 1)).astype(F32).astype(BF16)
    for copy in first:
        copy.wait()
    own[...] = lax.dot_general(
        order, own_x[...], (((1,), (1,)), ((), ())), preferred_element_type=F32
    ).astype(BF16)
    sends = []
    for i in range(n):
        cols = slice(i * step, (i + 1) * step)
        for copy in rest[i]:
            copy.wait()
        for j, out in enumerate((mine, theirs)):
            rows = slice(j * ROWS, (j + 1) * ROWS)
            y = jnp.dot(own[rows, :], x_v[:, cols], preferred_element_type=F32)
            o_v[rows, cols] = (y * (1.0 / tokens)).astype(BF16)
            copy = pltpu.make_async_copy(o_v.at[rows, cols], out.at[:, cols], sem_o.at[i, j])
            copy.start()
            sends.append(copy)
    for copy in sends:
        copy.wait()


def gram_rows(place, xs, tokens):
    hbm = pl.BlockSpec(memory_space=pltpu.HBM)
    return pl.pallas_call(
        functools.partial(gram_kernel, tokens),
        out_shape=(jax.ShapeDtypeStruct((ROWS, D), BF16),) * 2,
        in_specs=[pl.BlockSpec(memory_space=pltpu.SMEM)] + [hbm] * 8,
        out_specs=(hbm,) * 2,
        scratch_shapes=[
            pltpu.VMEM((8 * TOK, COLS), BF16),
            pltpu.VMEM((8 * TOK, D), BF16),
            pltpu.VMEM((COLS, 8 * TOK), BF16),
            pltpu.VMEM((COLS, D), BF16),
            pltpu.SemaphoreType.DMA((8,)),
            pltpu.SemaphoreType.DMA((4, 8)),
            pltpu.SemaphoreType.DMA((4, 2)),
        ],
        compiler_params=pltpu.CompilerParams(vmem_limit_bytes=48 * MIB),
        cost_estimate=pl.CostEstimate(flops=2 * COLS * 1024 * D, bytes_accessed=17 * 10**6, transcendentals=0),
        name="gram_rows",
    )(place, *xs)


def rope_tables(place):
    inside = jnp.arange(TOK, dtype=I32)[None, :]
    blocks = place[:, None]
    frame_pos = jnp.broadcast_to(blocks // 2, (8, TOK)).reshape(-1).astype(F32)
    row_pos = (blocks % 2 * 8 + inside // WIDTH).reshape(-1).astype(F32)
    col_pos = jnp.broadcast_to(inside % WIDTH, (8, TOK)).reshape(-1).astype(F32)
    half_dim = HEAD_DIM // 2
    spatial = HEAD_DIM // 6
    temporal = half_dim - 2 * spatial
    entry = jnp.arange(HEAD_DIM, dtype=I32)
    pair_ids = entry // 2
    exponent = jnp.where(
        pair_ids < temporal,
        2.0 * pair_ids / (2.0 * temporal),
        jnp.where(
            pair_ids < temporal + spatial,
            2.0 * (pair_ids - temporal) / (2.0 * spatial),
            2.0 * (pair_ids - temporal - spatial) / (2.0 * spatial),
        ),
    ).astype(F32)
    frequency = jnp.power(jnp.float32(10000.0), -exponent)
    chosen_pos = jnp.where(
        pair_ids[None, :] < temporal,
        frame_pos[:, None],
        jnp.where(pair_ids[None, :] < temporal + spatial, row_pos[:, None], col_pos[:, None]),
    )
    angles = chosen_pos * frequency[None, :]
    sine = jnp.sin(angles)
    even = (entry % 2 == 0)[None, :]
    return jnp.cos(angles), jnp.where(even, -sine, 0.0), jnp.where(even, 0.0, sine)


def attend_kernel(half, place, q_ref, k_ref, v_ref, *refs):
    squares, (gain_q, gain_k, cosine, sine_l, sine_r), outs = refs[:2], refs[2:7], refs[7:11]
    scale_v, line_v = refs[11:]

    @pl.when(pl.program_id(0) == 0)
    def _():
        factor = lax.rsqrt((squares[0][...] + squares[1][...]) / D + 1e-06)
        for b in range(8):
            line_v[b * 8 : (b + 1) * 8, :] = factor[b]
        for b in range(8):
            source = place[b]
            for part in range(2):
                line = line_v[pl.ds(source * 8 + part, 1), :]
                scale_v[part, b * TOK : (b + 1) * TOK, :] = jnp.broadcast_to(line, (TOK, TOK)).T

    def rotate(x, part, gain, rows):
        x = x * scale_v[part, rows, :] * gain
        left = pltpu.roll(x, HEAD_DIM - 1, 1)
        right = pltpu.roll(x, 1, 1)
        return (x * cosine[rows, :] + left * sine_l[rows, :] + right * sine_r[rows, :]).astype(BF16)

    every = slice(0, 8 * TOK)
    keys = rotate(k_ref[...], 1, gain_k[...], every)
    values = v_ref[...]
    factor = HEAD_DIM ** (-0.5) * 1.4426950408889634
    tile = 256
    for i in range(4 * TOK // tile):
        inside = slice(i * tile, (i + 1) * tile)
        rows = slice(half * 4 * TOK + i * tile, half * 4 * TOK + (i + 1) * tile)
        q = rotate(q_ref[inside, :], 0, gain_q[...], rows)
        scores = lax.dot_general(q, keys, (((1,), (1,)), ((), ())), preferred_element_type=F32)
        top = jnp.max(scores, axis=-1, keepdims=True)
        weights = jnp.exp2((scores - top) * factor)
        total = jnp.sum(weights, axis=-1, keepdims=True)
        out = jnp.dot(weights.astype(BF16), values, preferred_element_type=F32)
        out = (out * (1.0 / total)).astype(BF16)
        for b in range(tile // TOK):
            outs[i * (tile // TOK) + b][...] = out[b * TOK : (b + 1) * TOK, :]


def attend(half, place, q, k, v, squares, gain_q, gain_k, tables):
    query = pl.BlockSpec((4 * TOK, HEAD_DIM), lambda h: (half, h))
    head = pl.BlockSpec((8 * TOK, HEAD_DIM), lambda h: (0, h))
    gain = pl.BlockSpec((1, HEAD_DIM), lambda h: (0, h))
    table = pl.BlockSpec((8 * TOK, HEAD_DIM), lambda h: (0, 0))
    square = pl.BlockSpec((8, 8, TOK), lambda h: (0, 0, 0))
    return pl.pallas_call(
        functools.partial(attend_kernel, half),
        out_shape=(jax.ShapeDtypeStruct((TOK, COLS), BF16),) * 4,
        grid=(HEADS,),
        in_specs=[pl.BlockSpec(memory_space=pltpu.SMEM), query, head, head]
        + [square] * 2
        + [gain, gain, table, table, table],
        out_specs=(pl.BlockSpec((TOK, HEAD_DIM), lambda h: (0, h)),) * 4,
        scratch_shapes=[pltpu.VMEM((2, 8 * TOK, TOK), F32), pltpu.VMEM((64, TOK), F32)],
        compiler_params=pltpu.CompilerParams(vmem_limit_bytes=48 * MIB),
        cost_estimate=pl.CostEstimate(flops=2 * 1024 * 1024 * COLS, bytes_accessed=10**7, transcendentals=5 * 2**19),
        name=f"attend_{half}",
    )(place, q, k, v, *squares, gain_q[None], gain_k[None], *tables)


def gather_kernel(place, *refs):
    pieces, out = refs[:8], refs[8]
    for j in range(8):
        column = pl.multiple_of(place[j] * COLS, COLS)
        out[0, :, pl.ds(column, COLS)] = pieces[j][...]


def gather_columns(place, pieces):
    vmem = pl.BlockSpec(memory_space=pltpu.VMEM)
    return pl.pallas_call(
        gather_kernel,
        out_shape=jax.ShapeDtypeStruct((1, TOK, D), BF16),
        in_specs=[pl.BlockSpec(memory_space=pltpu.SMEM)] + [vmem] * 8,
        out_specs=vmem,
        compiler_params=pltpu.CompilerParams(vmem_limit_bytes=16 * MIB),
        cost_estimate=pl.CostEstimate(flops=0, bytes_accessed=3 * 10**6, transcendentals=0),
        name="gather_columns",
    )(place, *pieces)


def per_device(h, modulation, wq, wk, wv, mq, mk, mv, gain_q, gain_k):
    xh, z, c, y, xl = (lax.axis_index(a).astype(I32) for a in AXES)
    way = 1 - 2 * c
    blocks = [(s, dx) for dx in range(2) for s in range(4)]
    canonical = jnp.stack([((y - way * s) % Y) * 2 + (xl ^ dx) for s, dx in blocks])
    sources = jnp.stack([((y + way * s) % Y) * 2 + (xl ^ dx) for s, dx in blocks])
    rows = [((z - way * s) % Z) * 2 + c for s in range(4)] + [((z + way * s) % Z) * 2 + 1 - c for s in range(4)]
    place_1 = jnp.concatenate([jnp.stack([xh] + rows), canonical])
    place_2 = jnp.concatenate([jnp.stack([1 - xh] + rows), canonical])
    me = jnp.stack([y * 2 + xl, c])

    w0 = masked_weights(wq, wk, wv, mq, mk, mv)
    x0 = layer_norm(h, modulation)
    half = TOK // 2

    wide = (768, 768, 384)
    half = TOK // 2
    x1, w1, b0_lo, p0_lo = stage(ring_y(x0), ring_z(w0), swap_xl(x0[:half]), swap_xh(w0[:64]))
    x2, w2, b0_hi, p0_mid, e0 = stage(
        ring_y(x1), ring_z(w1), swap_xl(x0[half:]), swap_xh(w0[64:128]), swap_c(w0)
    )
    x3, w3, p0_hi, e1, e2 = stage(ring_y(x2), ring_z(w2), swap_xh(w0[128:]), swap_c(w1), swap_c(w2))
    b0 = jnp.concatenate([b0_lo, b0_hi])
    p0 = jnp.concatenate([p0_lo, p0_mid, p0_hi])
    e3 = swap_c(w3)
    own_half = [w0, w1, w2, w3, e0, e1, e2, e3]
    xs_a = [x0, x1, x2, x3]
    (acc_a,) = project(place_1, xs_a, own_half, wide)
    tables = rope_tables(canonical)
    b1, p1, b3_lo, acc_a, *tables = stage(ring_y(b0), ring_z(p0), swap_xl(x3[:half]), acc_a, *tables)
    f0 = swap_c(p0)
    f1 = swap_c(p1)
    b2, p2, b3_hi, f0, f1 = stage(ring_y(b1), ring_z(p1), swap_xl(x3[half:]), f0, f1)
    b3 = jnp.concatenate([b3_lo, b3_hi])
    xs_b = [b0, b1, b2, b3]

    f2 = swap_c(p2)
    mine, theirs = gram_rows(me, xs_a + xs_b, XH * Z * C * 8 * TOK)
    theirs, p3, f2, *xs_b = stage(theirs, ring_z(p2), f2, *xs_b)
    f3 = swap_c(p3)
    moved = swap_c(theirs)
    (acc_b,) = project(place_1, xs_b, own_half, wide)
    moved, f3, acc_b = stage(moved, f3, acc_b)
    pair = (mine.astype(F32) + moved.astype(F32)).astype(BF16)
    summed = lax.psum_scatter(pair, "z", scatter_dimension=0, tiled=True)
    pair, acc_a = stage(pair, acc_a)
    other_half = [p0, p1, p2, p3, f0, f1, f2, f3]

    accs = [acc_a, acc_b]
    q, k, squares = project(place_2, xs_a + xs_b, other_half, (COLS, COLS), accs, True)
    ring = squares + sum(to_owner(squares, s, 0) for s in range(1, Y))
    xs_a[0], squares = stage(xs_a[0], squares)
    (v,) = project(place_2, xs_a + xs_b, other_half, (COLS,), accs, True)
    ring, v = stage(ring, v)
    both = [ring, swap_xl(ring)]
    late = attend(1, canonical, q, k, v, both, gain_q, gain_k, tables)
    pieces_late = [to_owner(o, s, 1) for o, s in zip(late, range(Y))]
    early = attend(0, canonical, q, stage(k, late[0])[0], v, both, gain_q, gain_k, tables)
    *rest, summed = stage(*early, *pieces_late, summed)
    early, pieces_late = rest[:4], rest[4:]
    summed = summed.reshape(XH, 40, D)
    kept = lax.dynamic_index_in_dim(summed, xh, 0, False)
    sent = lax.dynamic_index_in_dim(summed, 1 - xh, 0, False)
    gram = kept.astype(F32) + swap_xh(sent).astype(F32)
    pieces = [early[0]] + [to_owner(o, s, 0) for o, s in zip(early[1:], range(1, Y))]
    return gather_columns(sources, pieces + pieces_late), gram[None]


def solution(mesh):
    fine = Mesh(mesh.devices.reshape(XH, Z, C, Y, XL), AXES)
    grp, sp = ("xh", "z", "c"), ("y", "xl")
    return jax.shard_map(
        per_device,
        mesh=fine,
        in_specs=(
            P(grp, sp, None),
            P(grp, None, None),
            P(grp, sp),
            P(grp, sp),
            P(grp, sp),
            P(grp, sp),
            P(grp, sp),
            P(grp, sp),
            P(sp),
            P(sp),
        ),
        out_specs=(P(grp, sp, None), P(sp, grp, None)),
        check_vma=False,
    )
```

```python
import functools

import jax
import jax.numpy as jnp
from jax import lax
from jax.experimental import pallas as pl
from jax.experimental.pallas import tpu as pltpu
from jax.sharding import Mesh
from jax.sharding import PartitionSpec as P

HEAD_DIM = 128
HEIGHT = 16
WIDTH = 16
XH, Z, C, Y, XL = 2, 4, 2, 4, 2
AXES = ("xh", "z", "c", "y", "xl")
TOK = 128
D = 5120
COLS = 640
ROWS = 320
HALF = D // 2
HEADS = 5
BF16, F32, I32 = jnp.bfloat16, jnp.float32, jnp.int32
MIB = 1 << 20


def linear(xh, z, c, y, xl):
    return (((xh * Z + z) * C + c) * Y + y) * XL + xl


def permute(x, move):
    pairs = []
    for xh in range(XH):
        for z in range(Z):
            for c in range(C):
                for y in range(Y):
                    for xl in range(XL):
                        pairs.append((linear(xh, z, c, y, xl), linear(*move(xh, z, c, y, xl))))
    return lax.ppermute(x, AXES, pairs)


def turn(c):
    return 1 if c == 0 else -1


def ring_y(x):
    return permute(x, lambda xh, z, c, y, xl: (xh, z, c, (y + turn(c)) % Y, xl))


def ring_z(x):
    return permute(x, lambda xh, z, c, y, xl: (xh, (z + turn(c)) % Z, c, y, xl))


def swap_xl(x):
    return permute(x, lambda xh, z, c, y, xl: (xh, z, c, y, 1 - xl))


def swap_xh(x):
    return permute(x, lambda xh, z, c, y, xl: (1 - xh, z, c, y, xl))


def swap_c(x):
    return permute(x, lambda xh, z, c, y, xl: (xh, z, 1 - c, y, xl))


def to_owner(x, s, dx):
    return permute(x, lambda xh, z, c, y, xl: (xh, z, c, (y - turn(c) * s) % Y, xl ^ dx))


def stage(*arrays):
    return lax.optimization_barrier(arrays)


HALVES = ((0, TOK // 2), (TOK // 2, TOK))
CHUNKS = ((0, 64), (64, 128), (128, ROWS))


def begin_kernel(h, modulation, wq, wk, wv, mq, mk, mv, *refs):
    x_out, x_lo, x_hi, w_out, w_lo, w_mid, w_hi = refs[:7]
    h_v, mod_v, w_v, m_v, sem = refs[7:]
    pairs = [(h.at[0], h_v), (modulation.at[0], mod_v)]
    pairs += [(w, w_v.at[i]) for i, w in enumerate((wq, wk, wv))]
    pairs += [(m, m_v.at[i]) for i, m in enumerate((mq, mk, mv))]
    copies = [pltpu.make_async_copy(source, target, sem.at[i]) for i, (source, target) in enumerate(pairs)]
    for copy in copies:
        copy.start()
    for copy in copies[:2]:
        copy.wait()
    scale = 1.0 + mod_v[1:2, :]
    shift = mod_v[0:1, :]
    step = 32
    for i in range(TOK // step):
        x = h_v[i * step : (i + 1) * step, :].astype(F32)
        average = jnp.mean(x, axis=-1, keepdims=True)
        centred = x - average
        variance = jnp.mean(centred * centred, axis=-1, keepdims=True)
        y = (centred * lax.rsqrt(variance + 1e-06) * scale + shift).astype(BF16)
        x_out[i * step : (i + 1) * step, :] = y
        piece, at = (x_lo, i * step) if i * step < TOK // 2 else (x_hi, i * step - TOK // 2)
        piece[at : at + step, :] = y
    group = lax.broadcasted_iota(I32, (ROWS, ROWS // 4), 0) // 4
    spread = (group == lax.broadcasted_iota(I32, (ROWS, ROWS // 4), 1)).astype(F32).astype(BF16)
    slot = lax.broadcasted_iota(I32, (ROWS, COLS), 0) % 4
    for i in range(3):
        copies[2 + i].wait()
        copies[5 + i].wait()
        p = m_v[i]
        bits = jnp.where(p == 0, 3, jnp.where(p == 1, 5, jnp.where(p == 2, 9, jnp.where(p == 3, 6, jnp.where(p == 4, 10, 12)))))
        rows = jnp.dot(spread, bits.astype(F32).astype(BF16), preferred_element_type=F32).astype(I32)
        kept = (lax.shift_right_logical(rows, slot) & 1) == 1
        masked = jnp.where(kept, w_v[i].astype(F32), 0.0).astype(BF16)
        cols = slice(i * COLS, (i + 1) * COLS)
        w_out[:, cols] = masked
        for piece, (low, high) in zip((w_lo, w_mid, w_hi), CHUNKS):
            piece[:, cols] = masked[low:high, :]


def begin(h, modulation, wq, wk, wv, mq, mk, mv):
    hbm = pl.BlockSpec(memory_space=pltpu.HBM)
    vmem = pl.BlockSpec(memory_space=pltpu.VMEM)
    rows = [TOK, TOK // 2, TOK // 2]
    tall = [ROWS] + [high - low for low, high in CHUNKS]
    out = [jax.ShapeDtypeStruct((r, D), BF16) for r in rows] + [jax.ShapeDtypeStruct((r, 3 * COLS), BF16) for r in tall]
    return pl.pallas_call(
        begin_kernel,
        out_shape=out,
        in_specs=[hbm] * 8,
        out_specs=[vmem] * 7,
        scratch_shapes=[
            pltpu.VMEM((TOK, D), BF16),
            pltpu.VMEM((2, D), F32),
            pltpu.VMEM((3, ROWS, COLS), BF16),
            pltpu.VMEM((3, ROWS // 4, COLS), I32),
            pltpu.SemaphoreType.DMA((8,)),
        ],
        compiler_params=pltpu.CompilerParams(vmem_limit_bytes=60 * MIB),
        cost_estimate=pl.CostEstimate(flops=10**8, bytes_accessed=6 * 10**6, transcendentals=0),
        name="norm_and_mask",
    )(h, modulation, wq, wk, wv, mq, mk, mv)


def offsets(xs):
    starts = [0]
    for x in xs:
        starts.append(starts[-1] + x.shape[0])
    return starts


def edges_of(parts):
    return [sum(parts[:p]) for p in range(len(parts) + 1)]


def start_all(copies):
    for copy in copies:
        copy.start()


def wait_all(copies):
    for copy in copies:
        copy.wait()


def in_order(groups):
    start_all(groups[0])
    begun = [1]

    def need(g):
        wait_all(groups[g])
        while begun[0] < min(g + 3, len(groups)):
            start_all(groups[begun[0]])
            begun[0] += 1

    return need


def copies_of_x(xs, x_v, sem, column):
    at = offsets(xs)
    return [
        pltpu.make_async_copy(x.at[:, pl.ds(column, HALF)], x_v.at[at[j] : at[j + 1], :], sem.at[j])
        for j, x in enumerate(xs)
    ]


def copies_of_w(place, ws, w_v, sem, there, here, base):
    out = []
    for j in range(8):
        row = pl.multiple_of(place[1 + j] * ROWS, ROWS)
        out.append(pltpu.make_async_copy(ws[j].at[:, there], w_v.at[pl.ds(row, ROWS), here], sem.at[base + j]))
    return out


def project_kernel(n_x, parts, place, *refs):
    xs, ws, (out, x_v, w_v, y_v, sem_x, sem_w, sem_y) = refs[:n_x], refs[n_x : n_x + 8], refs[n_x + 8 :]
    copies_x = copies_of_x(xs, x_v, sem_x, pl.multiple_of(place[0] * HALF, HALF))
    edges = edges_of(parts)
    here = [slice(edges[p], edges[p + 1]) for p in range(len(parts))]
    copies_w = [copies_of_w(place, ws, w_v, sem_w, cols, cols, p * 8) for p, cols in enumerate(here)]
    need = in_order([copies_w[0] + copies_x] + copies_w[1:])
    sent = []
    for p, cols in enumerate(here):
        need(p)
        y_v[:, cols] = jnp.dot(x_v[...], w_v[:, cols], preferred_element_type=F32)
        sent.append(pltpu.make_async_copy(y_v.at[:, cols], out.at[:, cols], sem_y.at[p]))
        sent[-1].start()
    wait_all(sent)


def project(place, xs, ws):
    n_x = len(xs)
    rows = offsets(xs)[-1]
    parts = (256, 512, 512, 640)
    width = 3 * COLS
    hbm = pl.BlockSpec(memory_space=pltpu.HBM)
    return pl.pallas_call(
        functools.partial(project_kernel, n_x, parts),
        out_shape=jax.ShapeDtypeStruct((rows, width), F32),
        in_specs=[pl.BlockSpec(memory_space=pltpu.SMEM)] + [hbm] * (n_x + 8),
        out_specs=hbm,
        scratch_shapes=[
            pltpu.VMEM((rows, HALF), BF16),
            pltpu.VMEM((HALF, width), BF16),
            pltpu.VMEM((rows, width), F32),
            pltpu.SemaphoreType.DMA((n_x,)),
            pltpu.SemaphoreType.DMA((8 * len(parts),)),
            pltpu.SemaphoreType.DMA((len(parts),)),
        ],
        compiler_params=pltpu.CompilerParams(vmem_limit_bytes=60 * MIB),
        cost_estimate=pl.CostEstimate(flops=2 * rows * HALF * width, bytes_accessed=15 * 10**6, transcendentals=0),
        name="project_first",
    )(place, *xs, *ws)


def finish_kernel(n_x, parts, place, *refs):
    xs, ws, accs, refs = refs[:n_x], refs[n_x : n_x + 8], refs[n_x + 8 : n_x + 10], refs[n_x + 10 :]
    qk_out, v_out, sq_out, x_v, w_v, a_v, y_v, v_v, sem_x, sem_w, sem_a, sem_y = refs
    copies_x = copies_of_x(xs, x_v, sem_x, pl.multiple_of(place[0] * HALF, HALF))
    n = len(parts)
    edges = edges_of(parts)
    middle = 4 * TOK
    groups = []
    for p in range(n):
        cols = slice(edges[p], edges[p + 1])
        copies_w = copies_of_w(place, ws, w_v, sem_w, cols, cols, p * 8)
        copies_a = [
            pltpu.make_async_copy(acc.at[:, cols], a_v.at[i * middle : (i + 1) * middle, cols], sem_a.at[p * 2 + i])
            for i, acc in enumerate(accs)
        ]
        groups += [copies_w + copies_x[:4], copies_x[4:] + copies_a] if p == 0 else [copies_w + copies_a]
    need = in_order(groups)
    need(0)
    sent = []
    for p in range(n):
        cols = slice(edges[p], edges[p + 1])
        if p:
            need(p + 1)
        for i in range(2):
            rows = slice(i * middle, (i + 1) * middle)
            y = jnp.dot(x_v[rows, :], w_v[:, cols], preferred_element_type=F32)
            if p == 0 and i == 0:
                need(1)
            y = y + a_v[rows, cols]
            if edges[p] >= 2 * COLS:
                v_v[rows, :] = y.astype(BF16)
                target, source = v_out, v_v
            else:
                y_v[rows, cols] = y
                target, source = qk_out.at[:, cols], y_v.at[:, cols]
            for part in range(2):
                low, high = max(edges[p], part * COLS), min(edges[p + 1], (part + 1) * COLS)
                if low >= high:
                    continue
                squares = y[:, low - edges[p] : high - edges[p]]
                squares = squares * squares
                lanes = sum(squares[:, h : h + 128] for h in range(0, high - low, 128))
                for b in range(4):
                    line = jnp.sum(lanes[b * TOK : (b + 1) * TOK, :].T, axis=0, keepdims=True)
                    at = place[9 + i * 4 + b]
                    if low > part * COLS:
                        line = line + sq_out[at, part : part + 1, :]
                    sq_out[at, part : part + 1, :] = line
        sent.append(pltpu.make_async_copy(source, target, sem_y.at[p]))
        sent[-1].start()
    wait_all(sent)


def finish(place, xs, ws, accs):
    parts = (256, 512, 512, 640)
    n = len(parts)
    rows = 8 * TOK
    width = 3 * COLS
    hbm = pl.BlockSpec(memory_space=pltpu.HBM)
    n_x = len(xs)
    return pl.pallas_call(
        functools.partial(finish_kernel, n_x, parts),
        out_shape=[
            jax.ShapeDtypeStruct((rows, 2 * COLS), F32),
            jax.ShapeDtypeStruct((rows, COLS), BF16),
            jax.ShapeDtypeStruct((8, 8, TOK), F32),
        ],
        in_specs=[pl.BlockSpec(memory_space=pltpu.SMEM)] + [hbm] * (n_x + 10),
        out_specs=[hbm, hbm, pl.BlockSpec(memory_space=pltpu.VMEM)],
        scratch_shapes=[
            pltpu.VMEM((rows, HALF), BF16),
            pltpu.VMEM((HALF, width), BF16),
            pltpu.VMEM((rows, width), F32),
            pltpu.VMEM((rows, 2 * COLS), F32),
            pltpu.VMEM((rows, COLS), BF16),
            pltpu.SemaphoreType.DMA((n_x,)),
            pltpu.SemaphoreType.DMA((8 * n,)),
            pltpu.SemaphoreType.DMA((2 * n,)),
            pltpu.SemaphoreType.DMA((n,)),
        ],
        compiler_params=pltpu.CompilerParams(vmem_limit_bytes=60 * MIB),
        cost_estimate=pl.CostEstimate(flops=2 * rows * HALF * width, bytes_accessed=30 * 10**6, transcendentals=0),
        name="project_last",
    )(place, *xs, *ws, *accs)


def gram_kernel(tokens, n_x, added, place, *refs):
    xs, refs = refs[:n_x], refs[n_x:]
    sums, refs = refs[: 2 * added], refs[2 * added :]
    outs, (own_x, x_v, own, o_v, sem_own, sem_x, sem_o), (*more,) = refs[:2], refs[2:9], refs[9:]
    at = offsets(xs)
    n = 4
    step = D // n
    column = pl.multiple_of(place[0] * COLS, COLS)
    first = [
        pltpu.make_async_copy(x.at[:, pl.ds(column, COLS)], own_x.at[at[j] : at[j + 1], :], sem_own.at[j])
        for j, x in enumerate(xs)
    ]
    rest = []
    for i in range(n):
        cols = slice(i * step, (i + 1) * step)
        some = [
            pltpu.make_async_copy(x.at[:, cols], x_v.at[at[j] : at[j + 1], cols], sem_x.at[i, j])
            for j, x in enumerate(xs)
        ]
        for j, old in enumerate(sums):
            s_v, sem_s = more
            some.append(
                pltpu.make_async_copy(old.at[:, cols], s_v.at[j * ROWS : (j + 1) * ROWS, cols], sem_s.at[i, j])
            )
        rest.append(some)
    need = in_order([first] + rest)
    line = lax.broadcasted_iota(I32, (COLS, COLS), 0)
    core = jnp.where(line < ROWS, 1 - place[1], place[1])
    source = ((line // 40 % XH * Z + line // 80 % Z) * C + core) * 40 + line % 40
    order = (source == lax.broadcasted_iota(I32, (COLS, COLS), 1)).astype(F32).astype(BF16)
    need(0)
    own[...] = lax.dot_general(
        order, own_x[...], (((1,), (1,)), ((), ())), preferred_element_type=F32
    ).astype(BF16)
    sends = []
    for i in range(n):
        cols = slice(i * step, (i + 1) * step)
        need(i + 1)
        for j, out in enumerate(outs):
            rows = slice(j * ROWS, (j + 1) * ROWS)
            y = jnp.dot(own[rows, :], x_v[:, cols], preferred_element_type=F32) * (1.0 / tokens)
            if added:
                y = y + more[0][rows, cols].astype(F32)
            o_v[rows, cols] = y.astype(BF16)
            sends.append(pltpu.make_async_copy(o_v.at[rows, cols], out.at[:, cols], sem_o.at[i, j]))
            sends[-1].start()
    wait_all(sends)


def gram_rows(place, xs, tokens, sums=()):
    hbm = pl.BlockSpec(memory_space=pltpu.HBM)
    n_x = len(xs)
    count = offsets(xs)[-1]
    scratch = [
        pltpu.VMEM((count, COLS), BF16),
        pltpu.VMEM((count, D), BF16),
        pltpu.VMEM((COLS, count), BF16),
        pltpu.VMEM((COLS, D), BF16),
        pltpu.SemaphoreType.DMA((n_x,)),
        pltpu.SemaphoreType.DMA((4, n_x)),
        pltpu.SemaphoreType.DMA((4, 2)),
    ]
    if sums:
        scratch += [pltpu.VMEM((COLS, D), BF16), pltpu.SemaphoreType.DMA((4, 2))]
    return pl.pallas_call(
        functools.partial(gram_kernel, tokens, n_x, bool(sums)),
        out_shape=[jax.ShapeDtypeStruct((ROWS, D), BF16)] * 2,
        in_specs=[pl.BlockSpec(memory_space=pltpu.SMEM)] + [hbm] * (n_x + len(sums)),
        out_specs=[hbm] * 2,
        scratch_shapes=scratch,
        compiler_params=pltpu.CompilerParams(vmem_limit_bytes=60 * MIB),
        cost_estimate=pl.CostEstimate(flops=2 * COLS * count * D, bytes_accessed=17 * 10**6, transcendentals=0),
        name=f"gram_rows_{count}",
    )(place, *xs, *sums)


Z_PART = ROWS // Z


def pair_kernel(place, mine, moved, own, *refs):
    outs, (m_v, sem) = refs[:3], refs[3:]
    order = (1, 3, 2, 0)
    groups = []
    for k in order:
        rows = pl.ds(pl.multiple_of(lax.rem(place[0] + k, Z) * Z_PART, 16), Z_PART)
        groups.append(
            [pltpu.make_async_copy(source.at[rows, :], m_v.at[j, k], sem.at[j, k]) for j, source in enumerate((mine, moved))]
        )
    for some in groups:
        start_all(some)
    for g, k in enumerate(order):
        wait_all(groups[g])
        y = m_v[0, k].astype(F32) + m_v[1, k].astype(F32)
        if k == 0:
            own[...] = y
        else:
            outs[k - 1][...] = y.astype(BF16)


def add_pair(place, mine, moved):
    hbm = pl.BlockSpec(memory_space=pltpu.HBM)
    vmem = pl.BlockSpec(memory_space=pltpu.VMEM)
    return pl.pallas_call(
        pair_kernel,
        out_shape=[jax.ShapeDtypeStruct((Z_PART, D), F32)] + [jax.ShapeDtypeStruct((Z_PART, D), BF16)] * 3,
        in_specs=[pl.BlockSpec(memory_space=pltpu.SMEM), hbm, hbm],
        out_specs=[vmem] * 4,
        scratch_shapes=[pltpu.VMEM((2, Z, Z_PART, D), BF16), pltpu.SemaphoreType.DMA((2, Z))],
        compiler_params=pltpu.CompilerParams(vmem_limit_bytes=60 * MIB),
        cost_estimate=pl.CostEstimate(flops=10**6, bytes_accessed=10**7, transcendentals=0),
        name="gram_pair",
    )(place, mine, moved)


def z_kernel(place, own, one, two, three, kept, sent, total_v):
    total_v[...] = own[...] + one[...].astype(F32) + two[...].astype(F32) + three[...].astype(F32)
    rows = Z_PART // XH
    kept[...] = total_v[pl.ds(pl.multiple_of(place[0] * rows, 8), rows), :]
    sent[...] = total_v[pl.ds(pl.multiple_of((1 - place[0]) * rows, 8), rows), :].astype(BF16)


def add_z(place, own, *others):
    vmem = pl.BlockSpec(memory_space=pltpu.VMEM)
    rows = Z_PART // XH
    return pl.pallas_call(
        z_kernel,
        out_shape=[jax.ShapeDtypeStruct((rows, D), F32), jax.ShapeDtypeStruct((rows, D), BF16)],
        in_specs=[pl.BlockSpec(memory_space=pltpu.SMEM)] + [vmem] * 4,
        out_specs=[vmem] * 2,
        scratch_shapes=[pltpu.VMEM((Z_PART, D), F32)],
        compiler_params=pltpu.CompilerParams(vmem_limit_bytes=32 * MIB),
        cost_estimate=pl.CostEstimate(flops=10**6, bytes_accessed=4 * 10**6, transcendentals=0),
        name="gram_z",
    )(place, own, *others)


def up_z(x, k):
    return permute(x, lambda xh, z, c, y, xl: (xh, (z + k) % Z, c, y, xl))


def rope_tables(place):
    inside = jnp.arange(TOK, dtype=I32)[None, :]
    blocks = place[:, None]
    frame_pos = jnp.broadcast_to(blocks // 2, (8, TOK)).reshape(-1).astype(F32)
    row_pos = (blocks % 2 * 8 + inside // WIDTH).reshape(-1).astype(F32)
    col_pos = jnp.broadcast_to(inside % WIDTH, (8, TOK)).reshape(-1).astype(F32)
    half_dim = HEAD_DIM // 2
    spatial = HEAD_DIM // 6
    temporal = half_dim - 2 * spatial
    entry = jnp.arange(HEAD_DIM, dtype=I32)
    pair_ids = entry // 2
    exponent = jnp.where(
        pair_ids < temporal,
        2.0 * pair_ids / (2.0 * temporal),
        jnp.where(
            pair_ids < temporal + spatial,
            2.0 * (pair_ids - temporal) / (2.0 * spatial),
            2.0 * (pair_ids - temporal - spatial) / (2.0 * spatial),
        ),
    ).astype(F32)
    frequency = jnp.power(jnp.float32(10000.0), -exponent)
    chosen_pos = jnp.where(
        pair_ids[None, :] < temporal,
        frame_pos[:, None],
        jnp.where(pair_ids[None, :] < temporal + spatial, row_pos[:, None], col_pos[:, None]),
    )
    angles = chosen_pos * frequency[None, :]
    sine = jnp.sin(angles)
    even = (entry % 2 == 0)[None, :]
    return jnp.cos(angles), jnp.where(even, -sine, 0.0), jnp.where(even, 0.0, sine)


def attend_kernel(half, place, q_ref, k_ref, v_ref, *refs):
    squares, (gain_q, gain_k, cosine, sine_l, sine_r), outs = refs[:2], refs[2:7], refs[7:11]
    scale_v, line_v = refs[11:]

    @pl.when(pl.program_id(0) == 0)
    def _():
        scale = lax.rsqrt((squares[0][...] + squares[1][...]) / D + 1e-06)
        for b in range(8):
            line_v[b * 8 : (b + 1) * 8, :] = scale[b]
        for b in range(8):
            source = place[b]
            for part in range(2):
                line = line_v[pl.ds(source * 8 + part, 1), :]
                scale_v[part, b * TOK : (b + 1) * TOK, :] = jnp.broadcast_to(line, (TOK, TOK)).T

    factor = HEAD_DIM ** (-0.5) * 1.4426950408889634

    def rotate(x, part, gain, rows):
        x = x * scale_v[part, rows, :] * gain
        left = pltpu.roll(x, HEAD_DIM - 1, 1)
        right = pltpu.roll(x, 1, 1)
        return (x * cosine[rows, :] + left * sine_l[rows, :] + right * sine_r[rows, :]).astype(BF16)

    every = slice(0, 8 * TOK)
    keys = rotate(k_ref[...], 1, gain_k[...], every)
    values = v_ref[...]
    tile = 256
    for i in range(4 * TOK // tile):
        inside = slice(i * tile, (i + 1) * tile)
        rows = slice(half * 4 * TOK + i * tile, half * 4 * TOK + (i + 1) * tile)
        q = rotate(q_ref[inside, :], 0, gain_q[...] * factor, rows)
        scores = lax.dot_general(q, keys, (((1,), (1,)), ((), ())), preferred_element_type=F32)
        top = jnp.max(scores, axis=-1, keepdims=True)
        weights = jnp.exp2(scores - top)
        total = jnp.sum(weights, axis=-1, keepdims=True)
        out = jnp.dot(weights.astype(BF16), values, preferred_element_type=F32)
        out = (out * (1.0 / total)).astype(BF16)
        for b in range(tile // TOK):
            outs[i * (tile // TOK) + b][...] = out[b * TOK : (b + 1) * TOK, :]


def attend(half, place, qk, v, squares, gain_q, gain_k, tables):
    query = pl.BlockSpec((4 * TOK, HEAD_DIM), lambda h: (half, h))
    key = pl.BlockSpec((8 * TOK, HEAD_DIM), lambda h: (0, HEADS + h))
    head = pl.BlockSpec((8 * TOK, HEAD_DIM), lambda h: (0, h))
    gain = pl.BlockSpec((1, HEAD_DIM), lambda h: (0, h))
    table = pl.BlockSpec((8 * TOK, HEAD_DIM), lambda h: (0, 0))
    square = pl.BlockSpec((8, 8, TOK), lambda h: (0, 0, 0))
    return pl.pallas_call(
        functools.partial(attend_kernel, half),
        out_shape=(jax.ShapeDtypeStruct((TOK, COLS), BF16),) * 4,
        grid=(HEADS,),
        in_specs=[pl.BlockSpec(memory_space=pltpu.SMEM), query, key, head]
        + [square] * 2
        + [gain, gain, table, table, table],
        out_specs=(pl.BlockSpec((TOK, HEAD_DIM), lambda h: (0, h)),) * 4,
        scratch_shapes=[pltpu.VMEM((2, 8 * TOK, TOK), F32), pltpu.VMEM((64, TOK), F32)],
        compiler_params=pltpu.CompilerParams(vmem_limit_bytes=60 * MIB),
        cost_estimate=pl.CostEstimate(flops=2 * 1024 * 1024 * COLS, bytes_accessed=10**7, transcendentals=5 * 2**19),
        name=f"attend_{half}",
    )(place, qk, qk, v, *squares, gain_q[None], gain_k[None], *tables)


def gather_kernel(place, *refs):
    pieces, out = refs[:8], refs[8]
    for j in range(8):
        column = pl.multiple_of(place[j] * COLS, COLS)
        out[0, :, pl.ds(column, COLS)] = pieces[j][...]


def gather_columns(place, pieces):
    vmem = pl.BlockSpec(memory_space=pltpu.VMEM)
    return pl.pallas_call(
        gather_kernel,
        out_shape=jax.ShapeDtypeStruct((1, TOK, D), BF16),
        in_specs=[pl.BlockSpec(memory_space=pltpu.SMEM)] + [vmem] * 8,
        out_specs=vmem,
        compiler_params=pltpu.CompilerParams(vmem_limit_bytes=16 * MIB),
        cost_estimate=pl.CostEstimate(flops=0, bytes_accessed=3 * 10**6, transcendentals=0),
        name="gather_columns",
    )(place, *pieces)


def per_device(h, modulation, wq, wk, wv, mq, mk, mv, gain_q, gain_k):
    xh, z, c, y, xl = (lax.axis_index(a).astype(I32) for a in AXES)
    way = 1 - 2 * c
    blocks = [(s, dx) for dx in range(2) for s in range(4)]
    canonical = jnp.stack([((y - way * s) % Y) * 2 + (xl ^ dx) for s, dx in blocks])
    sources = jnp.stack([((y + way * s) % Y) * 2 + (xl ^ dx) for s, dx in blocks])
    rows = [((z - way * s) % Z) * 2 + c for s in range(4)] + [((z + way * s) % Z) * 2 + 1 - c for s in range(4)]
    place_1 = jnp.concatenate([jnp.stack([xh] + rows), canonical])
    place_2 = jnp.concatenate([jnp.stack([1 - xh] + rows), canonical])
    me = jnp.stack([y * 2 + xl, c])

    x0, x0_lo, x0_hi, w0, w0_lo, w0_mid, w0_hi = begin(h, modulation, wq, wk, wv, mq, mk, mv)

    half = TOK // 2
    x1, w1, b0_lo, p0_lo = stage(ring_y(x0), ring_z(w0), swap_xl(x0_lo), swap_xh(w0_lo))
    x2, w2, b0_hi, p0_mid, e0 = stage(ring_y(x1), ring_z(w1), swap_xl(x0_hi), swap_xh(w0_mid), swap_c(w0))
    x3, w3, p0_hi, e1, e2 = stage(ring_y(x2), ring_z(w2), swap_xh(w0_hi), swap_c(w1), swap_c(w2))
    b0 = jnp.concatenate([b0_lo, b0_hi])
    p0 = jnp.concatenate([p0_lo, p0_mid, p0_hi])
    e3 = swap_c(w3)
    own_half = [w0, w1, w2, w3, e0, e1, e2, e3]
    xs_a = [x0, x1, x2, x3]
    acc_a = project(place_1, xs_a, own_half)
    tables = rope_tables(canonical)
    b1, p1, b3_lo, acc_a, *tables = stage(ring_y(b0), ring_z(p0), swap_xl(x3[:half]), acc_a, *tables)
    f0 = swap_c(p0)
    f1 = swap_c(p1)
    tokens = XH * Z * C * 8 * TOK
    sums = gram_rows(me, xs_a + [b0, b1], tokens)
    b2, p2, b3_hi, f0, f1, *sums = stage(ring_y(b1), ring_z(p1), swap_xl(x3[half:]), f0, f1, *sums)
    xs_b = [b0, b1, b2, b3_lo, b3_hi]

    f2 = swap_c(p2)
    theirs, mine = gram_rows(me, [b2, b3_lo, b3_hi], tokens, sums)
    theirs, f2, *xs_b = stage(theirs, f2, *xs_b)
    moved = swap_c(theirs)
    acc_b = project(place_1, xs_b, own_half)
    moved, mine, p3, acc_b = stage(moved, mine, ring_z(p2), acc_b)
    f3 = swap_c(p3)
    part_0, part_1, part_2, part_3 = add_pair(z[None], mine, moved)
    part_0, part_1, part_2, part_3, f3, acc_a = stage(part_0, part_1, part_2, part_3, f3, acc_a)
    summed = [part_0, up_z(part_1, 1), up_z(part_2, 2), up_z(part_3, 3)]
    other_half = [p0, p1, p2, p3, f0, f1, f2, f3]

    qk, v, squares = finish(place_2, xs_a + xs_b, other_half, [acc_a, acc_b])
    ring = squares + sum(to_owner(squares, s, 0) for s in range(1, Y))
    both = [ring, swap_xl(ring)]
    late = attend(1, canonical, qk, v, both, gain_q, gain_k, tables)
    late = list(late)
    late[0], *summed = stage(late[0], *summed)
    kept, sent = add_z(xh[None], *summed)
    gram = kept + swap_xh(sent).astype(F32)
    pieces_late = [to_owner(o, s, 1) for o, s in zip(late, range(Y))]
    early = attend(0, canonical, stage(qk, late[0])[0], v, both, gain_q, gain_k, tables)
    rest = list(stage(*early, *pieces_late))
    early, pieces_late = rest[:4], rest[4:]
    pieces = [early[0]] + [to_owner(o, s, 0) for o, s in zip(early[1:], range(1, Y))]
    return gather_columns(sources, pieces + pieces_late), gram[None]


def solution(mesh):
    fine = Mesh(mesh.devices.reshape(XH, Z, C, Y, XL), AXES)
    grp, sp = ("xh", "z", "c"), ("y", "xl")
    return jax.shard_map(
        per_device,
        mesh=fine,
        in_specs=(
            P(grp, sp, None),
            P(grp, None, None),
            P(grp, sp),
            P(grp, sp),
            P(grp, sp),
            P(grp, sp),
            P(grp, sp),
            P(grp, sp),
            P(sp),
            P(sp),
        ),
        out_specs=(P(grp, sp, None), P(sp, grp, None)),
        check_vma=False,
    )
```

```python
import functools

import jax
import jax.numpy as jnp
from jax import lax
from jax.experimental import pallas as pl
from jax.experimental.pallas import tpu as pltpu
from jax.sharding import Mesh
from jax.sharding import PartitionSpec as P

HEAD_DIM = 128
HEIGHT = 16
WIDTH = 16
XH, Z, C, Y, XL = 2, 4, 2, 4, 2
AXES = ("xh", "z", "c", "y", "xl")
TOK = 128
D = 5120
COLS = 640
ROWS = 320
HALF = D // 2
HEADS = 5
BF16, F32, I32 = jnp.bfloat16, jnp.float32, jnp.int32
MIB = 1 << 20


def linear(xh, z, c, y, xl):
    return (((xh * Z + z) * C + c) * Y + y) * XL + xl


def permute(x, move):
    pairs = []
    for xh in range(XH):
        for z in range(Z):
            for c in range(C):
                for y in range(Y):
                    for xl in range(XL):
                        pairs.append((linear(xh, z, c, y, xl), linear(*move(xh, z, c, y, xl))))
    return lax.ppermute(x, AXES, pairs)


def turn(c):
    return 1 if c == 0 else -1


def ring_y(x):
    return permute(x, lambda xh, z, c, y, xl: (xh, z, c, (y + turn(c)) % Y, xl))


def ring_z(x):
    return permute(x, lambda xh, z, c, y, xl: (xh, (z + turn(c)) % Z, c, y, xl))


def swap_xl(x):
    return permute(x, lambda xh, z, c, y, xl: (xh, z, c, y, 1 - xl))


def swap_xh(x):
    return permute(x, lambda xh, z, c, y, xl: (1 - xh, z, c, y, xl))


def swap_c(x):
    return permute(x, lambda xh, z, c, y, xl: (xh, z, 1 - c, y, xl))


def to_owner(x, s, dx):
    return permute(x, lambda xh, z, c, y, xl: (xh, z, c, (y - turn(c) * s) % Y, xl ^ dx))


def stage(*arrays):
    return lax.optimization_barrier(arrays)


HALVES = ((0, TOK // 2), (TOK // 2, TOK))
CHUNKS = ((0, 64), (64, 128), (128, ROWS))


def begin_kernel(h, modulation, wq, wk, wv, mq, mk, mv, *refs):
    x_out, x_lo, x_hi, w_out, w_lo, w_mid, w_hi = refs[:7]
    h_v, mod_v, w_v, m_v, sem = refs[7:]
    pairs = [(h.at[0], h_v), (modulation.at[0], mod_v)]
    pairs += [(w, w_v.at[i]) for i, w in enumerate((wq, wk, wv))]
    pairs += [(m, m_v.at[i]) for i, m in enumerate((mq, mk, mv))]
    copies = [pltpu.make_async_copy(source, target, sem.at[i]) for i, (source, target) in enumerate(pairs)]
    for copy in copies:
        copy.start()
    for copy in copies[:2]:
        copy.wait()
    scale = 1.0 + mod_v[1:2, :]
    shift = mod_v[0:1, :]
    step = 32
    for i in range(TOK // step):
        x = h_v[i * step : (i + 1) * step, :].astype(F32)
        average = jnp.mean(x, axis=-1, keepdims=True)
        centred = x - average
        variance = jnp.mean(centred * centred, axis=-1, keepdims=True)
        y = (centred * lax.rsqrt(variance + 1e-06) * scale + shift).astype(BF16)
        x_out[i * step : (i + 1) * step, :] = y
        piece, at = (x_lo, i * step) if i * step < TOK // 2 else (x_hi, i * step - TOK // 2)
        piece[at : at + step, :] = y
    group = lax.broadcasted_iota(I32, (ROWS, ROWS // 4), 0) // 4
    spread = (group == lax.broadcasted_iota(I32, (ROWS, ROWS // 4), 1)).astype(F32).astype(BF16)
    slot = lax.broadcasted_iota(I32, (ROWS, COLS), 0) % 4
    for i in range(3):
        copies[2 + i].wait()
        copies[5 + i].wait()
        p = m_v[i]
        bits = jnp.where(p == 0, 3, jnp.where(p == 1, 5, jnp.where(p == 2, 9, jnp.where(p == 3, 6, jnp.where(p == 4, 10, 12)))))
        rows = jnp.dot(spread, bits.astype(F32).astype(BF16), preferred_element_type=F32).astype(I32)
        kept = (lax.shift_right_logical(rows, slot) & 1) == 1
        masked = jnp.where(kept, w_v[i].astype(F32), 0.0).astype(BF16)
        cols = slice(i * COLS, (i + 1) * COLS)
        w_out[:, cols] = masked
        for piece, (low, high) in zip((w_lo, w_mid, w_hi), CHUNKS):
            piece[:, cols] = masked[low:high, :]


def begin(h, modulation, wq, wk, wv, mq, mk, mv):
    hbm = pl.BlockSpec(memory_space=pltpu.HBM)
    vmem = pl.BlockSpec(memory_space=pltpu.VMEM)
    rows = [TOK, TOK // 2, TOK // 2]
    tall = [ROWS] + [high - low for low, high in CHUNKS]
    out = [jax.ShapeDtypeStruct((r, D), BF16) for r in rows] + [jax.ShapeDtypeStruct((r, 3 * COLS), BF16) for r in tall]
    return pl.pallas_call(
        begin_kernel,
        out_shape=out,
        in_specs=[hbm] * 8,
        out_specs=[vmem] * 7,
        scratch_shapes=[
            pltpu.VMEM((TOK, D), BF16),
            pltpu.VMEM((2, D), F32),
            pltpu.VMEM((3, ROWS, COLS), BF16),
            pltpu.VMEM((3, ROWS // 4, COLS), I32),
            pltpu.SemaphoreType.DMA((8,)),
        ],
        compiler_params=pltpu.CompilerParams(vmem_limit_bytes=60 * MIB),
        cost_estimate=pl.CostEstimate(flops=10**8, bytes_accessed=6 * 10**6, transcendentals=0),
        name="norm_and_mask",
    )(h, modulation, wq, wk, wv, mq, mk, mv)


def offsets(xs):
    starts = [0]
    for x in xs:
        starts.append(starts[-1] + x.shape[0])
    return starts


def edges_of(parts):
    return [sum(parts[:p]) for p in range(len(parts) + 1)]


def start_all(copies):
    for copy in copies:
        copy.start()


def wait_all(copies):
    for copy in copies:
        copy.wait()


def in_order(groups):
    start_all(groups[0])
    begun = [1]

    def need(g):
        wait_all(groups[g])
        while begun[0] < min(g + 3, len(groups)):
            start_all(groups[begun[0]])
            begun[0] += 1

    return need


def copies_of_x(xs, x_v, sem, column):
    at = offsets(xs)
    return [
        pltpu.make_async_copy(x.at[:, pl.ds(column, HALF)], x_v.at[at[j] : at[j + 1], :], sem.at[j])
        for j, x in enumerate(xs)
    ]


def copies_of_w(place, ws, w_v, sem, there, here, base):
    out = []
    for j in range(8):
        row = pl.multiple_of(place[1 + j] * ROWS, ROWS)
        out.append(pltpu.make_async_copy(ws[j].at[:, there], w_v.at[pl.ds(row, ROWS), here], sem.at[base + j]))
    return out


def project_kernel(n_x, parts, place, *refs):
    xs, ws, (out, x_v, w_v, y_v, sem_x, sem_w, sem_y) = refs[:n_x], refs[n_x : n_x + 8], refs[n_x + 8 :]
    copies_x = copies_of_x(xs, x_v, sem_x, pl.multiple_of(place[0] * HALF, HALF))
    edges = edges_of(parts)
    here = [slice(edges[p], edges[p + 1]) for p in range(len(parts))]
    copies_w = [copies_of_w(place, ws, w_v, sem_w, cols, cols, p * 8) for p, cols in enumerate(here)]
    need = in_order([copies_w[0] + copies_x] + copies_w[1:])
    sent = []
    for p, cols in enumerate(here):
        need(p)
        y_v[:, cols] = jnp.dot(x_v[...], w_v[:, cols], preferred_element_type=F32)
        sent.append(pltpu.make_async_copy(y_v.at[:, cols], out.at[:, cols], sem_y.at[p]))
        sent[-1].start()
    wait_all(sent)


def project(place, xs, ws):
    n_x = len(xs)
    rows = offsets(xs)[-1]
    parts = (256, 512, 512, 640)
    width = 3 * COLS
    hbm = pl.BlockSpec(memory_space=pltpu.HBM)
    return pl.pallas_call(
        functools.partial(project_kernel, n_x, parts),
        out_shape=jax.ShapeDtypeStruct((rows, width), F32),
        in_specs=[pl.BlockSpec(memory_space=pltpu.SMEM)] + [hbm] * (n_x + 8),
        out_specs=hbm,
        scratch_shapes=[
            pltpu.VMEM((rows, HALF), BF16),
            pltpu.VMEM((HALF, width), BF16),
            pltpu.VMEM((rows, width), F32),
            pltpu.SemaphoreType.DMA((n_x,)),
            pltpu.SemaphoreType.DMA((8 * len(parts),)),
            pltpu.SemaphoreType.DMA((len(parts),)),
        ],
        compiler_params=pltpu.CompilerParams(vmem_limit_bytes=60 * MIB),
        cost_estimate=pl.CostEstimate(flops=10**6, bytes_accessed=10**5, transcendentals=0),
        name="project_first",
    )(place, *xs, *ws)


def finish_kernel(n_x, parts, place, *refs):
    xs, ws, accs, refs = refs[:n_x], refs[n_x : n_x + 8], refs[n_x + 8 : n_x + 10], refs[n_x + 10 :]
    qk_out, v_out, sq_out, x_v, w_v, a_v, y_v, v_v, sem_x, sem_w, sem_a, sem_y = refs
    copies_x = copies_of_x(xs, x_v, sem_x, pl.multiple_of(place[0] * HALF, HALF))
    n = len(parts)
    edges = edges_of(parts)
    middle = 4 * TOK
    groups = []
    for p in range(n):
        cols = slice(edges[p], edges[p + 1])
        copies_w = copies_of_w(place, ws, w_v, sem_w, cols, cols, p * 8)
        copies_a = [
            pltpu.make_async_copy(acc.at[:, cols], a_v.at[i * middle : (i + 1) * middle, cols], sem_a.at[p * 2 + i])
            for i, acc in enumerate(accs)
        ]
        groups += [copies_w + copies_x[:4], copies_x[4:] + copies_a] if p == 0 else [copies_w + copies_a]
    need = in_order(groups)
    need(0)
    sent = []
    for p in range(n):
        cols = slice(edges[p], edges[p + 1])
        if p:
            need(p + 1)
        for i in range(2):
            rows = slice(i * middle, (i + 1) * middle)
            y = jnp.dot(x_v[rows, :], w_v[:, cols], preferred_element_type=F32)
            if p == 0 and i == 0:
                need(1)
            y = y + a_v[rows, cols]
            if edges[p] >= 2 * COLS:
                v_v[rows, :] = y.astype(BF16)
                target, source = v_out, v_v
            else:
                y_v[rows, cols] = y
                target, source = qk_out.at[:, cols], y_v.at[:, cols]
            for part in range(2):
                low, high = max(edges[p], part * COLS), min(edges[p + 1], (part + 1) * COLS)
                if low >= high:
                    continue
                squares = y[:, low - edges[p] : high - edges[p]]
                squares = squares * squares
                lanes = sum(squares[:, h : h + 128] for h in range(0, high - low, 128))
                for b in range(4):
                    line = jnp.sum(lanes[b * TOK : (b + 1) * TOK, :].T, axis=0, keepdims=True)
                    at = place[9 + i * 4 + b]
                    if low > part * COLS:
                        line = line + sq_out[at, part : part + 1, :]
                    sq_out[at, part : part + 1, :] = line
        sent.append(pltpu.make_async_copy(source, target, sem_y.at[p]))
        sent[-1].start()
    wait_all(sent)


def finish(place, xs, ws, accs):
    parts = (256, 512, 512, 640)
    n = len(parts)
    rows = 8 * TOK
    width = 3 * COLS
    hbm = pl.BlockSpec(memory_space=pltpu.HBM)
    n_x = len(xs)
    return pl.pallas_call(
        functools.partial(finish_kernel, n_x, parts),
        out_shape=[
            jax.ShapeDtypeStruct((rows, 2 * COLS), F32),
            jax.ShapeDtypeStruct((rows, COLS), BF16),
            jax.ShapeDtypeStruct((8, 8, TOK), F32),
        ],
        in_specs=[pl.BlockSpec(memory_space=pltpu.SMEM)] + [hbm] * (n_x + 10),
        out_specs=[hbm, hbm, pl.BlockSpec(memory_space=pltpu.VMEM)],
        scratch_shapes=[
            pltpu.VMEM((rows, HALF), BF16),
            pltpu.VMEM((HALF, width), BF16),
            pltpu.VMEM((rows, width), F32),
            pltpu.VMEM((rows, 2 * COLS), F32),
            pltpu.VMEM((rows, COLS), BF16),
            pltpu.SemaphoreType.DMA((n_x,)),
            pltpu.SemaphoreType.DMA((8 * n,)),
            pltpu.SemaphoreType.DMA((2 * n,)),
            pltpu.SemaphoreType.DMA((n,)),
        ],
        compiler_params=pltpu.CompilerParams(vmem_limit_bytes=60 * MIB),
        cost_estimate=pl.CostEstimate(flops=2 * rows * HALF * width, bytes_accessed=30 * 10**6, transcendentals=0),
        name="project_last",
    )(place, *xs, *ws, *accs)


def gram_kernel(tokens, n_x, added, place, *refs):
    xs, refs = refs[:n_x], refs[n_x:]
    sums, refs = refs[: 2 * added], refs[2 * added :]
    outs, (own_x, x_v, own, o_v, sem_own, sem_x, sem_o), (*more,) = refs[:2], refs[2:9], refs[9:]
    at = offsets(xs)
    n = 4
    step = D // n
    column = pl.multiple_of(place[0] * COLS, COLS)
    first = [
        pltpu.make_async_copy(x.at[:, pl.ds(column, COLS)], own_x.at[at[j] : at[j + 1], :], sem_own.at[j])
        for j, x in enumerate(xs)
    ]
    rest = []
    for i in range(n):
        cols = slice(i * step, (i + 1) * step)
        some = [
            pltpu.make_async_copy(x.at[:, cols], x_v.at[at[j] : at[j + 1], cols], sem_x.at[i, j])
            for j, x in enumerate(xs)
        ]
        for j, old in enumerate(sums):
            s_v, sem_s = more
            some.append(
                pltpu.make_async_copy(old.at[:, cols], s_v.at[j * ROWS : (j + 1) * ROWS, cols], sem_s.at[i, j])
            )
        rest.append(some)
    need = in_order([first] + rest)
    line = lax.broadcasted_iota(I32, (COLS, COLS), 0)
    core = jnp.where(line < ROWS, 1 - place[1], place[1])
    source = ((line // 40 % XH * Z + line // 80 % Z) * C + core) * 40 + line % 40
    order = (source == lax.broadcasted_iota(I32, (COLS, COLS), 1)).astype(F32).astype(BF16)
    need(0)
    own[...] = lax.dot_general(
        order, own_x[...], (((1,), (1,)), ((), ())), preferred_element_type=F32
    ).astype(BF16)
    sends = []
    for i in range(n):
        cols = slice(i * step, (i + 1) * step)
        need(i + 1)
        for j, out in enumerate(outs):
            rows = slice(j * ROWS, (j + 1) * ROWS)
            y = jnp.dot(own[rows, :], x_v[:, cols], preferred_element_type=F32) * (1.0 / tokens)
            if added:
                y = y + more[0][rows, cols].astype(F32)
            o_v[rows, cols] = y.astype(BF16)
            sends.append(pltpu.make_async_copy(o_v.at[rows, cols], out.at[:, cols], sem_o.at[i, j]))
            sends[-1].start()
    wait_all(sends)


def gram_rows(place, xs, tokens, sums=()):
    hbm = pl.BlockSpec(memory_space=pltpu.HBM)
    n_x = len(xs)
    count = offsets(xs)[-1]
    scratch = [
        pltpu.VMEM((count, COLS), BF16),
        pltpu.VMEM((count, D), BF16),
        pltpu.VMEM((COLS, count), BF16),
        pltpu.VMEM((COLS, D), BF16),
        pltpu.SemaphoreType.DMA((n_x,)),
        pltpu.SemaphoreType.DMA((4, n_x)),
        pltpu.SemaphoreType.DMA((4, 2)),
    ]
    if sums:
        scratch += [pltpu.VMEM((COLS, D), BF16), pltpu.SemaphoreType.DMA((4, 2))]
    return pl.pallas_call(
        functools.partial(gram_kernel, tokens, n_x, bool(sums)),
        out_shape=[jax.ShapeDtypeStruct((ROWS, D), BF16)] * 2,
        in_specs=[pl.BlockSpec(memory_space=pltpu.SMEM)] + [hbm] * (n_x + len(sums)),
        out_specs=[hbm] * 2,
        scratch_shapes=scratch,
        compiler_params=pltpu.CompilerParams(vmem_limit_bytes=60 * MIB),
        cost_estimate=pl.CostEstimate(flops=10**6, bytes_accessed=10**5, transcendentals=0),
        name=f"gram_rows_{count}",
    )(place, *xs, *sums)


Z_PART = ROWS // Z


def pair_kernel(place, mine, moved, own, *refs):
    outs, (m_v, sem) = refs[:3], refs[3:]
    order = (1, 3, 2, 0)
    groups = []
    for k in order:
        rows = pl.ds(pl.multiple_of(lax.rem(place[0] + k, Z) * Z_PART, 16), Z_PART)
        groups.append(
            [pltpu.make_async_copy(source.at[rows, :], m_v.at[j, k], sem.at[j, k]) for j, source in enumerate((mine, moved))]
        )
    for some in groups:
        start_all(some)
    for g, k in enumerate(order):
        wait_all(groups[g])
        y = m_v[0, k].astype(F32) + m_v[1, k].astype(F32)
        if k == 0:
            own[...] = y
        else:
            outs[k - 1][...] = y.astype(BF16)


def add_pair(place, mine, moved):
    hbm = pl.BlockSpec(memory_space=pltpu.HBM)
    vmem = pl.BlockSpec(memory_space=pltpu.VMEM)
    return pl.pallas_call(
        pair_kernel,
        out_shape=[jax.ShapeDtypeStruct((Z_PART, D), F32)] + [jax.ShapeDtypeStruct((Z_PART, D), BF16)] * 3,
        in_specs=[pl.BlockSpec(memory_space=pltpu.SMEM), hbm, hbm],
        out_specs=[vmem] * 4,
        scratch_shapes=[pltpu.VMEM((2, Z, Z_PART, D), BF16), pltpu.SemaphoreType.DMA((2, Z))],
        compiler_params=pltpu.CompilerParams(vmem_limit_bytes=60 * MIB),
        cost_estimate=pl.CostEstimate(flops=10**6, bytes_accessed=10**7, transcendentals=0),
        name="gram_pair",
    )(place, mine, moved)


def z_kernel(place, own, one, two, three, kept, sent, total_v):
    total_v[...] = own[...] + one[...].astype(F32) + two[...].astype(F32) + three[...].astype(F32)
    rows = Z_PART // XH
    kept[...] = total_v[pl.ds(pl.multiple_of(place[0] * rows, 8), rows), :]
    sent[...] = total_v[pl.ds(pl.multiple_of((1 - place[0]) * rows, 8), rows), :].astype(BF16)


def add_z(place, own, *others):
    vmem = pl.BlockSpec(memory_space=pltpu.VMEM)
    rows = Z_PART // XH
    return pl.pallas_call(
        z_kernel,
        out_shape=[jax.ShapeDtypeStruct((rows, D), F32), jax.ShapeDtypeStruct((rows, D), BF16)],
        in_specs=[pl.BlockSpec(memory_space=pltpu.SMEM)] + [vmem] * 4,
        out_specs=[vmem] * 2,
        scratch_shapes=[pltpu.VMEM((Z_PART, D), F32)],
        compiler_params=pltpu.CompilerParams(vmem_limit_bytes=32 * MIB),
        cost_estimate=pl.CostEstimate(flops=10**6, bytes_accessed=4 * 10**6, transcendentals=0),
        name="gram_z",
    )(place, own, *others)


def up_z(x, k):
    return permute(x, lambda xh, z, c, y, xl: (xh, (z + k) % Z, c, y, xl))


def rope_tables(place):
    inside = jnp.arange(TOK, dtype=I32)[None, :]
    blocks = place[:, None]
    frame_pos = jnp.broadcast_to(blocks // 2, (8, TOK)).reshape(-1).astype(F32)
    row_pos = (blocks % 2 * 8 + inside // WIDTH).reshape(-1).astype(F32)
    col_pos = jnp.broadcast_to(inside % WIDTH, (8, TOK)).reshape(-1).astype(F32)
    half_dim = HEAD_DIM // 2
    spatial = HEAD_DIM // 6
    temporal = half_dim - 2 * spatial
    entry = jnp.arange(HEAD_DIM, dtype=I32)
    pair_ids = entry // 2
    exponent = jnp.where(
        pair_ids < temporal,
        2.0 * pair_ids / (2.0 * temporal),
        jnp.where(
            pair_ids < temporal + spatial,
            2.0 * (pair_ids - temporal) / (2.0 * spatial),
            2.0 * (pair_ids - temporal - spatial) / (2.0 * spatial),
        ),
    ).astype(F32)
    frequency = jnp.power(jnp.float32(10000.0), -exponent)
    chosen_pos = jnp.where(
        pair_ids[None, :] < temporal,
        frame_pos[:, None],
        jnp.where(pair_ids[None, :] < temporal + spatial, row_pos[:, None], col_pos[:, None]),
    )
    angles = chosen_pos * frequency[None, :]
    sine = jnp.sin(angles)
    even = (entry % 2 == 0)[None, :]
    return jnp.cos(angles), jnp.where(even, -sine, 0.0), jnp.where(even, 0.0, sine)


def attend_kernel(half, place, q_ref, k_ref, v_ref, *refs):
    squares, (gain_q, gain_k, cosine, sine_l, sine_r), outs = refs[:2], refs[2:7], refs[7:11]
    scale_v, line_v = refs[11:]

    @pl.when(pl.program_id(0) == 0)
    def _():
        scale = lax.rsqrt((squares[0][...] + squares[1][...]) / D + 1e-06)
        for b in range(8):
            line_v[b * 8 : (b + 1) * 8, :] = scale[b]
        for b in range(8):
            source = place[b]
            for part in range(2):
                line = line_v[pl.ds(source * 8 + part, 1), :]
                scale_v[part, b * TOK : (b + 1) * TOK, :] = jnp.broadcast_to(line, (TOK, TOK)).T

    factor = HEAD_DIM ** (-0.5) * 1.4426950408889634

    def rotate(x, part, gain, rows):
        x = x * scale_v[part, rows, :] * gain
        left = pltpu.roll(x, HEAD_DIM - 1, 1)
        right = pltpu.roll(x, 1, 1)
        return (x * cosine[rows, :] + left * sine_l[rows, :] + right * sine_r[rows, :]).astype(BF16)

    every = slice(0, 8 * TOK)
    keys = rotate(k_ref[...], 1, gain_k[...], every)
    values = v_ref[...]
    tile = 256
    for i in range(4 * TOK // tile):
        inside = slice(i * tile, (i + 1) * tile)
        rows = slice(half * 4 * TOK + i * tile, half * 4 * TOK + (i + 1) * tile)
        q = rotate(q_ref[inside, :], 0, gain_q[...] * factor, rows)
        scores = lax.dot_general(q, keys, (((1,), (1,)), ((), ())), preferred_element_type=F32)
        top = jnp.max(scores, axis=-1, keepdims=True)
        weights = jnp.exp2(scores - top)
        total = jnp.sum(weights, axis=-1, keepdims=True)
        out = jnp.dot(weights.astype(BF16), values, preferred_element_type=F32)
        out = (out * (1.0 / total)).astype(BF16)
        for b in range(tile // TOK):
            outs[i * (tile // TOK) + b][...] = out[b * TOK : (b + 1) * TOK, :]


def attend(half, place, qk, v, squares, gain_q, gain_k, tables):
    query = pl.BlockSpec((4 * TOK, HEAD_DIM), lambda h: (half, h))
    key = pl.BlockSpec((8 * TOK, HEAD_DIM), lambda h: (0, HEADS + h))
    head = pl.BlockSpec((8 * TOK, HEAD_DIM), lambda h: (0, h))
    gain = pl.BlockSpec((1, HEAD_DIM), lambda h: (0, h))
    table = pl.BlockSpec((8 * TOK, HEAD_DIM), lambda h: (0, 0))
    square = pl.BlockSpec((8, 8, TOK), lambda h: (0, 0, 0))
    return pl.pallas_call(
        functools.partial(attend_kernel, half),
        out_shape=(jax.ShapeDtypeStruct((TOK, COLS), BF16),) * 4,
        grid=(HEADS,),
        in_specs=[pl.BlockSpec(memory_space=pltpu.SMEM), query, key, head]
        + [square] * 2
        + [gain, gain, table, table, table],
        out_specs=(pl.BlockSpec((TOK, HEAD_DIM), lambda h: (0, h)),) * 4,
        scratch_shapes=[pltpu.VMEM((2, 8 * TOK, TOK), F32), pltpu.VMEM((64, TOK), F32)],
        compiler_params=pltpu.CompilerParams(vmem_limit_bytes=60 * MIB),
        cost_estimate=pl.CostEstimate(flops=2 * 1024 * 1024 * COLS, bytes_accessed=10**7, transcendentals=5 * 2**19),
        name=f"attend_{half}",
    )(place, qk, qk, v, *squares, gain_q[None], gain_k[None], *tables)


def gather_kernel(place, *refs):
    pieces, out = refs[:8], refs[8]
    for j in range(8):
        column = pl.multiple_of(place[j] * COLS, COLS)
        out[0, :, pl.ds(column, COLS)] = pieces[j][...]


def gather_columns(place, pieces):
    vmem = pl.BlockSpec(memory_space=pltpu.VMEM)
    return pl.pallas_call(
        gather_kernel,
        out_shape=jax.ShapeDtypeStruct((1, TOK, D), BF16),
        in_specs=[pl.BlockSpec(memory_space=pltpu.SMEM)] + [vmem] * 8,
        out_specs=vmem,
        compiler_params=pltpu.CompilerParams(vmem_limit_bytes=16 * MIB),
        cost_estimate=pl.CostEstimate(flops=0, bytes_accessed=3 * 10**6, transcendentals=0),
        name="gather_columns",
    )(place, *pieces)


def per_device(h, modulation, wq, wk, wv, mq, mk, mv, gain_q, gain_k):
    xh, z, c, y, xl = (lax.axis_index(a).astype(I32) for a in AXES)
    way = 1 - 2 * c
    blocks = [(s, dx) for dx in range(2) for s in range(4)]
    canonical = jnp.stack([((y - way * s) % Y) * 2 + (xl ^ dx) for s, dx in blocks])
    sources = jnp.stack([((y + way * s) % Y) * 2 + (xl ^ dx) for s, dx in blocks])
    rows = [((z - way * s) % Z) * 2 + c for s in range(4)] + [((z + way * s) % Z) * 2 + 1 - c for s in range(4)]
    place_1 = jnp.concatenate([jnp.stack([xh] + rows), canonical])
    place_2 = jnp.concatenate([jnp.stack([1 - xh] + rows), canonical])
    me = jnp.stack([y * 2 + xl, c])

    x0, x0_lo, x0_hi, w0, w0_lo, w0_mid, w0_hi = begin(h, modulation, wq, wk, wv, mq, mk, mv)

    half = TOK // 2
    x1, w1, b0_lo, p0_lo = stage(ring_y(x0), ring_z(w0), swap_xl(x0_lo), swap_xh(w0_lo))
    x2, w2, b0_hi, p0_mid, e0, *tables = stage(
        ring_y(x1), ring_z(w1), swap_xl(x0_hi), swap_xh(w0_mid), swap_c(w0), *rope_tables(canonical)
    )
    x3, w3, p0_hi, e1, e2 = stage(ring_y(x2), ring_z(w2), swap_xh(w0_hi), swap_c(w1), swap_c(w2))
    b0 = jnp.concatenate([b0_lo, b0_hi])
    p0 = jnp.concatenate([p0_lo, p0_mid, p0_hi])
    e3 = swap_c(w3)
    own_half = [w0, w1, w2, w3, e0, e1, e2, e3]
    xs_a = [x0, x1, x2, x3]
    acc_a = project(place_1, xs_a, own_half)
    b1, p1, b3_lo, acc_a = stage(ring_y(b0), ring_z(p0), swap_xl(x3[:half]), acc_a)
    f0 = swap_c(p0)
    f1 = swap_c(p1)
    tokens = XH * Z * C * 8 * TOK
    sums = gram_rows(me, xs_a + [b0, b1], tokens)
    b2, p2, b3_hi, f0, f1, *sums = stage(ring_y(b1), ring_z(p1), swap_xl(x3[half:]), f0, f1, *sums)
    xs_b = [b0, b1, b2, b3_lo, b3_hi]

    f2 = swap_c(p2)
    theirs, mine = gram_rows(me, [b2, b3_lo, b3_hi], tokens, sums)
    theirs, f2, *xs_b = stage(theirs, f2, *xs_b)
    moved = swap_c(theirs)
    acc_b = project(place_1, xs_b, own_half)
    moved, mine, acc_b = stage(moved, mine, acc_b)
    part_0, part_1, part_2, part_3 = add_pair(z[None], mine, moved)
    part_0, part_1, part_2, part_3, p3, acc_a = stage(part_0, part_1, part_2, part_3, ring_z(p2), acc_a)
    f3 = swap_c(p3)
    summed = [part_0, up_z(part_1, 1), up_z(part_2, 2), up_z(part_3, 3)]
    other_half = [p0, p1, p2, p3, f0, f1, f2, f3]

    qk, v, squares = finish(place_2, xs_a + xs_b, other_half, [acc_a, acc_b])
    ring = squares + sum(to_owner(squares, s, 0) for s in range(1, Y))
    both = [ring, swap_xl(ring)]
    late = attend(1, canonical, qk, v, both, gain_q, gain_k, tables)
    late = list(late)
    late[0], *summed = stage(late[0], *summed)
    kept, sent = add_z(xh[None], *summed)
    gram = kept + swap_xh(sent).astype(F32)
    pieces_late = [to_owner(o, s, 1) for o, s in zip(late, range(Y))]
    early = attend(0, canonical, stage(qk, late[0])[0], v, both, gain_q, gain_k, tables)
    rest = list(stage(*early, *pieces_late))
    early, pieces_late = rest[:4], rest[4:]
    pieces = [early[0]] + [to_owner(o, s, 0) for o, s in zip(early[1:], range(1, Y))]
    return gather_columns(sources, pieces + pieces_late), gram[None]


def solution(mesh):
    fine = Mesh(mesh.devices.reshape(XH, Z, C, Y, XL), AXES)
    grp, sp = ("xh", "z", "c"), ("y", "xl")
    return jax.shard_map(
        per_device,
        mesh=fine,
        in_specs=(
            P(grp, sp, None),
            P(grp, None, None),
            P(grp, sp),
            P(grp, sp),
            P(grp, sp),
            P(grp, sp),
            P(grp, sp),
            P(grp, sp),
            P(sp),
            P(sp),
        ),
        out_specs=(P(grp, sp, None), P(sp, grp, None)),
        check_vma=False,
    )
```

```python
import functools

import jax
import jax.numpy as jnp
from jax import lax
from jax.experimental import pallas as pl
from jax.experimental.pallas import tpu as pltpu
from jax.sharding import Mesh
from jax.sharding import PartitionSpec as P

HEAD_DIM = 128
HEIGHT = 16
WIDTH = 16
XH, Z, C, Y, XL = 2, 4, 2, 4, 2
AXES = ("xh", "z", "c", "y", "xl")
TOK = 128
D = 5120
COLS = 640
ROWS = 320
HALF = D // 2
HEADS = 5
BF16, F32, I32 = jnp.bfloat16, jnp.float32, jnp.int32
MIB = 1 << 20


def linear(xh, z, c, y, xl):
    return (((xh * Z + z) * C + c) * Y + y) * XL + xl


def permute(x, move):
    pairs = []
    for xh in range(XH):
        for z in range(Z):
            for c in range(C):
                for y in range(Y):
                    for xl in range(XL):
                        pairs.append((linear(xh, z, c, y, xl), linear(*move(xh, z, c, y, xl))))
    return lax.ppermute(x, AXES, pairs)


def turn(c):
    return 1 if c == 0 else -1


def ring_y(x):
    return permute(x, lambda xh, z, c, y, xl: (xh, z, c, (y + turn(c)) % Y, xl))


def ring_z(x):
    return permute(x, lambda xh, z, c, y, xl: (xh, (z + turn(c)) % Z, c, y, xl))


def swap_xl(x):
    return permute(x, lambda xh, z, c, y, xl: (xh, z, c, y, 1 - xl))


def swap_xh(x):
    return permute(x, lambda xh, z, c, y, xl: (1 - xh, z, c, y, xl))


def swap_c(x):
    return permute(x, lambda xh, z, c, y, xl: (xh, z, 1 - c, y, xl))


def to_owner(x, s, dx):
    return permute(x, lambda xh, z, c, y, xl: (xh, z, c, (y - turn(c) * s) % Y, xl ^ dx))


def stage(*arrays):
    return lax.optimization_barrier(arrays)


HALVES = ((0, TOK // 2), (TOK // 2, TOK))
CHUNKS = ((0, 64), (64, 128), (128, ROWS))


def begin_kernel(h, modulation, wq, wk, wv, mq, mk, mv, *refs):
    x_out, x_lo, x_hi, w_out, w_lo, w_mid, w_hi = refs[:7]
    h_v, mod_v, w_v, m_v, sem = refs[7:]
    pairs = [(h.at[0], h_v), (modulation.at[0], mod_v)]
    pairs += [(w, w_v.at[i]) for i, w in enumerate((wq, wk, wv))]
    pairs += [(m, m_v.at[i]) for i, m in enumerate((mq, mk, mv))]
    copies = [pltpu.make_async_copy(source, target, sem.at[i]) for i, (source, target) in enumerate(pairs)]
    for copy in copies:
        copy.start()
    for copy in copies[:2]:
        copy.wait()
    scale = 1.0 + mod_v[1:2, :]
    shift = mod_v[0:1, :]
    step = 32
    for i in range(TOK // step):
        x = h_v[i * step : (i + 1) * step, :].astype(F32)
        average = jnp.mean(x, axis=-1, keepdims=True)
        centred = x - average
        variance = jnp.mean(centred * centred, axis=-1, keepdims=True)
        y = (centred * lax.rsqrt(variance + 1e-06) * scale + shift).astype(BF16)
        x_out[i * step : (i + 1) * step, :] = y
        piece, at = (x_lo, i * step) if i * step < TOK // 2 else (x_hi, i * step - TOK // 2)
        piece[at : at + step, :] = y
    group = lax.broadcasted_iota(I32, (ROWS, ROWS // 4), 0) // 4
    spread = (group == lax.broadcasted_iota(I32, (ROWS, ROWS // 4), 1)).astype(F32).astype(BF16)
    slot = lax.broadcasted_iota(I32, (ROWS, COLS), 0) % 4
    for i in range(3):
        copies[2 + i].wait()
        copies[5 + i].wait()
        p = m_v[i]
        bits = jnp.where(p == 0, 3, jnp.where(p == 1, 5, jnp.where(p == 2, 9, jnp.where(p == 3, 6, jnp.where(p == 4, 10, 12)))))
        rows = jnp.dot(spread, bits.astype(F32).astype(BF16), preferred_element_type=F32).astype(I32)
        kept = (lax.shift_right_logical(rows, slot) & 1) == 1
        masked = jnp.where(kept, w_v[i].astype(F32), 0.0).astype(BF16)
        cols = slice(i * COLS, (i + 1) * COLS)
        w_out[:, cols] = masked
        for piece, (low, high) in zip((w_lo, w_mid, w_hi), CHUNKS):
            piece[:, cols] = masked[low:high, :]


def begin(h, modulation, wq, wk, wv, mq, mk, mv):
    hbm = pl.BlockSpec(memory_space=pltpu.HBM)
    vmem = pl.BlockSpec(memory_space=pltpu.VMEM)
    rows = [TOK, TOK // 2, TOK // 2]
    tall = [ROWS] + [high - low for low, high in CHUNKS]
    out = [jax.ShapeDtypeStruct((r, D), BF16) for r in rows] + [jax.ShapeDtypeStruct((r, 3 * COLS), BF16) for r in tall]
    return pl.pallas_call(
        begin_kernel,
        out_shape=out,
        in_specs=[hbm] * 8,
        out_specs=[vmem] * 7,
        scratch_shapes=[
            pltpu.VMEM((TOK, D), BF16),
            pltpu.VMEM((2, D), F32),
            pltpu.VMEM((3, ROWS, COLS), BF16),
            pltpu.VMEM((3, ROWS // 4, COLS), I32),
            pltpu.SemaphoreType.DMA((8,)),
        ],
        compiler_params=pltpu.CompilerParams(vmem_limit_bytes=60 * MIB),
        cost_estimate=pl.CostEstimate(flops=10**8, bytes_accessed=6 * 10**6, transcendentals=0),
        name="norm_and_mask",
    )(h, modulation, wq, wk, wv, mq, mk, mv)


def offsets(xs):
    starts = [0]
    for x in xs:
        starts.append(starts[-1] + x.shape[0])
    return starts


def edges_of(parts):
    return [sum(parts[:p]) for p in range(len(parts) + 1)]


def start_all(copies):
    for copy in copies:
        copy.start()


def wait_all(copies):
    for copy in copies:
        copy.wait()


def in_order(groups):
    start_all(groups[0])
    begun = [1]

    def need(g):
        wait_all(groups[g])
        while begun[0] < min(g + 3, len(groups)):
            start_all(groups[begun[0]])
            begun[0] += 1

    return need


def copies_of_x(xs, x_v, sem, column):
    at = offsets(xs)
    return [
        pltpu.make_async_copy(x.at[:, pl.ds(column, HALF)], x_v.at[at[j] : at[j + 1], :], sem.at[j])
        for j, x in enumerate(xs)
    ]


def copies_of_w(place, ws, w_v, sem, there, here, base):
    out = []
    for j in range(8):
        row = pl.multiple_of(place[1 + j] * ROWS, ROWS)
        out.append(pltpu.make_async_copy(ws[j].at[:, there], w_v.at[pl.ds(row, ROWS), here], sem.at[base + j]))
    return out


def project_kernel(n_x, parts, place, *refs):
    xs, ws, (out, x_v, w_v, y_v, sem_x, sem_w, sem_y) = refs[:n_x], refs[n_x : n_x + 8], refs[n_x + 8 :]
    copies_x = copies_of_x(xs, x_v, sem_x, pl.multiple_of(place[0] * HALF, HALF))
    edges = edges_of(parts)
    here = [slice(edges[p], edges[p + 1]) for p in range(len(parts))]
    copies_w = [copies_of_w(place, ws, w_v, sem_w, cols, cols, p * 8) for p, cols in enumerate(here)]
    need = in_order([copies_w[0] + copies_x] + copies_w[1:])
    sent = []
    for p, cols in enumerate(here):
        need(p)
        y_v[:, cols] = jnp.dot(x_v[...], w_v[:, cols], preferred_element_type=F32)
        sent.append(pltpu.make_async_copy(y_v.at[:, cols], out.at[:, cols], sem_y.at[p]))
        sent[-1].start()
    wait_all(sent)


def project(place, xs, ws):
    n_x = len(xs)
    rows = offsets(xs)[-1]
    parts = (256, 512, 512, 640)
    width = 3 * COLS
    hbm = pl.BlockSpec(memory_space=pltpu.HBM)
    return pl.pallas_call(
        functools.partial(project_kernel, n_x, parts),
        out_shape=jax.ShapeDtypeStruct((rows, width), F32),
        in_specs=[pl.BlockSpec(memory_space=pltpu.SMEM)] + [hbm] * (n_x + 8),
        out_specs=hbm,
        scratch_shapes=[
            pltpu.VMEM((rows, HALF), BF16),
            pltpu.VMEM((HALF, width), BF16),
            pltpu.VMEM((rows, width), F32),
            pltpu.SemaphoreType.DMA((n_x,)),
            pltpu.SemaphoreType.DMA((8 * len(parts),)),
            pltpu.SemaphoreType.DMA((len(parts),)),
        ],
        compiler_params=pltpu.CompilerParams(vmem_limit_bytes=60 * MIB),
        cost_estimate=pl.CostEstimate(flops=10**6, bytes_accessed=10**5, transcendentals=0),
        name="project_first",
    )(place, *xs, *ws)


def finish_kernel(n_x, parts, place, *refs):
    xs, ws, accs, refs = refs[:n_x], refs[n_x : n_x + 8], refs[n_x + 8 : n_x + 10], refs[n_x + 10 :]
    qk_out, v_out, sq_out, x_v, w_v, a_v, y_v, v_v, sem_x, sem_w, sem_a, sem_y = refs
    copies_x = copies_of_x(xs, x_v, sem_x, pl.multiple_of(place[0] * HALF, HALF))
    n = len(parts)
    edges = edges_of(parts)
    middle = 4 * TOK
    groups = []
    for p in range(n):
        cols = slice(edges[p], edges[p + 1])
        copies_w = copies_of_w(place, ws, w_v, sem_w, cols, cols, p * 8)
        copies_a = [
            pltpu.make_async_copy(acc.at[:, cols], a_v.at[i * middle : (i + 1) * middle, cols], sem_a.at[p * 2 + i])
            for i, acc in enumerate(accs)
        ]
        groups += [copies_w + copies_x[:4], copies_x[4:] + copies_a] if p == 0 else [copies_w + copies_a]
    need = in_order(groups)
    need(0)
    sent = []
    for p in range(n):
        cols = slice(edges[p], edges[p + 1])
        if p:
            need(p + 1)
        for i in range(2):
            rows = slice(i * middle, (i + 1) * middle)
            y = jnp.dot(x_v[rows, :], w_v[:, cols], preferred_element_type=F32)
            if p == 0 and i == 0:
                need(1)
            y = y + a_v[rows, cols]
            if edges[p] >= 2 * COLS:
                v_v[rows, :] = y.astype(BF16)
                target, source = v_out, v_v
            else:
                y_v[rows, cols] = y
                target, source = qk_out.at[:, cols], y_v.at[:, cols]
            for part in range(2):
                low, high = max(edges[p], part * COLS), min(edges[p + 1], (part + 1) * COLS)
                if low >= high:
                    continue
                squares = y[:, low - edges[p] : high - edges[p]]
                squares = squares * squares
                lanes = sum(squares[:, h : h + 128] for h in range(0, high - low, 128))
                for b in range(4):
                    line = jnp.sum(lanes[b * TOK : (b + 1) * TOK, :].T, axis=0, keepdims=True)
                    at = place[9 + i * 4 + b]
                    if low > part * COLS:
                        line = line + sq_out[at, part : part + 1, :]
                    sq_out[at, part : part + 1, :] = line
        sent.append(pltpu.make_async_copy(source, target, sem_y.at[p]))
        sent[-1].start()
    wait_all(sent)


def finish(place, xs, ws, accs):
    parts = (256, 512, 512, 640)
    n = len(parts)
    rows = 8 * TOK
    width = 3 * COLS
    hbm = pl.BlockSpec(memory_space=pltpu.HBM)
    n_x = len(xs)
    return pl.pallas_call(
        functools.partial(finish_kernel, n_x, parts),
        out_shape=[
            jax.ShapeDtypeStruct((rows, 2 * COLS), F32),
            jax.ShapeDtypeStruct((rows, COLS), BF16),
            jax.ShapeDtypeStruct((8, 8, TOK), F32),
        ],
        in_specs=[pl.BlockSpec(memory_space=pltpu.SMEM)] + [hbm] * (n_x + 10),
        out_specs=[hbm, hbm, pl.BlockSpec(memory_space=pltpu.VMEM)],
        scratch_shapes=[
            pltpu.VMEM((rows, HALF), BF16),
            pltpu.VMEM((HALF, width), BF16),
            pltpu.VMEM((rows, width), F32),
            pltpu.VMEM((rows, 2 * COLS), F32),
            pltpu.VMEM((rows, COLS), BF16),
            pltpu.SemaphoreType.DMA((n_x,)),
            pltpu.SemaphoreType.DMA((8 * n,)),
            pltpu.SemaphoreType.DMA((2 * n,)),
            pltpu.SemaphoreType.DMA((n,)),
        ],
        compiler_params=pltpu.CompilerParams(vmem_limit_bytes=60 * MIB),
        cost_estimate=pl.CostEstimate(flops=2 * rows * HALF * width, bytes_accessed=30 * 10**6, transcendentals=0),
        name="project_last",
    )(place, *xs, *ws, *accs)


def gram_kernel(tokens, n_x, added, place, *refs):
    xs, refs = refs[:n_x], refs[n_x:]
    sums, refs = refs[: 2 * added], refs[2 * added :]
    outs, (own_x, x_v, own, o_v, sem_own, sem_x, sem_o), (*more,) = refs[:2], refs[2:9], refs[9:]
    at = offsets(xs)
    n = 4
    step = D // n
    column = pl.multiple_of(place[0] * COLS, COLS)
    first = [
        pltpu.make_async_copy(x.at[:, pl.ds(column, COLS)], own_x.at[at[j] : at[j + 1], :], sem_own.at[j])
        for j, x in enumerate(xs)
    ]
    rest = []
    for i in range(n):
        cols = slice(i * step, (i + 1) * step)
        some = [
            pltpu.make_async_copy(x.at[:, cols], x_v.at[at[j] : at[j + 1], cols], sem_x.at[i, j])
            for j, x in enumerate(xs)
        ]
        for j, old in enumerate(sums):
            s_v, sem_s = more
            some.append(
                pltpu.make_async_copy(old.at[:, cols], s_v.at[j * ROWS : (j + 1) * ROWS, cols], sem_s.at[i, j])
            )
        rest.append(some)
    need = in_order([first] + rest)
    line = lax.broadcasted_iota(I32, (COLS, COLS), 0)
    core = jnp.where(line < ROWS, 1 - place[1], place[1])
    source = ((line // 40 % XH * Z + line // 80 % Z) * C + core) * 40 + line % 40
    order = (source == lax.broadcasted_iota(I32, (COLS, COLS), 1)).astype(F32).astype(BF16)
    need(0)
    own[...] = lax.dot_general(
        order, own_x[...], (((1,), (1,)), ((), ())), preferred_element_type=F32
    ).astype(BF16)
    sends = []
    for i in range(n):
        cols = slice(i * step, (i + 1) * step)
        need(i + 1)
        for j, out in enumerate(outs):
            rows = slice(j * ROWS, (j + 1) * ROWS)
            y = jnp.dot(own[rows, :], x_v[:, cols], preferred_element_type=F32) * (1.0 / tokens)
            if added:
                y = y + more[0][rows, cols].astype(F32)
            o_v[rows, cols] = y.astype(BF16)
            sends.append(pltpu.make_async_copy(o_v.at[rows, cols], out.at[:, cols], sem_o.at[i, j]))
            sends[-1].start()
    wait_all(sends)


def gram_rows(place, xs, tokens, sums=()):
    hbm = pl.BlockSpec(memory_space=pltpu.HBM)
    n_x = len(xs)
    count = offsets(xs)[-1]
    scratch = [
        pltpu.VMEM((count, COLS), BF16),
        pltpu.VMEM((count, D), BF16),
        pltpu.VMEM((COLS, count), BF16),
        pltpu.VMEM((COLS, D), BF16),
        pltpu.SemaphoreType.DMA((n_x,)),
        pltpu.SemaphoreType.DMA((4, n_x)),
        pltpu.SemaphoreType.DMA((4, 2)),
    ]
    if sums:
        scratch += [pltpu.VMEM((COLS, D), BF16), pltpu.SemaphoreType.DMA((4, 2))]
    return pl.pallas_call(
        functools.partial(gram_kernel, tokens, n_x, bool(sums)),
        out_shape=[jax.ShapeDtypeStruct((ROWS, D), BF16)] * 2,
        in_specs=[pl.BlockSpec(memory_space=pltpu.SMEM)] + [hbm] * (n_x + len(sums)),
        out_specs=[hbm] * 2,
        scratch_shapes=scratch,
        compiler_params=pltpu.CompilerParams(vmem_limit_bytes=60 * MIB),
        cost_estimate=pl.CostEstimate(flops=10**6, bytes_accessed=10**5, transcendentals=0),
        name=f"gram_rows_{count}",
    )(place, *xs, *sums)


Z_PART = ROWS // Z


def pair_kernel(place, mine, moved, own, *refs):
    outs, (m_v, sem) = refs[:3], refs[3:]
    order = (1, 3, 2, 0)
    groups = []
    for k in order:
        rows = pl.ds(pl.multiple_of(lax.rem(place[0] + k, Z) * Z_PART, 16), Z_PART)
        groups.append(
            [pltpu.make_async_copy(source.at[rows, :], m_v.at[j, k], sem.at[j, k]) for j, source in enumerate((mine, moved))]
        )
    for some in groups:
        start_all(some)
    for g, k in enumerate(order):
        wait_all(groups[g])
        y = m_v[0, k].astype(F32) + m_v[1, k].astype(F32)
        if k == 0:
            own[...] = y
        else:
            outs[k - 1][...] = y.astype(BF16)


def add_pair(place, mine, moved):
    hbm = pl.BlockSpec(memory_space=pltpu.HBM)
    vmem = pl.BlockSpec(memory_space=pltpu.VMEM)
    return pl.pallas_call(
        pair_kernel,
        out_shape=[jax.ShapeDtypeStruct((Z_PART, D), F32)] + [jax.ShapeDtypeStruct((Z_PART, D), BF16)] * 3,
        in_specs=[pl.BlockSpec(memory_space=pltpu.SMEM), hbm, hbm],
        out_specs=[vmem] * 4,
        scratch_shapes=[pltpu.VMEM((2, Z, Z_PART, D), BF16), pltpu.SemaphoreType.DMA((2, Z))],
        compiler_params=pltpu.CompilerParams(vmem_limit_bytes=60 * MIB),
        cost_estimate=pl.CostEstimate(flops=10**6, bytes_accessed=10**7, transcendentals=0),
        name="gram_pair",
    )(place, mine, moved)


def z_kernel(place, own, one, two, three, kept, sent, total_v):
    total_v[...] = own[...] + one[...].astype(F32) + two[...].astype(F32) + three[...].astype(F32)
    rows = Z_PART // XH
    kept[...] = total_v[pl.ds(pl.multiple_of(place[0] * rows, 8), rows), :]
    sent[...] = total_v[pl.ds(pl.multiple_of((1 - place[0]) * rows, 8), rows), :].astype(BF16)


def add_z(place, own, *others):
    vmem = pl.BlockSpec(memory_space=pltpu.VMEM)
    rows = Z_PART // XH
    return pl.pallas_call(
        z_kernel,
        out_shape=[jax.ShapeDtypeStruct((rows, D), F32), jax.ShapeDtypeStruct((rows, D), BF16)],
        in_specs=[pl.BlockSpec(memory_space=pltpu.SMEM)] + [vmem] * 4,
        out_specs=[vmem] * 2,
        scratch_shapes=[pltpu.VMEM((Z_PART, D), F32)],
        compiler_params=pltpu.CompilerParams(vmem_limit_bytes=32 * MIB),
        cost_estimate=pl.CostEstimate(flops=10**6, bytes_accessed=4 * 10**6, transcendentals=0),
        name="gram_z",
    )(place, own, *others)


def up_z(x, k):
    return permute(x, lambda xh, z, c, y, xl: (xh, (z + k) % Z, c, y, xl))


def rope_tables(place):
    inside = jnp.arange(TOK, dtype=I32)[None, :]
    blocks = place[:, None]
    frame_pos = jnp.broadcast_to(blocks // 2, (8, TOK)).reshape(-1).astype(F32)
    row_pos = (blocks % 2 * 8 + inside // WIDTH).reshape(-1).astype(F32)
    col_pos = jnp.broadcast_to(inside % WIDTH, (8, TOK)).reshape(-1).astype(F32)
    half_dim = HEAD_DIM // 2
    spatial = HEAD_DIM // 6
    temporal = half_dim - 2 * spatial
    entry = jnp.arange(HEAD_DIM, dtype=I32)
    pair_ids = entry // 2
    exponent = jnp.where(
        pair_ids < temporal,
        2.0 * pair_ids / (2.0 * temporal),
        jnp.where(
            pair_ids < temporal + spatial,
            2.0 * (pair_ids - temporal) / (2.0 * spatial),
            2.0 * (pair_ids - temporal - spatial) / (2.0 * spatial),
        ),
    ).astype(F32)
    frequency = jnp.power(jnp.float32(10000.0), -exponent)
    chosen_pos = jnp.where(
        pair_ids[None, :] < temporal,
        frame_pos[:, None],
        jnp.where(pair_ids[None, :] < temporal + spatial, row_pos[:, None], col_pos[:, None]),
    )
    angles = chosen_pos * frequency[None, :]
    sine = jnp.sin(angles)
    even = (entry % 2 == 0)[None, :]
    return jnp.cos(angles), jnp.where(even, -sine, 0.0), jnp.where(even, 0.0, sine)


def attend_kernel(half, place, q_ref, k_ref, v_ref, *refs):
    squares, (gain_q, gain_k, cosine, sine_l, sine_r), outs = refs[:2], refs[2:7], refs[7:11]
    scale_v, line_v = refs[11:]

    @pl.when(pl.program_id(0) == 0)
    def _():
        scale = lax.rsqrt((squares[0][...] + squares[1][...]) / D + 1e-06)
        for b in range(8):
            line_v[b * 8 : (b + 1) * 8, :] = scale[b]
        for b in range(8):
            source = place[b]
            for part in range(2):
                line = line_v[pl.ds(source * 8 + part, 1), :]
                scale_v[part, b * TOK : (b + 1) * TOK, :] = jnp.broadcast_to(line, (TOK, TOK)).T

    factor = HEAD_DIM ** (-0.5) * 1.4426950408889634

    def rotate(x, part, gain, rows):
        x = x * scale_v[part, rows, :] * gain
        left = pltpu.roll(x, HEAD_DIM - 1, 1)
        right = pltpu.roll(x, 1, 1)
        return (x * cosine[rows, :] + left * sine_l[rows, :] + right * sine_r[rows, :]).astype(BF16)

    every = slice(0, 8 * TOK)
    keys = rotate(k_ref[...], 1, gain_k[...], every)
    values = v_ref[...]
    tile = 256
    for i in range(4 * TOK // tile):
        inside = slice(i * tile, (i + 1) * tile)
        rows = slice(half * 4 * TOK + i * tile, half * 4 * TOK + (i + 1) * tile)
        q = rotate(q_ref[inside, :], 0, gain_q[...] * factor, rows)
        scores = lax.dot_general(q, keys, (((1,), (1,)), ((), ())), preferred_element_type=F32)
        top = jnp.max(scores, axis=-1, keepdims=True)
        weights = jnp.exp2(scores - top)
        total = jnp.sum(weights, axis=-1, keepdims=True)
        out = jnp.dot(weights.astype(BF16), values, preferred_element_type=F32)
        out = (out * (1.0 / total)).astype(BF16)
        for b in range(tile // TOK):
            outs[i * (tile // TOK) + b][...] = out[b * TOK : (b + 1) * TOK, :]


def attend(half, place, qk, v, squares, gain_q, gain_k, tables):
    query = pl.BlockSpec((4 * TOK, HEAD_DIM), lambda h: (half, h))
    key = pl.BlockSpec((8 * TOK, HEAD_DIM), lambda h: (0, HEADS + h))
    head = pl.BlockSpec((8 * TOK, HEAD_DIM), lambda h: (0, h))
    gain = pl.BlockSpec((1, HEAD_DIM), lambda h: (0, h))
    table = pl.BlockSpec((8 * TOK, HEAD_DIM), lambda h: (0, 0))
    square = pl.BlockSpec((8, 8, TOK), lambda h: (0, 0, 0))
    return pl.pallas_call(
        functools.partial(attend_kernel, half),
        out_shape=(jax.ShapeDtypeStruct((TOK, COLS), BF16),) * 4,
        grid=(HEADS,),
        in_specs=[pl.BlockSpec(memory_space=pltpu.SMEM), query, key, head]
        + [square] * 2
        + [gain, gain, table, table, table],
        out_specs=(pl.BlockSpec((TOK, HEAD_DIM), lambda h: (0, h)),) * 4,
        scratch_shapes=[pltpu.VMEM((2, 8 * TOK, TOK), F32), pltpu.VMEM((64, TOK), F32)],
        compiler_params=pltpu.CompilerParams(vmem_limit_bytes=60 * MIB),
        cost_estimate=pl.CostEstimate(flops=2 * 1024 * 1024 * COLS, bytes_accessed=10**7, transcendentals=5 * 2**19),
        name=f"attend_{half}",
    )(place, qk, qk, v, *squares, gain_q[None], gain_k[None], *tables)


def gather_kernel(place, *refs):
    pieces, out = refs[:8], refs[8]
    for j in range(8):
        column = pl.multiple_of(place[j] * COLS, COLS)
        out[0, :, pl.ds(column, COLS)] = pieces[j][...]


def gather_columns(place, pieces):
    vmem = pl.BlockSpec(memory_space=pltpu.VMEM)
    return pl.pallas_call(
        gather_kernel,
        out_shape=jax.ShapeDtypeStruct((1, TOK, D), BF16),
        in_specs=[pl.BlockSpec(memory_space=pltpu.SMEM)] + [vmem] * 8,
        out_specs=vmem,
        compiler_params=pltpu.CompilerParams(vmem_limit_bytes=16 * MIB),
        cost_estimate=pl.CostEstimate(flops=0, bytes_accessed=3 * 10**6, transcendentals=0),
        name="gather_columns",
    )(place, *pieces)


def per_device(h, modulation, wq, wk, wv, mq, mk, mv, gain_q, gain_k):
    xh, z, c, y, xl = (lax.axis_index(a).astype(I32) for a in AXES)
    way = 1 - 2 * c
    blocks = [(s, dx) for dx in range(2) for s in range(4)]
    canonical = jnp.stack([((y - way * s) % Y) * 2 + (xl ^ dx) for s, dx in blocks])
    sources = jnp.stack([((y + way * s) % Y) * 2 + (xl ^ dx) for s, dx in blocks])
    rows = [((z - way * s) % Z) * 2 + c for s in range(4)] + [((z + way * s) % Z) * 2 + 1 - c for s in range(4)]
    place_1 = jnp.concatenate([jnp.stack([xh] + rows), canonical])
    place_2 = jnp.concatenate([jnp.stack([1 - xh] + rows), canonical])
    me = jnp.stack([y * 2 + xl, c])

    x0, x0_lo, x0_hi, w0, w0_lo, w0_mid, w0_hi = begin(h, modulation, wq, wk, wv, mq, mk, mv)

    half = TOK // 2
    x1, w1, b0_lo, p0_lo = stage(ring_y(x0), ring_z(w0), swap_xl(x0_lo), swap_xh(w0_lo))
    x2, w2, b0_hi, p0_mid, e0, *tables = stage(
        ring_y(x1), ring_z(w1), swap_xl(x0_hi), swap_xh(w0_mid), swap_c(w0), *rope_tables(canonical)
    )
    x3, w3, p0_hi, e1, e2 = stage(ring_y(x2), ring_z(w2), swap_xh(w0_hi), swap_c(w1), swap_c(w2))
    b0 = jnp.concatenate([b0_lo, b0_hi])
    p0 = jnp.concatenate([p0_lo, p0_mid, p0_hi])
    e3 = swap_c(w3)
    own_half = [w0, w1, w2, w3, e0, e1, e2, e3]
    xs_a = [x0, x1, x2, x3]
    acc_a = project(place_1, xs_a, own_half)
    b1, p1, b3_lo, acc_a = stage(ring_y(b0), ring_z(p0), swap_xl(x3[:half]), acc_a)
    f0 = swap_c(p0)
    f1 = swap_c(p1)
    tokens = XH * Z * C * 8 * TOK
    sums = gram_rows(me, xs_a + [b0, b1], tokens)
    b2, p2, b3_hi, f0, f1, *sums = stage(ring_y(b1), ring_z(p1), swap_xl(x3[half:]), f0, f1, *sums)
    xs_b = [b0, b1, b2, b3_lo, b3_hi]

    f2 = swap_c(p2)
    theirs, mine = gram_rows(me, [b2, b3_lo, b3_hi], tokens, sums)
    theirs, f2, *xs_b = stage(theirs, f2, *xs_b)
    moved = swap_c(theirs)
    acc_b = project(place_1, xs_b, own_half)
    moved, mine, acc_b = stage(moved, mine, acc_b)
    part_0, part_1, part_2, part_3 = add_pair(z[None], mine, moved)
    part_0, part_1, part_2, part_3, p3, acc_a = stage(part_0, part_1, part_2, part_3, ring_z(p2), acc_a)
    f3 = swap_c(p3)
    summed = [part_0, up_z(part_1, 1), up_z(part_2, 2), up_z(part_3, 3)]
    other_half = [p0, p1, p2, p3, f0, f1, f2, f3]

    qk, v, squares = finish(place_2, xs_a + xs_b, other_half, [acc_a, acc_b])
    ring = squares + sum(to_owner(squares, s, 0) for s in range(1, Y))
    both = [ring, swap_xl(ring)]
    late = attend(1, canonical, qk, v, both, gain_q, gain_k, tables)
    late = list(late)
    late[0], *summed = stage(late[0], *summed)
    kept, sent = add_z(xh[None], *summed)
    pieces_late = [to_owner(o, s, 1) for o, s in zip(late, range(Y))]
    early = attend(0, canonical, stage(qk, late[0])[0], v, both, gain_q, gain_k, tables)
    *rest, sent = stage(*early, *pieces_late, sent)
    early, pieces_late = rest[:4], rest[4:]
    gram = kept + swap_xh(sent).astype(F32)
    pieces = [early[0]] + [to_owner(o, s, 0) for o, s in zip(early[1:], range(1, Y))]
    return gather_columns(sources, pieces + pieces_late), gram[None]


def solution(mesh):
    fine = Mesh(mesh.devices.reshape(XH, Z, C, Y, XL), AXES)
    grp, sp = ("xh", "z", "c"), ("y", "xl")
    return jax.shard_map(
        per_device,
        mesh=fine,
        in_specs=(
            P(grp, sp, None),
            P(grp, None, None),
            P(grp, sp),
            P(grp, sp),
            P(grp, sp),
            P(grp, sp),
            P(grp, sp),
            P(grp, sp),
            P(sp),
            P(sp),
        ),
        out_specs=(P(grp, sp, None), P(sp, grp, None)),
        check_vma=False,
    )
```

```python
import functools

import jax
import jax.numpy as jnp
from jax import lax
from jax.experimental import pallas as pl
from jax.experimental.pallas import tpu as pltpu
from jax.sharding import Mesh
from jax.sharding import PartitionSpec as P

HEAD_DIM = 128
HEIGHT = 16
WIDTH = 16
XH, Z, C, Y, XL = 2, 4, 2, 4, 2
AXES = ("xh", "z", "c", "y", "xl")
TOK = 128
D = 5120
COLS = 640
ROWS = 320
HALF = D // 2
HEADS = 5
BF16, F32, I32 = jnp.bfloat16, jnp.float32, jnp.int32
MIB = 1 << 20


def linear(xh, z, c, y, xl):
    return (((xh * Z + z) * C + c) * Y + y) * XL + xl


def permute(x, move):
    pairs = []
    for xh in range(XH):
        for z in range(Z):
            for c in range(C):
                for y in range(Y):
                    for xl in range(XL):
                        pairs.append((linear(xh, z, c, y, xl), linear(*move(xh, z, c, y, xl))))
    return lax.ppermute(x, AXES, pairs)


def turn(c):
    return 1 if c == 0 else -1


def ring_y(x):
    return permute(x, lambda xh, z, c, y, xl: (xh, z, c, (y + turn(c)) % Y, xl))


def ring_z(x):
    return permute(x, lambda xh, z, c, y, xl: (xh, (z + turn(c)) % Z, c, y, xl))


def swap_xl(x):
    return permute(x, lambda xh, z, c, y, xl: (xh, z, c, y, 1 - xl))


def swap_xh(x):
    return permute(x, lambda xh, z, c, y, xl: (1 - xh, z, c, y, xl))


def swap_c(x):
    return permute(x, lambda xh, z, c, y, xl: (xh, z, 1 - c, y, xl))


def to_owner(x, s, dx):
    return permute(x, lambda xh, z, c, y, xl: (xh, z, c, (y - turn(c) * s) % Y, xl ^ dx))


def stage(*arrays):
    return lax.optimization_barrier(arrays)


HALVES = ((0, TOK // 2), (TOK // 2, TOK))
CHUNKS = ((0, 32), (32, 64), (64, ROWS))


def begin_kernel(h, modulation, wq, wk, wv, mq, mk, mv, *refs):
    x_out, x_lo, x_hi, w_out, w_lo, w_mid, w_hi = refs[:7]
    h_v, mod_v, w_v, m_v, sem = refs[7:]
    pairs = [(h.at[0], h_v), (modulation.at[0], mod_v)]
    pairs += [(w, w_v.at[i]) for i, w in enumerate((wq, wk, wv))]
    pairs += [(m, m_v.at[i]) for i, m in enumerate((mq, mk, mv))]
    copies = [pltpu.make_async_copy(source, target, sem.at[i]) for i, (source, target) in enumerate(pairs)]
    for copy in copies:
        copy.start()
    for copy in copies[:2]:
        copy.wait()
    scale = 1.0 + mod_v[1:2, :]
    shift = mod_v[0:1, :]
    step = 32
    for i in range(TOK // step):
        x = h_v[i * step : (i + 1) * step, :].astype(F32)
        average = jnp.mean(x, axis=-1, keepdims=True)
        centred = x - average
        variance = jnp.mean(centred * centred, axis=-1, keepdims=True)
        y = (centred * lax.rsqrt(variance + 1e-06) * scale + shift).astype(BF16)
        x_out[i * step : (i + 1) * step, :] = y
        piece, at = (x_lo, i * step) if i * step < TOK // 2 else (x_hi, i * step - TOK // 2)
        piece[at : at + step, :] = y
    group = lax.broadcasted_iota(I32, (ROWS, ROWS // 4), 0) // 4
    spread = (group == lax.broadcasted_iota(I32, (ROWS, ROWS // 4), 1)).astype(F32).astype(BF16)
    slot = lax.broadcasted_iota(I32, (ROWS, COLS), 0) % 4
    for i in range(3):
        copies[2 + i].wait()
        copies[5 + i].wait()
        p = m_v[i]
        bits = jnp.where(p == 0, 3, jnp.where(p == 1, 5, jnp.where(p == 2, 9, jnp.where(p == 3, 6, jnp.where(p == 4, 10, 12)))))
        rows = jnp.dot(spread, bits.astype(F32).astype(BF16), preferred_element_type=F32).astype(I32)
        kept = (lax.shift_right_logical(rows, slot) & 1) == 1
        masked = jnp.where(kept, w_v[i].astype(F32), 0.0).astype(BF16)
        cols = slice(i * COLS, (i + 1) * COLS)
        w_out[:, cols] = masked
        for piece, (low, high) in zip((w_lo, w_mid, w_hi), CHUNKS):
            piece[:, cols] = masked[low:high, :]


def begin(h, modulation, wq, wk, wv, mq, mk, mv):
    hbm = pl.BlockSpec(memory_space=pltpu.HBM)
    vmem = pl.BlockSpec(memory_space=pltpu.VMEM)
    rows = [TOK, TOK // 2, TOK // 2]
    tall = [ROWS] + [high - low for low, high in CHUNKS]
    out = [jax.ShapeDtypeStruct((r, D), BF16) for r in rows] + [jax.ShapeDtypeStruct((r, 3 * COLS), BF16) for r in tall]
    return pl.pallas_call(
        begin_kernel,
        out_shape=out,
        in_specs=[hbm] * 8,
        out_specs=[vmem] * 7,
        scratch_shapes=[
            pltpu.VMEM((TOK, D), BF16),
            pltpu.VMEM((2, D), F32),
            pltpu.VMEM((3, ROWS, COLS), BF16),
            pltpu.VMEM((3, ROWS // 4, COLS), I32),
            pltpu.SemaphoreType.DMA((8,)),
        ],
        compiler_params=pltpu.CompilerParams(vmem_limit_bytes=60 * MIB),
        cost_estimate=pl.CostEstimate(flops=10**8, bytes_accessed=6 * 10**6, transcendentals=0),
        name="norm_and_mask",
    )(h, modulation, wq, wk, wv, mq, mk, mv)


def offsets(xs):
    starts = [0]
    for x in xs:
        starts.append(starts[-1] + x.shape[0])
    return starts


def edges_of(parts):
    return [sum(parts[:p]) for p in range(len(parts) + 1)]


def start_all(copies):
    for copy in copies:
        copy.start()


def wait_all(copies):
    for copy in copies:
        copy.wait()


def in_order(groups):
    start_all(groups[0])
    begun = [1]

    def need(g):
        wait_all(groups[g])
        while begun[0] < min(g + 3, len(groups)):
            start_all(groups[begun[0]])
            begun[0] += 1

    return need


def copies_of_x(xs, x_v, sem, column):
    at = offsets(xs)
    return [
        pltpu.make_async_copy(x.at[:, pl.ds(column, HALF)], x_v.at[at[j] : at[j + 1], :], sem.at[j])
        for j, x in enumerate(xs)
    ]


def copies_of_w(place, ws, w_v, sem, there, here, base):
    out = []
    for j in range(8):
        row = pl.multiple_of(place[1 + j] * ROWS, ROWS)
        out.append(pltpu.make_async_copy(ws[j].at[:, there], w_v.at[pl.ds(row, ROWS), here], sem.at[base + j]))
    return out


def project_kernel(n_x, parts, place, *refs):
    xs, ws, (out, x_v, w_v, y_v, sem_x, sem_w, sem_y) = refs[:n_x], refs[n_x : n_x + 8], refs[n_x + 8 :]
    copies_x = copies_of_x(xs, x_v, sem_x, pl.multiple_of(place[0] * HALF, HALF))
    edges = edges_of(parts)
    here = [slice(edges[p], edges[p + 1]) for p in range(len(parts))]
    copies_w = [copies_of_w(place, ws, w_v, sem_w, cols, cols, p * 8) for p, cols in enumerate(here)]
    need = in_order([copies_w[0] + copies_x] + copies_w[1:])
    sent = []
    for p, cols in enumerate(here):
        need(p)
        y_v[:, cols] = jnp.dot(x_v[...], w_v[:, cols], preferred_element_type=F32)
        sent.append(pltpu.make_async_copy(y_v.at[:, cols], out.at[:, cols], sem_y.at[p]))
        sent[-1].start()
    wait_all(sent)


def project(place, xs, ws):
    n_x = len(xs)
    rows = offsets(xs)[-1]
    parts = (256, 512, 512, 640)
    width = 3 * COLS
    hbm = pl.BlockSpec(memory_space=pltpu.HBM)
    return pl.pallas_call(
        functools.partial(project_kernel, n_x, parts),
        out_shape=jax.ShapeDtypeStruct((rows, width), F32),
        in_specs=[pl.BlockSpec(memory_space=pltpu.SMEM)] + [hbm] * (n_x + 8),
        out_specs=hbm,
        scratch_shapes=[
            pltpu.VMEM((rows, HALF), BF16),
            pltpu.VMEM((HALF, width), BF16),
            pltpu.VMEM((rows, width), F32),
            pltpu.SemaphoreType.DMA((n_x,)),
            pltpu.SemaphoreType.DMA((8 * len(parts),)),
            pltpu.SemaphoreType.DMA((len(parts),)),
        ],
        compiler_params=pltpu.CompilerParams(vmem_limit_bytes=60 * MIB),
        cost_estimate=pl.CostEstimate(flops=10**6, bytes_accessed=10**5, transcendentals=0),
        name="project_first",
    )(place, *xs, *ws)


def finish_kernel(n_x, parts, place, *refs):
    xs, ws, accs, refs = refs[:n_x], refs[n_x : n_x + 8], refs[n_x + 8 : n_x + 10], refs[n_x + 10 :]
    qk_out, v_out, sq_out, x_v, w_v, a_v, y_v, v_v, sem_x, sem_w, sem_a, sem_y = refs
    copies_x = copies_of_x(xs, x_v, sem_x, pl.multiple_of(place[0] * HALF, HALF))
    n = len(parts)
    edges = edges_of(parts)
    middle = 4 * TOK
    groups = []
    for p in range(n):
        cols = slice(edges[p], edges[p + 1])
        copies_w = copies_of_w(place, ws, w_v, sem_w, cols, cols, p * 8)
        copies_a = [
            pltpu.make_async_copy(acc.at[:, cols], a_v.at[i * middle : (i + 1) * middle, cols], sem_a.at[p * 2 + i])
            for i, acc in enumerate(accs)
        ]
        groups += [copies_w + copies_x[:4], copies_x[4:] + copies_a] if p == 0 else [copies_w + copies_a]
    need = in_order(groups)
    need(0)
    sent = []
    for p in range(n):
        cols = slice(edges[p], edges[p + 1])
        if p:
            need(p + 1)
        for i in range(2):
            rows = slice(i * middle, (i + 1) * middle)
            y = jnp.dot(x_v[rows, :], w_v[:, cols], preferred_element_type=F32)
            if p == 0 and i == 0:
                need(1)
            y = y + a_v[rows, cols]
            if edges[p] >= 2 * COLS:
                v_v[rows, :] = y.astype(BF16)
                target, source = v_out, v_v
            else:
                y_v[rows, cols] = y
                target, source = qk_out.at[:, cols], y_v.at[:, cols]
            for part in range(2):
                low, high = max(edges[p], part * COLS), min(edges[p + 1], (part + 1) * COLS)
                if low >= high:
                    continue
                squares = y[:, low - edges[p] : high - edges[p]]
                squares = squares * squares
                lanes = sum(squares[:, h : h + 128] for h in range(0, high - low, 128))
                for b in range(4):
                    line = jnp.sum(lanes[b * TOK : (b + 1) * TOK, :].T, axis=0, keepdims=True)
                    at = place[9 + i * 4 + b]
                    if low > part * COLS:
                        line = line + sq_out[at, part : part + 1, :]
                    sq_out[at, part : part + 1, :] = line
        sent.append(pltpu.make_async_copy(source, target, sem_y.at[p]))
        sent[-1].start()
    wait_all(sent)


def finish(place, xs, ws, accs):
    parts = (256, 512, 512, 640)
    n = len(parts)
    rows = 8 * TOK
    width = 3 * COLS
    hbm = pl.BlockSpec(memory_space=pltpu.HBM)
    n_x = len(xs)
    return pl.pallas_call(
        functools.partial(finish_kernel, n_x, parts),
        out_shape=[
            jax.ShapeDtypeStruct((rows, 2 * COLS), F32),
            jax.ShapeDtypeStruct((rows, COLS), BF16),
            jax.ShapeDtypeStruct((8, 8, TOK), F32),
        ],
        in_specs=[pl.BlockSpec(memory_space=pltpu.SMEM)] + [hbm] * (n_x + 10),
        out_specs=[hbm, hbm, pl.BlockSpec(memory_space=pltpu.VMEM)],
        scratch_shapes=[
            pltpu.VMEM((rows, HALF), BF16),
            pltpu.VMEM((HALF, width), BF16),
            pltpu.VMEM((rows, width), F32),
            pltpu.VMEM((rows, 2 * COLS), F32),
            pltpu.VMEM((rows, COLS), BF16),
            pltpu.SemaphoreType.DMA((n_x,)),
            pltpu.SemaphoreType.DMA((8 * n,)),
            pltpu.SemaphoreType.DMA((2 * n,)),
            pltpu.SemaphoreType.DMA((n,)),
        ],
        compiler_params=pltpu.CompilerParams(vmem_limit_bytes=60 * MIB),
        cost_estimate=pl.CostEstimate(flops=2 * rows * HALF * width, bytes_accessed=30 * 10**6, transcendentals=0),
        name="project_last",
    )(place, *xs, *ws, *accs)


def gram_kernel(tokens, n_x, added, place, *refs):
    xs, refs = refs[:n_x], refs[n_x:]
    sums, refs = refs[: 2 * added], refs[2 * added :]
    outs, (own_x, x_v, own, o_v, sem_own, sem_x, sem_o), (*more,) = refs[:2], refs[2:9], refs[9:]
    at = offsets(xs)
    n = 4
    step = D // n
    column = pl.multiple_of(place[0] * COLS, COLS)
    first = [
        pltpu.make_async_copy(x.at[:, pl.ds(column, COLS)], own_x.at[at[j] : at[j + 1], :], sem_own.at[j])
        for j, x in enumerate(xs)
    ]
    rest = []
    for i in range(n):
        cols = slice(i * step, (i + 1) * step)
        some = [
            pltpu.make_async_copy(x.at[:, cols], x_v.at[at[j] : at[j + 1], cols], sem_x.at[i, j])
            for j, x in enumerate(xs)
        ]
        for j, old in enumerate(sums):
            s_v, sem_s = more
            some.append(
                pltpu.make_async_copy(old.at[:, cols], s_v.at[j * ROWS : (j + 1) * ROWS, cols], sem_s.at[i, j])
            )
        rest.append(some)
    need = in_order([first] + rest)
    line = lax.broadcasted_iota(I32, (COLS, COLS), 0)
    core = jnp.where(line < ROWS, 1 - place[1], place[1])
    source = ((line // 40 % XH * Z + line // 80 % Z) * C + core) * 40 + line % 40
    order = (source == lax.broadcasted_iota(I32, (COLS, COLS), 1)).astype(F32).astype(BF16)
    need(0)
    own[...] = lax.dot_general(
        order, own_x[...], (((1,), (1,)), ((), ())), preferred_element_type=F32
    ).astype(BF16)
    sends = []
    for i in range(n):
        cols = slice(i * step, (i + 1) * step)
        need(i + 1)
        for j, out in enumerate(outs):
            rows = slice(j * ROWS, (j + 1) * ROWS)
            y = jnp.dot(own[rows, :], x_v[:, cols], preferred_element_type=F32) * (1.0 / tokens)
            if added:
                y = y + more[0][rows, cols].astype(F32)
            o_v[rows, cols] = y.astype(BF16)
            sends.append(pltpu.make_async_copy(o_v.at[rows, cols], out.at[:, cols], sem_o.at[i, j]))
            sends[-1].start()
    wait_all(sends)


def gram_rows(place, xs, tokens, sums=()):
    hbm = pl.BlockSpec(memory_space=pltpu.HBM)
    n_x = len(xs)
    count = offsets(xs)[-1]
    scratch = [
        pltpu.VMEM((count, COLS), BF16),
        pltpu.VMEM((count, D), BF16),
        pltpu.VMEM((COLS, count), BF16),
        pltpu.VMEM((COLS, D), BF16),
        pltpu.SemaphoreType.DMA((n_x,)),
        pltpu.SemaphoreType.DMA((4, n_x)),
        pltpu.SemaphoreType.DMA((4, 2)),
    ]
    if sums:
        scratch += [pltpu.VMEM((COLS, D), BF16), pltpu.SemaphoreType.DMA((4, 2))]
    return pl.pallas_call(
        functools.partial(gram_kernel, tokens, n_x, bool(sums)),
        out_shape=[jax.ShapeDtypeStruct((ROWS, D), BF16)] * 2,
        in_specs=[pl.BlockSpec(memory_space=pltpu.SMEM)] + [hbm] * (n_x + len(sums)),
        out_specs=[hbm] * 2,
        scratch_shapes=scratch,
        compiler_params=pltpu.CompilerParams(vmem_limit_bytes=60 * MIB),
        cost_estimate=pl.CostEstimate(flops=10**6, bytes_accessed=10**5, transcendentals=0),
        name=f"gram_rows_{count}",
    )(place, *xs, *sums)


Z_PART = ROWS // Z


def pair_kernel(place, mine, moved, own, *refs):
    outs, (m_v, sem) = refs[:3], refs[3:]
    order = (1, 3, 2, 0)
    groups = []
    for k in order:
        rows = pl.ds(pl.multiple_of(lax.rem(place[0] + k, Z) * Z_PART, 16), Z_PART)
        groups.append(
            [pltpu.make_async_copy(source.at[rows, :], m_v.at[j, k], sem.at[j, k]) for j, source in enumerate((mine, moved))]
        )
    for some in groups:
        start_all(some)
    for g, k in enumerate(order):
        wait_all(groups[g])
        y = m_v[0, k].astype(F32) + m_v[1, k].astype(F32)
        if k == 0:
            own[...] = y
        else:
            outs[k - 1][...] = y.astype(BF16)


def add_pair(place, mine, moved):
    hbm = pl.BlockSpec(memory_space=pltpu.HBM)
    vmem = pl.BlockSpec(memory_space=pltpu.VMEM)
    return pl.pallas_call(
        pair_kernel,
        out_shape=[jax.ShapeDtypeStruct((Z_PART, D), F32)] + [jax.ShapeDtypeStruct((Z_PART, D), BF16)] * 3,
        in_specs=[pl.BlockSpec(memory_space=pltpu.SMEM), hbm, hbm],
        out_specs=[vmem] * 4,
        scratch_shapes=[pltpu.VMEM((2, Z, Z_PART, D), BF16), pltpu.SemaphoreType.DMA((2, Z))],
        compiler_params=pltpu.CompilerParams(vmem_limit_bytes=60 * MIB),
        cost_estimate=pl.CostEstimate(flops=10**6, bytes_accessed=10**7, transcendentals=0),
        name="gram_pair",
    )(place, mine, moved)


def z_kernel(place, own, one, two, three, kept, sent, total_v):
    total_v[...] = own[...] + one[...].astype(F32) + two[...].astype(F32) + three[...].astype(F32)
    rows = Z_PART // XH
    kept[...] = total_v[pl.ds(pl.multiple_of(place[0] * rows, 8), rows), :]
    sent[...] = total_v[pl.ds(pl.multiple_of((1 - place[0]) * rows, 8), rows), :].astype(BF16)


def add_z(place, own, *others):
    vmem = pl.BlockSpec(memory_space=pltpu.VMEM)
    rows = Z_PART // XH
    return pl.pallas_call(
        z_kernel,
        out_shape=[jax.ShapeDtypeStruct((rows, D), F32), jax.ShapeDtypeStruct((rows, D), BF16)],
        in_specs=[pl.BlockSpec(memory_space=pltpu.SMEM)] + [vmem] * 4,
        out_specs=[vmem] * 2,
        scratch_shapes=[pltpu.VMEM((Z_PART, D), F32)],
        compiler_params=pltpu.CompilerParams(vmem_limit_bytes=32 * MIB),
        cost_estimate=pl.CostEstimate(flops=10**6, bytes_accessed=4 * 10**6, transcendentals=0),
        name="gram_z",
    )(place, own, *others)


def up_z(x, k):
    return permute(x, lambda xh, z, c, y, xl: (xh, (z + k) % Z, c, y, xl))


def rope_tables(place):
    inside = jnp.arange(TOK, dtype=I32)[None, :]
    blocks = place[:, None]
    frame_pos = jnp.broadcast_to(blocks // 2, (8, TOK)).reshape(-1).astype(F32)
    row_pos = (blocks % 2 * 8 + inside // WIDTH).reshape(-1).astype(F32)
    col_pos = jnp.broadcast_to(inside % WIDTH, (8, TOK)).reshape(-1).astype(F32)
    half_dim = HEAD_DIM // 2
    spatial = HEAD_DIM // 6
    temporal = half_dim - 2 * spatial
    entry = jnp.arange(HEAD_DIM, dtype=I32)
    pair_ids = entry // 2
    exponent = jnp.where(
        pair_ids < temporal,
        2.0 * pair_ids / (2.0 * temporal),
        jnp.where(
            pair_ids < temporal + spatial,
            2.0 * (pair_ids - temporal) / (2.0 * spatial),
            2.0 * (pair_ids - temporal - spatial) / (2.0 * spatial),
        ),
    ).astype(F32)
    frequency = jnp.power(jnp.float32(10000.0), -exponent)
    chosen_pos = jnp.where(
        pair_ids[None, :] < temporal,
        frame_pos[:, None],
        jnp.where(pair_ids[None, :] < temporal + spatial, row_pos[:, None], col_pos[:, None]),
    )
    angles = chosen_pos * frequency[None, :]
    sine = jnp.sin(angles)
    even = (entry % 2 == 0)[None, :]
    return jnp.cos(angles), jnp.where(even, -sine, 0.0), jnp.where(even, 0.0, sine)


def attend_kernel(half, place, q_ref, k_ref, v_ref, *refs):
    squares, (gain_q, gain_k, cosine, sine_l, sine_r), outs = refs[:2], refs[2:7], refs[7:11]
    scale_v, line_v = refs[11:]

    @pl.when(pl.program_id(0) == 0)
    def _():
        scale = lax.rsqrt((squares[0][...] + squares[1][...]) / D + 1e-06)
        for b in range(8):
            line_v[b * 8 : (b + 1) * 8, :] = scale[b]
        for b in range(8):
            source = place[b]
            for part in range(2):
                line = line_v[pl.ds(source * 8 + part, 1), :]
                scale_v[part, b * TOK : (b + 1) * TOK, :] = jnp.broadcast_to(line, (TOK, TOK)).T

    factor = HEAD_DIM ** (-0.5) * 1.4426950408889634

    def rotate(x, part, gain, rows):
        x = x * scale_v[part, rows, :] * gain
        left = pltpu.roll(x, HEAD_DIM - 1, 1)
        right = pltpu.roll(x, 1, 1)
        return (x * cosine[rows, :] + left * sine_l[rows, :] + right * sine_r[rows, :]).astype(BF16)

    every = slice(0, 8 * TOK)
    keys = rotate(k_ref[...], 1, gain_k[...], every)
    values = v_ref[...]
    tile = 256
    for i in range(4 * TOK // tile):
        inside = slice(i * tile, (i + 1) * tile)
        rows = slice(half * 4 * TOK + i * tile, half * 4 * TOK + (i + 1) * tile)
        q = rotate(q_ref[inside, :], 0, gain_q[...] * factor, rows)
        scores = lax.dot_general(q, keys, (((1,), (1,)), ((), ())), preferred_element_type=F32)
        top = jnp.max(scores, axis=-1, keepdims=True)
        weights = jnp.exp2(scores - top)
        total = jnp.sum(weights, axis=-1, keepdims=True)
        out = jnp.dot(weights.astype(BF16), values, preferred_element_type=F32)
        out = (out * (1.0 / total)).astype(BF16)
        for b in range(tile // TOK):
            outs[i * (tile // TOK) + b][...] = out[b * TOK : (b + 1) * TOK, :]


def attend(half, place, qk, v, squares, gain_q, gain_k, tables):
    query = pl.BlockSpec((4 * TOK, HEAD_DIM), lambda h: (half, h))
    key = pl.BlockSpec((8 * TOK, HEAD_DIM), lambda h: (0, HEADS + h))
    head = pl.BlockSpec((8 * TOK, HEAD_DIM), lambda h: (0, h))
    gain = pl.BlockSpec((1, HEAD_DIM), lambda h: (0, h))
    table = pl.BlockSpec((8 * TOK, HEAD_DIM), lambda h: (0, 0))
    square = pl.BlockSpec((8, 8, TOK), lambda h: (0, 0, 0))
    return pl.pallas_call(
        functools.partial(attend_kernel, half),
        out_shape=(jax.ShapeDtypeStruct((TOK, COLS), BF16),) * 4,
        grid=(HEADS,),
        in_specs=[pl.BlockSpec(memory_space=pltpu.SMEM), query, key, head]
        + [square] * 2
        + [gain, gain, table, table, table],
        out_specs=(pl.BlockSpec((TOK, HEAD_DIM), lambda h: (0, h)),) * 4,
        scratch_shapes=[pltpu.VMEM((2, 8 * TOK, TOK), F32), pltpu.VMEM((64, TOK), F32)],
        compiler_params=pltpu.CompilerParams(vmem_limit_bytes=60 * MIB),
        cost_estimate=pl.CostEstimate(flops=2 * 1024 * 1024 * COLS, bytes_accessed=10**7, transcendentals=5 * 2**19),
        name=f"attend_{half}",
    )(place, qk, qk, v, *squares, gain_q[None], gain_k[None], *tables)


def gather_kernel(place, *refs):
    pieces, out = refs[:8], refs[8]
    for j in range(8):
        column = pl.multiple_of(place[j] * COLS, COLS)
        out[0, :, pl.ds(column, COLS)] = pieces[j][...]


def gather_columns(place, pieces):
    vmem = pl.BlockSpec(memory_space=pltpu.VMEM)
    return pl.pallas_call(
        gather_kernel,
        out_shape=jax.ShapeDtypeStruct((1, TOK, D), BF16),
        in_specs=[pl.BlockSpec(memory_space=pltpu.SMEM)] + [vmem] * 8,
        out_specs=vmem,
        compiler_params=pltpu.CompilerParams(vmem_limit_bytes=16 * MIB),
        cost_estimate=pl.CostEstimate(flops=0, bytes_accessed=3 * 10**6, transcendentals=0),
        name="gather_columns",
    )(place, *pieces)


def per_device(h, modulation, wq, wk, wv, mq, mk, mv, gain_q, gain_k):
    xh, z, c, y, xl = (lax.axis_index(a).astype(I32) for a in AXES)
    way = 1 - 2 * c
    blocks = [(s, dx) for dx in range(2) for s in range(4)]
    canonical = jnp.stack([((y - way * s) % Y) * 2 + (xl ^ dx) for s, dx in blocks])
    sources = jnp.stack([((y + way * s) % Y) * 2 + (xl ^ dx) for s, dx in blocks])
    rows = [((z - way * s) % Z) * 2 + c for s in range(4)] + [((z + way * s) % Z) * 2 + 1 - c for s in range(4)]
    place_1 = jnp.concatenate([jnp.stack([xh] + rows), canonical])
    place_2 = jnp.concatenate([jnp.stack([1 - xh] + rows), canonical])
    me = jnp.stack([y * 2 + xl, c])

    x0, x0_lo, x0_hi, w0, w0_lo, w0_mid, w0_hi = begin(h, modulation, wq, wk, wv, mq, mk, mv)

    half = TOK // 2
    x1, w1, b0_lo, p0_lo = stage(ring_y(x0), ring_z(w0), swap_xl(x0_lo), swap_xh(w0_lo))
    x2, w2, b0_hi, p0_mid, e0, *tables = stage(
        ring_y(x1), ring_z(w1), swap_xl(x0_hi), swap_xh(w0_mid), swap_c(w0), *rope_tables(canonical)
    )
    x3, w3, p0_hi, e1, e2 = stage(ring_y(x2), ring_z(w2), swap_xh(w0_hi), swap_c(w1), swap_c(w2))
    b0 = jnp.concatenate([b0_lo, b0_hi])
    p0 = jnp.concatenate([p0_lo, p0_mid, p0_hi])
    e3 = swap_c(w3)
    own_half = [w0, w1, w2, w3, e0, e1, e2, e3]
    xs_a = [x0, x1, x2, x3]
    acc_a = project(place_1, xs_a, own_half)
    b1, p1, b3_lo, acc_a = stage(ring_y(b0), ring_z(p0), swap_xl(x3[:half]), acc_a)
    f0 = swap_c(p0)
    f1 = swap_c(p1)
    tokens = XH * Z * C * 8 * TOK
    sums = gram_rows(me, xs_a + [b0, b1], tokens)
    b2, p2, b3_hi, f0, f1, *sums = stage(ring_y(b1), ring_z(p1), swap_xl(x3[half:]), f0, f1, *sums)
    xs_b = [b0, b1, b2, b3_lo, b3_hi]

    f2 = swap_c(p2)
    theirs, mine = gram_rows(me, [b2, b3_lo, b3_hi], tokens, sums)
    theirs, f2, *xs_b = stage(theirs, f2, *xs_b)
    moved = swap_c(theirs)
    acc_b = project(place_1, xs_b, own_half)
    moved, mine, acc_b = stage(moved, mine, acc_b)
    part_0, part_1, part_2, part_3 = add_pair(z[None], mine, moved)
    part_0, part_1, part_2, part_3, p3, acc_a = stage(part_0, part_1, part_2, part_3, ring_z(p2), acc_a)
    f3 = swap_c(p3)
    summed = [part_0, up_z(part_1, 1), up_z(part_2, 2), up_z(part_3, 3)]
    other_half = [p0, p1, p2, p3, f0, f1, f2, f3]

    qk, v, squares = finish(place_2, xs_a + xs_b, other_half, [acc_a, acc_b])
    ring = squares + sum(to_owner(squares, s, 0) for s in range(1, Y))
    both = [ring, swap_xl(ring)]
    late = attend(1, canonical, qk, v, both, gain_q, gain_k, tables)
    late = list(late)
    late[0], *summed = stage(late[0], *summed)
    kept, sent = add_z(xh[None], *summed)
    pieces_late = [to_owner(o, s, 1) for o, s in zip(late, range(Y))]
    early = attend(0, canonical, stage(qk, late[0])[0], v, both, gain_q, gain_k, tables)
    *rest, sent = stage(*early, *pieces_late, sent)
    early, pieces_late = rest[:4], rest[4:]
    gram = kept + swap_xh(sent).astype(F32)
    pieces = [early[0]] + [to_owner(o, s, 0) for o, s in zip(early[1:], range(1, Y))]
    return gather_columns(sources, pieces + pieces_late), gram[None]


def solution(mesh):
    fine = Mesh(mesh.devices.reshape(XH, Z, C, Y, XL), AXES)
    grp, sp = ("xh", "z", "c"), ("y", "xl")
    return jax.shard_map(
        per_device,
        mesh=fine,
        in_specs=(
            P(grp, sp, None),
            P(grp, None, None),
            P(grp, sp),
            P(grp, sp),
            P(grp, sp),
            P(grp, sp),
            P(grp, sp),
            P(grp, sp),
            P(sp),
            P(sp),
        ),
        out_specs=(P(grp, sp, None), P(sp, grp, None)),
        check_vma=False,
    )
```

```python
import functools

import jax
import jax.numpy as jnp
from jax import lax
from jax.experimental import pallas as pl
from jax.experimental.pallas import tpu as pltpu
from jax.sharding import Mesh
from jax.sharding import PartitionSpec as P

HEAD_DIM = 128
HEIGHT = 16
WIDTH = 16
XH, Z, C, Y, XL = 2, 4, 2, 4, 2
AXES = ("xh", "z", "c", "y", "xl")
TOK = 128
D = 5120
COLS = 640
ROWS = 320
HALF = D // 2
HEADS = 5
BF16, F32, I32 = jnp.bfloat16, jnp.float32, jnp.int32
MIB = 1 << 20


def linear(xh, z, c, y, xl):
    return (((xh * Z + z) * C + c) * Y + y) * XL + xl


def permute(x, move):
    pairs = []
    for xh in range(XH):
        for z in range(Z):
            for c in range(C):
                for y in range(Y):
                    for xl in range(XL):
                        pairs.append((linear(xh, z, c, y, xl), linear(*move(xh, z, c, y, xl))))
    return lax.ppermute(x, AXES, pairs)


def turn(c):
    return 1 if c == 0 else -1


def ring_y(x):
    return permute(x, lambda xh, z, c, y, xl: (xh, z, c, (y + turn(c)) % Y, xl))


def ring_z(x):
    return permute(x, lambda xh, z, c, y, xl: (xh, (z + turn(c)) % Z, c, y, xl))


def swap_xl(x):
    return permute(x, lambda xh, z, c, y, xl: (xh, z, c, y, 1 - xl))


def swap_xh(x):
    return permute(x, lambda xh, z, c, y, xl: (1 - xh, z, c, y, xl))


def swap_c(x):
    return permute(x, lambda xh, z, c, y, xl: (xh, z, 1 - c, y, xl))


def to_owner(x, s, dx):
    return permute(x, lambda xh, z, c, y, xl: (xh, z, c, (y - turn(c) * s) % Y, xl ^ dx))


def stage(*arrays):
    return lax.optimization_barrier(arrays)


HALVES = ((0, TOK // 2), (TOK // 2, TOK))
CHUNKS = ((0, 64), (64, 128), (128, ROWS))


def begin_kernel(h, modulation, wq, wk, wv, mq, mk, mv, *refs):
    x_out, x_lo, x_hi, w_out, w_lo, w_mid, w_hi = refs[:7]
    h_v, mod_v, w_v, m_v, sem = refs[7:]
    pairs = [(h.at[0], h_v), (modulation.at[0], mod_v)]
    pairs += [(w, w_v.at[i]) for i, w in enumerate((wq, wk, wv))]
    pairs += [(m, m_v.at[i]) for i, m in enumerate((mq, mk, mv))]
    copies = [pltpu.make_async_copy(source, target, sem.at[i]) for i, (source, target) in enumerate(pairs)]
    for copy in copies:
        copy.start()
    for copy in copies[:2]:
        copy.wait()
    scale = 1.0 + mod_v[1:2, :]
    shift = mod_v[0:1, :]
    step = 32
    for i in range(TOK // step):
        x = h_v[i * step : (i + 1) * step, :].astype(F32)
        average = jnp.mean(x, axis=-1, keepdims=True)
        centred = x - average
        variance = jnp.mean(centred * centred, axis=-1, keepdims=True)
        y = (centred * lax.rsqrt(variance + 1e-06) * scale + shift).astype(BF16)
        x_out[i * step : (i + 1) * step, :] = y
        piece, at = (x_lo, i * step) if i * step < TOK // 2 else (x_hi, i * step - TOK // 2)
        piece[at : at + step, :] = y
    group = lax.broadcasted_iota(I32, (ROWS, ROWS // 4), 0) // 4
    spread = (group == lax.broadcasted_iota(I32, (ROWS, ROWS // 4), 1)).astype(F32).astype(BF16)
    slot = lax.broadcasted_iota(I32, (ROWS, COLS), 0) % 4
    for i in range(3):
        copies[2 + i].wait()
        copies[5 + i].wait()
        p = m_v[i]
        bits = jnp.where(p == 0, 3, jnp.where(p == 1, 5, jnp.where(p == 2, 9, jnp.where(p == 3, 6, jnp.where(p == 4, 10, 12)))))
        rows = jnp.dot(spread, bits.astype(F32).astype(BF16), preferred_element_type=F32).astype(I32)
        kept = (lax.shift_right_logical(rows, slot) & 1) == 1
        masked = jnp.where(kept, w_v[i].astype(F32), 0.0).astype(BF16)
        cols = slice(i * COLS, (i + 1) * COLS)
        w_out[:, cols] = masked
        for piece, (low, high) in zip((w_lo, w_mid, w_hi), CHUNKS):
            piece[:, cols] = masked[low:high, :]


def begin(h, modulation, wq, wk, wv, mq, mk, mv):
    hbm = pl.BlockSpec(memory_space=pltpu.HBM)
    vmem = pl.BlockSpec(memory_space=pltpu.VMEM)
    rows = [TOK, TOK // 2, TOK // 2]
    tall = [ROWS] + [high - low for low, high in CHUNKS]
    out = [jax.ShapeDtypeStruct((r, D), BF16) for r in rows] + [jax.ShapeDtypeStruct((r, 3 * COLS), BF16) for r in tall]
    return pl.pallas_call(
        begin_kernel,
        out_shape=out,
        in_specs=[hbm] * 8,
        out_specs=[vmem] * 7,
        scratch_shapes=[
            pltpu.VMEM((TOK, D), BF16),
            pltpu.VMEM((2, D), F32),
            pltpu.VMEM((3, ROWS, COLS), BF16),
            pltpu.VMEM((3, ROWS // 4, COLS), I32),
            pltpu.SemaphoreType.DMA((8,)),
        ],
        compiler_params=pltpu.CompilerParams(vmem_limit_bytes=60 * MIB),
        cost_estimate=pl.CostEstimate(flops=10**8, bytes_accessed=6 * 10**6, transcendentals=0),
        name="norm_and_mask",
    )(h, modulation, wq, wk, wv, mq, mk, mv)


def offsets(xs):
    starts = [0]
    for x in xs:
        starts.append(starts[-1] + x.shape[0])
    return starts


def edges_of(parts):
    return [sum(parts[:p]) for p in range(len(parts) + 1)]


def start_all(copies):
    for copy in copies:
        copy.start()


def wait_all(copies):
    for copy in copies:
        copy.wait()


def in_order(groups):
    start_all(groups[0])
    begun = [1]

    def need(g):
        wait_all(groups[g])
        while begun[0] < min(g + 3, len(groups)):
            start_all(groups[begun[0]])
            begun[0] += 1

    return need


def copies_of_x(xs, x_v, sem, column):
    at = offsets(xs)
    return [
        pltpu.make_async_copy(x.at[:, pl.ds(column, HALF)], x_v.at[at[j] : at[j + 1], :], sem.at[j])
        for j, x in enumerate(xs)
    ]


def copies_of_w(place, ws, w_v, sem, there, here, base):
    out = []
    for j in range(8):
        row = pl.multiple_of(place[1 + j] * ROWS, ROWS)
        out.append(pltpu.make_async_copy(ws[j].at[:, there], w_v.at[pl.ds(row, ROWS), here], sem.at[base + j]))
    return out


def project_kernel(n_x, parts, place, *refs):
    xs, ws, (out, x_v, w_v, y_v, sem_x, sem_w, sem_y) = refs[:n_x], refs[n_x : n_x + 8], refs[n_x + 8 :]
    copies_x = copies_of_x(xs, x_v, sem_x, pl.multiple_of(place[0] * HALF, HALF))
    edges = edges_of(parts)
    here = [slice(edges[p], edges[p + 1]) for p in range(len(parts))]
    copies_w = [copies_of_w(place, ws, w_v, sem_w, cols, cols, p * 8) for p, cols in enumerate(here)]
    need = in_order([copies_w[0] + copies_x] + copies_w[1:])
    sent = []
    for p, cols in enumerate(here):
        need(p)
        y_v[:, cols] = jnp.dot(x_v[...], w_v[:, cols], preferred_element_type=F32)
        sent.append(pltpu.make_async_copy(y_v.at[:, cols], out.at[:, cols], sem_y.at[p]))
        sent[-1].start()
    wait_all(sent)


def project(place, xs, ws):
    n_x = len(xs)
    rows = offsets(xs)[-1]
    parts = (256, 512, 512, 640)
    width = 3 * COLS
    hbm = pl.BlockSpec(memory_space=pltpu.HBM)
    return pl.pallas_call(
        functools.partial(project_kernel, n_x, parts),
        out_shape=jax.ShapeDtypeStruct((rows, width), F32),
        in_specs=[pl.BlockSpec(memory_space=pltpu.SMEM)] + [hbm] * (n_x + 8),
        out_specs=hbm,
        scratch_shapes=[
            pltpu.VMEM((rows, HALF), BF16),
            pltpu.VMEM((HALF, width), BF16),
            pltpu.VMEM((rows, width), F32),
            pltpu.SemaphoreType.DMA((n_x,)),
            pltpu.SemaphoreType.DMA((8 * len(parts),)),
            pltpu.SemaphoreType.DMA((len(parts),)),
        ],
        compiler_params=pltpu.CompilerParams(vmem_limit_bytes=60 * MIB),
        cost_estimate=pl.CostEstimate(flops=10**6, bytes_accessed=10**5, transcendentals=0),
        name="project_first",
    )(place, *xs, *ws)


def finish_kernel(n_x, parts, place, *refs):
    xs, ws, accs, refs = refs[:n_x], refs[n_x : n_x + 8], refs[n_x + 8 : n_x + 10], refs[n_x + 10 :]
    qk_out, v_out, sq_out, x_v, w_v, a_v, y_v, v_v, sem_x, sem_w, sem_a, sem_y = refs
    copies_x = copies_of_x(xs, x_v, sem_x, pl.multiple_of(place[0] * HALF, HALF))
    n = len(parts)
    edges = edges_of(parts)
    middle = 4 * TOK
    groups = []
    for p in range(n):
        cols = slice(edges[p], edges[p + 1])
        copies_w = copies_of_w(place, ws, w_v, sem_w, cols, cols, p * 8)
        copies_a = [
            pltpu.make_async_copy(acc.at[:, cols], a_v.at[i * middle : (i + 1) * middle, cols], sem_a.at[p * 2 + i])
            for i, acc in enumerate(accs)
        ]
        groups += [copies_w + copies_x[:4], copies_x[4:] + copies_a] if p == 0 else [copies_w + copies_a]
    need = in_order(groups)
    need(0)
    sent = []
    for p in range(n):
        cols = slice(edges[p], edges[p + 1])
        if p:
            need(p + 1)
        for i in range(2):
            rows = slice(i * middle, (i + 1) * middle)
            y = jnp.dot(x_v[rows, :], w_v[:, cols], preferred_element_type=F32)
            if p == 0 and i == 0:
                need(1)
            y = y + a_v[rows, cols]
            if edges[p] >= 2 * COLS:
                v_v[rows, :] = y.astype(BF16)
                target, source = v_out, v_v
            else:
                y_v[rows, cols] = y
                target, source = qk_out.at[:, cols], y_v.at[:, cols]
            for part in range(2):
                low, high = max(edges[p], part * COLS), min(edges[p + 1], (part + 1) * COLS)
                if low >= high:
                    continue
                squares = y[:, low - edges[p] : high - edges[p]]
                squares = squares * squares
                lanes = sum(squares[:, h : h + 128] for h in range(0, high - low, 128))
                for b in range(4):
                    line = jnp.sum(lanes[b * TOK : (b + 1) * TOK, :].T, axis=0, keepdims=True)
                    at = place[9 + i * 4 + b]
                    if low > part * COLS:
                        line = line + sq_out[at, part : part + 1, :]
                    sq_out[at, part : part + 1, :] = line
        sent.append(pltpu.make_async_copy(source, target, sem_y.at[p]))
        sent[-1].start()
    wait_all(sent)


def finish(place, xs, ws, accs):
    parts = (256, 512, 512, 640)
    n = len(parts)
    rows = 8 * TOK
    width = 3 * COLS
    hbm = pl.BlockSpec(memory_space=pltpu.HBM)
    n_x = len(xs)
    return pl.pallas_call(
        functools.partial(finish_kernel, n_x, parts),
        out_shape=[
            jax.ShapeDtypeStruct((rows, 2 * COLS), F32),
            jax.ShapeDtypeStruct((rows, COLS), BF16),
            jax.ShapeDtypeStruct((8, 8, TOK), F32),
        ],
        in_specs=[pl.BlockSpec(memory_space=pltpu.SMEM)] + [hbm] * (n_x + 10),
        out_specs=[hbm, hbm, pl.BlockSpec(memory_space=pltpu.VMEM)],
        scratch_shapes=[
            pltpu.VMEM((rows, HALF), BF16),
            pltpu.VMEM((HALF, width), BF16),
            pltpu.VMEM((rows, width), F32),
            pltpu.VMEM((rows, 2 * COLS), F32),
            pltpu.VMEM((rows, COLS), BF16),
            pltpu.SemaphoreType.DMA((n_x,)),
            pltpu.SemaphoreType.DMA((8 * n,)),
            pltpu.SemaphoreType.DMA((2 * n,)),
            pltpu.SemaphoreType.DMA((n,)),
        ],
        compiler_params=pltpu.CompilerParams(vmem_limit_bytes=60 * MIB),
        cost_estimate=pl.CostEstimate(flops=2 * rows * HALF * width, bytes_accessed=30 * 10**6, transcendentals=0),
        name="project_last",
    )(place, *xs, *ws, *accs)


def gram_kernel(tokens, n_x, added, place, *refs):
    xs, refs = refs[:n_x], refs[n_x:]
    sums, refs = refs[: 2 * added], refs[2 * added :]
    outs, (own_x, x_v, own, o_v, sem_own, sem_x, sem_o), (*more,) = refs[:2], refs[2:9], refs[9:]
    at = offsets(xs)
    n = 4
    step = D // n
    column = pl.multiple_of(place[0] * COLS, COLS)
    first = [
        pltpu.make_async_copy(x.at[:, pl.ds(column, COLS)], own_x.at[at[j] : at[j + 1], :], sem_own.at[j])
        for j, x in enumerate(xs)
    ]
    rest = []
    for i in range(n):
        cols = slice(i * step, (i + 1) * step)
        some = [
            pltpu.make_async_copy(x.at[:, cols], x_v.at[at[j] : at[j + 1], cols], sem_x.at[i, j])
            for j, x in enumerate(xs)
        ]
        for j, old in enumerate(sums):
            s_v, sem_s = more
            some.append(
                pltpu.make_async_copy(old.at[:, cols], s_v.at[j * ROWS : (j + 1) * ROWS, cols], sem_s.at[i, j])
            )
        rest.append(some)
    need = in_order([first] + rest)
    line = lax.broadcasted_iota(I32, (COLS, COLS), 0)
    core = jnp.where(line < ROWS, 1 - place[1], place[1])
    source = ((line // 40 % XH * Z + line // 80 % Z) * C + core) * 40 + line % 40
    order = (source == lax.broadcasted_iota(I32, (COLS, COLS), 1)).astype(F32).astype(BF16)
    need(0)
    own[...] = lax.dot_general(
        order, own_x[...], (((1,), (1,)), ((), ())), preferred_element_type=F32
    ).astype(BF16)
    sends = []
    for i in range(n):
        cols = slice(i * step, (i + 1) * step)
        need(i + 1)
        for j, out in enumerate(outs):
            rows = slice(j * ROWS, (j + 1) * ROWS)
            y = jnp.dot(own[rows, :], x_v[:, cols], preferred_element_type=F32) * (1.0 / tokens)
            if added:
                y = y + more[0][rows, cols].astype(F32)
            o_v[rows, cols] = y.astype(BF16)
            sends.append(pltpu.make_async_copy(o_v.at[rows, cols], out.at[:, cols], sem_o.at[i, j]))
            sends[-1].start()
    wait_all(sends)


def gram_rows(place, xs, tokens, sums=()):
    hbm = pl.BlockSpec(memory_space=pltpu.HBM)
    n_x = len(xs)
    count = offsets(xs)[-1]
    scratch = [
        pltpu.VMEM((count, COLS), BF16),
        pltpu.VMEM((count, D), BF16),
        pltpu.VMEM((COLS, count), BF16),
        pltpu.VMEM((COLS, D), BF16),
        pltpu.SemaphoreType.DMA((n_x,)),
        pltpu.SemaphoreType.DMA((4, n_x)),
        pltpu.SemaphoreType.DMA((4, 2)),
    ]
    if sums:
        scratch += [pltpu.VMEM((COLS, D), BF16), pltpu.SemaphoreType.DMA((4, 2))]
    return pl.pallas_call(
        functools.partial(gram_kernel, tokens, n_x, bool(sums)),
        out_shape=[jax.ShapeDtypeStruct((ROWS, D), BF16)] * 2,
        in_specs=[pl.BlockSpec(memory_space=pltpu.SMEM)] + [hbm] * (n_x + len(sums)),
        out_specs=[hbm] * 2,
        scratch_shapes=scratch,
        compiler_params=pltpu.CompilerParams(vmem_limit_bytes=60 * MIB),
        cost_estimate=pl.CostEstimate(flops=10**6, bytes_accessed=10**5, transcendentals=0),
        name=f"gram_rows_{count}",
    )(place, *xs, *sums)


Z_PART = ROWS // Z


def pair_kernel(place, mine, moved, own, *refs):
    outs, (m_v, sem) = refs[:3], refs[3:]
    order = (1, 3, 2, 0)
    groups = []
    for k in order:
        rows = pl.ds(pl.multiple_of(lax.rem(place[0] + k, Z) * Z_PART, 16), Z_PART)
        groups.append(
            [pltpu.make_async_copy(source.at[rows, :], m_v.at[j, k], sem.at[j, k]) for j, source in enumerate((mine, moved))]
        )
    for some in groups:
        start_all(some)
    for g, k in enumerate(order):
        wait_all(groups[g])
        y = m_v[0, k].astype(F32) + m_v[1, k].astype(F32)
        if k == 0:
            own[...] = y
        else:
            outs[k - 1][...] = y.astype(BF16)


def add_pair(place, mine, moved):
    hbm = pl.BlockSpec(memory_space=pltpu.HBM)
    vmem = pl.BlockSpec(memory_space=pltpu.VMEM)
    return pl.pallas_call(
        pair_kernel,
        out_shape=[jax.ShapeDtypeStruct((Z_PART, D), F32)] + [jax.ShapeDtypeStruct((Z_PART, D), BF16)] * 3,
        in_specs=[pl.BlockSpec(memory_space=pltpu.SMEM), hbm, hbm],
        out_specs=[vmem] * 4,
        scratch_shapes=[pltpu.VMEM((2, Z, Z_PART, D), BF16), pltpu.SemaphoreType.DMA((2, Z))],
        compiler_params=pltpu.CompilerParams(vmem_limit_bytes=60 * MIB),
        cost_estimate=pl.CostEstimate(flops=10**6, bytes_accessed=10**7, transcendentals=0),
        name="gram_pair",
    )(place, mine, moved)


def z_kernel(place, own, one, two, three, kept, sent, total_v):
    total_v[...] = own[...] + one[...].astype(F32) + two[...].astype(F32) + three[...].astype(F32)
    rows = Z_PART // XH
    kept[...] = total_v[pl.ds(pl.multiple_of(place[0] * rows, 8), rows), :]
    sent[...] = total_v[pl.ds(pl.multiple_of((1 - place[0]) * rows, 8), rows), :].astype(BF16)


def add_z(place, own, *others):
    vmem = pl.BlockSpec(memory_space=pltpu.VMEM)
    rows = Z_PART // XH
    return pl.pallas_call(
        z_kernel,
        out_shape=[jax.ShapeDtypeStruct((rows, D), F32), jax.ShapeDtypeStruct((rows, D), BF16)],
        in_specs=[pl.BlockSpec(memory_space=pltpu.SMEM)] + [vmem] * 4,
        out_specs=[vmem] * 2,
        scratch_shapes=[pltpu.VMEM((Z_PART, D), F32)],
        compiler_params=pltpu.CompilerParams(vmem_limit_bytes=32 * MIB),
        cost_estimate=pl.CostEstimate(flops=10**6, bytes_accessed=4 * 10**6, transcendentals=0),
        name="gram_z",
    )(place, own, *others)


def up_z(x, k):
    return permute(x, lambda xh, z, c, y, xl: (xh, (z + k) % Z, c, y, xl))


def rope_tables(place):
    inside = jnp.arange(TOK, dtype=I32)[None, :]
    blocks = place[:, None]
    frame_pos = jnp.broadcast_to(blocks // 2, (8, TOK)).reshape(-1).astype(F32)
    row_pos = (blocks % 2 * 8 + inside // WIDTH).reshape(-1).astype(F32)
    col_pos = jnp.broadcast_to(inside % WIDTH, (8, TOK)).reshape(-1).astype(F32)
    half_dim = HEAD_DIM // 2
    spatial = HEAD_DIM // 6
    temporal = half_dim - 2 * spatial
    entry = jnp.arange(HEAD_DIM, dtype=I32)
    pair_ids = entry // 2
    exponent = jnp.where(
        pair_ids < temporal,
        2.0 * pair_ids / (2.0 * temporal),
        jnp.where(
            pair_ids < temporal + spatial,
            2.0 * (pair_ids - temporal) / (2.0 * spatial),
            2.0 * (pair_ids - temporal - spatial) / (2.0 * spatial),
        ),
    ).astype(F32)
    frequency = jnp.power(jnp.float32(10000.0), -exponent)
    chosen_pos = jnp.where(
        pair_ids[None, :] < temporal,
        frame_pos[:, None],
        jnp.where(pair_ids[None, :] < temporal + spatial, row_pos[:, None], col_pos[:, None]),
    )
    angles = chosen_pos * frequency[None, :]
    sine = jnp.sin(angles)
    even = (entry % 2 == 0)[None, :]
    return jnp.cos(angles), jnp.where(even, -sine, 0.0), jnp.where(even, 0.0, sine)


def attend_kernel(half, place, q_ref, k_ref, v_ref, *refs):
    squares, (gain_q, gain_k, cosine, sine_l, sine_r), outs = refs[:2], refs[2:7], refs[7:11]
    scale_v, line_v = refs[11:]

    @pl.when(pl.program_id(0) == 0)
    def _():
        scale = lax.rsqrt((squares[0][...] + squares[1][...]) / D + 1e-06)
        for b in range(8):
            line_v[b * 8 : (b + 1) * 8, :] = scale[b]
        for b in range(8):
            source = place[b]
            for part in range(2):
                line = line_v[pl.ds(source * 8 + part, 1), :]
                scale_v[part, b * TOK : (b + 1) * TOK, :] = jnp.broadcast_to(line, (TOK, TOK)).T

    factor = HEAD_DIM ** (-0.5) * 1.4426950408889634

    def rotate(x, part, gain, rows):
        x = x * scale_v[part, rows, :] * gain
        left = pltpu.roll(x, HEAD_DIM - 1, 1)
        right = pltpu.roll(x, 1, 1)
        return (x * cosine[rows, :] + left * sine_l[rows, :] + right * sine_r[rows, :]).astype(BF16)

    every = slice(0, 8 * TOK)
    keys = rotate(k_ref[...], 1, gain_k[...], every)
    values = v_ref[...]
    tile = 256
    for i in range(4 * TOK // tile):
        inside = slice(i * tile, (i + 1) * tile)
        rows = slice(half * 4 * TOK + i * tile, half * 4 * TOK + (i + 1) * tile)
        q = rotate(q_ref[inside, :], 0, gain_q[...] * factor, rows)
        scores = lax.dot_general(q, keys, (((1,), (1,)), ((), ())), preferred_element_type=F32)
        top = jnp.max(scores, axis=-1, keepdims=True)
        weights = jnp.exp2(scores - top)
        total = jnp.sum(weights, axis=-1, keepdims=True)
        out = jnp.dot(weights.astype(BF16), values, preferred_element_type=F32)
        out = (out * (1.0 / total)).astype(BF16)
        for b in range(tile // TOK):
            outs[i * (tile // TOK) + b][...] = out[b * TOK : (b + 1) * TOK, :]


def attend(half, place, qk, v, squares, gain_q, gain_k, tables):
    query = pl.BlockSpec((4 * TOK, HEAD_DIM), lambda h: (half, h))
    key = pl.BlockSpec((8 * TOK, HEAD_DIM), lambda h: (0, HEADS + h))
    head = pl.BlockSpec((8 * TOK, HEAD_DIM), lambda h: (0, h))
    gain = pl.BlockSpec((1, HEAD_DIM), lambda h: (0, h))
    table = pl.BlockSpec((8 * TOK, HEAD_DIM), lambda h: (0, 0))
    square = pl.BlockSpec((8, 8, TOK), lambda h: (0, 0, 0))
    return pl.pallas_call(
        functools.partial(attend_kernel, half),
        out_shape=(jax.ShapeDtypeStruct((TOK, COLS), BF16),) * 4,
        grid=(HEADS,),
        in_specs=[pl.BlockSpec(memory_space=pltpu.SMEM), query, key, head]
        + [square] * 2
        + [gain, gain, table, table, table],
        out_specs=(pl.BlockSpec((TOK, HEAD_DIM), lambda h: (0, h)),) * 4,
        scratch_shapes=[pltpu.VMEM((2, 8 * TOK, TOK), F32), pltpu.VMEM((64, TOK), F32)],
        compiler_params=pltpu.CompilerParams(vmem_limit_bytes=60 * MIB),
        cost_estimate=pl.CostEstimate(flops=2 * 1024 * 1024 * COLS, bytes_accessed=10**7, transcendentals=5 * 2**19),
        name=f"attend_{half}",
    )(place, qk, qk, v, *squares, gain_q[None], gain_k[None], *tables)


def gather_kernel(place, *refs):
    pieces, out = refs[:8], refs[8]
    for j in range(8):
        column = pl.multiple_of(place[j] * COLS, COLS)
        out[0, :, pl.ds(column, COLS)] = pieces[j][...]


def gather_columns(place, pieces):
    vmem = pl.BlockSpec(memory_space=pltpu.VMEM)
    return pl.pallas_call(
        gather_kernel,
        out_shape=jax.ShapeDtypeStruct((1, TOK, D), BF16),
        in_specs=[pl.BlockSpec(memory_space=pltpu.SMEM)] + [vmem] * 8,
        out_specs=vmem,
        compiler_params=pltpu.CompilerParams(vmem_limit_bytes=16 * MIB),
        cost_estimate=pl.CostEstimate(flops=0, bytes_accessed=3 * 10**6, transcendentals=0),
        name="gather_columns",
    )(place, *pieces)


def per_device(h, modulation, wq, wk, wv, mq, mk, mv, gain_q, gain_k):
    xh, z, c, y, xl = (lax.axis_index(a).astype(I32) for a in AXES)
    way = 1 - 2 * c
    blocks = [(s, dx) for dx in range(2) for s in range(4)]
    canonical = jnp.stack([((y - way * s) % Y) * 2 + (xl ^ dx) for s, dx in blocks])
    sources = jnp.stack([((y + way * s) % Y) * 2 + (xl ^ dx) for s, dx in blocks])
    rows = [((z - way * s) % Z) * 2 + c for s in range(4)] + [((z + way * s) % Z) * 2 + 1 - c for s in range(4)]
    place_1 = jnp.concatenate([jnp.stack([xh] + rows), canonical])
    place_2 = jnp.concatenate([jnp.stack([1 - xh] + rows), canonical])
    me = jnp.stack([y * 2 + xl, c])

    x0, x0_lo, x0_hi, w0, w0_lo, w0_mid, w0_hi = begin(h, modulation, wq, wk, wv, mq, mk, mv)

    half = TOK // 2
    x1, w1, b0_lo, p0_lo = stage(ring_y(x0), ring_z(w0), swap_xl(x0_lo), swap_xh(w0_lo))
    x2, w2, b0_hi, p0_mid, e0, *tables = stage(
        ring_y(x1), ring_z(w1), swap_xl(x0_hi), swap_xh(w0_mid), swap_c(w0), *rope_tables(canonical)
    )
    x3, w3, p0_hi, e1 = stage(ring_y(x2), ring_z(w2), swap_xh(w0_hi), swap_c(w1))
    b0 = jnp.concatenate([b0_lo, b0_hi])
    p0 = jnp.concatenate([p0_lo, p0_mid, p0_hi])
    e2, e3 = swap_c(w2), swap_c(w3)
    own_half = [w0, w1, w2, w3, e0, e1, e2, e3]
    xs_a = [x0, x1, x2, x3]
    acc_a = project(place_1, xs_a, own_half)
    b1, p1, b3_lo, acc_a = stage(ring_y(b0), ring_z(p0), swap_xl(x3[:half]), acc_a)
    f0 = swap_c(p0)
    f1 = swap_c(p1)
    tokens = XH * Z * C * 8 * TOK
    sums = gram_rows(me, xs_a + [b0, b1], tokens)
    b2, p2, b3_hi, f0, f1, *sums = stage(ring_y(b1), ring_z(p1), swap_xl(x3[half:]), f0, f1, *sums)
    xs_b = [b0, b1, b2, b3_lo, b3_hi]

    f2 = swap_c(p2)
    theirs, mine = gram_rows(me, [b2, b3_lo, b3_hi], tokens, sums)
    theirs, f2, *xs_b = stage(theirs, f2, *xs_b)
    moved = swap_c(theirs)
    acc_b = project(place_1, xs_b, own_half)
    moved, mine, acc_b = stage(moved, mine, acc_b)
    part_0, part_1, part_2, part_3 = add_pair(z[None], mine, moved)
    part_0, part_1, part_2, part_3, p3, acc_a = stage(part_0, part_1, part_2, part_3, ring_z(p2), acc_a)
    f3 = swap_c(p3)
    summed = [part_0, up_z(part_1, 1), up_z(part_2, 2), up_z(part_3, 3)]
    other_half = [p0, p1, p2, p3, f0, f1, f2, f3]

    qk, v, squares = finish(place_2, xs_a + xs_b, other_half, [acc_a, acc_b])
    ring = squares + sum(to_owner(squares, s, 0) for s in range(1, Y))
    both = [ring, swap_xl(ring)]
    late = attend(1, canonical, qk, v, both, gain_q, gain_k, tables)
    late = list(late)
    late[0], *summed = stage(late[0], *summed)
    kept, sent = add_z(xh[None], *summed)
    pieces_late = [to_owner(o, s, 1) for o, s in zip(late, range(Y))]
    early = attend(0, canonical, stage(qk, late[0])[0], v, both, gain_q, gain_k, tables)
    *rest, sent = stage(*early, *pieces_late, sent)
    early, pieces_late = rest[:4], rest[4:]
    gram = kept + swap_xh(sent).astype(F32)
    pieces = [early[0]] + [to_owner(o, s, 0) for o, s in zip(early[1:], range(1, Y))]
    return gather_columns(sources, pieces + pieces_late), gram[None]


def solution(mesh):
    fine = Mesh(mesh.devices.reshape(XH, Z, C, Y, XL), AXES)
    grp, sp = ("xh", "z", "c"), ("y", "xl")
    return jax.shard_map(
        per_device,
        mesh=fine,
        in_specs=(
            P(grp, sp, None),
            P(grp, None, None),
            P(grp, sp),
            P(grp, sp),
            P(grp, sp),
            P(grp, sp),
            P(grp, sp),
            P(grp, sp),
            P(sp),
            P(sp),
        ),
        out_specs=(P(grp, sp, None), P(sp, grp, None)),
        check_vma=False,
    )
```
